32 devices in a mesh: grp: 2 (over y), ctx: 4 (over z), tp: 2 (over x), sub: 2 (over core).
Axes of the slice: x: 2, y: 2, z: 4, core: 2. Of those that a mesh axis runs over, the one named last changes fastest.
Arguments:
- queries: bfloat16 [2048, 8192], P(('grp', 'ctx', 'sub'), 'tp'), parts along dimension 0
- keys: bfloat16 [2048, 1024], P(('grp', 'ctx', 'sub'), 'tp'), parts along dimension 0
- values: bfloat16 [2048, 1024], P(('grp', 'ctx', 'sub'), 'tp'), parts along dimension 0, may hold values from -6 to 6
- beacon_keys: bfloat16 [1024, 1024], P(('grp', 'ctx', 'sub'), 'tp'), parts along dimension 0, may hold values from -6 to 6
- beacon_values: bfloat16 [1024, 1024], P(('grp', 'ctx', 'sub'), 'tp'), parts along dimension 0, may hold values from -6 to 6
- grad_out: bfloat16 [2048, 8192], P(('grp', 'ctx', 'sub'), 'tp'), parts along dimension 0, may hold values from -6 to 6
- ratios: int32 [8], P('grp'), parts along dimension 0, may hold values from 2 to 32, as said below
Outputs:
- grad_queries: bfloat16 [2048, 8192], P(('grp', 'ctx', 'sub'), 'tp'), parts along dimension 0
- grad_keys: bfloat16 [2048, 1024], P(('grp', 'ctx', 'sub'), 'tp'), parts along dimension 0
- grad_values: bfloat16 [2048, 1024], P(('grp', 'ctx', 'sub'), 'tp'), parts along dimension 0
- grad_beacon_keys: bfloat16 [1024, 1024], P(('grp', 'ctx', 'sub'), 'tp'), parts along dimension 0
- grad_beacon_values: bfloat16 [1024, 1024], P(('grp', 'ctx', 'sub'), 'tp'), parts along dimension 0
The draws below stay inside these ranges and needn't reach their ends.
There are 2 independent parts, one for each index of `grp`. The reference program is written for one: setup_inputs(seed, part) draws one part's arguments, and reference() takes and returns one part's arrays. A program takes and returns all parts, laid end to end along the dimension named above; each array names one. Nothing has to cross between parts.
Inputs may be any that keep to these rules, and one draw needn't show every extreme that they name: `ratios`: every ratio is a power of two, and some span other than the last has ratio 2, so that it fills all 128 of its slots.
All inputs are finite; a program needn't handle non-finite values.
Results may differ from the reference program's by a relative error of at most 0.012.
The reference program's roundings to bfloat16 on the way count: a program that leaves them out, or rounds other values in their place, can miss the bound.
Values may be sent and summed in bfloat16 or wider, within the bound.
No kernel may reach another device: no remote copies, remote signals or barrier semaphores. Data moves between devices by JAX's collectives and lax.ppermute only.
A program may use at most 64 MiB of HBM per device.

```python
import jax
import jax.numpy as jnp
from jax import lax

H = 64
KVH = 8
DH = 128
SPAN = 256
TOKENS = 1024
BEACONS = 512
N_CTX = 4


def shared_base(key):
    return jax.random.normal(key, (TOKENS, KVH * DH), jnp.float32)


def draw_keys(key, part):
    base = shared_base(key)
    return base.astype(jnp.bfloat16)


def draw_queries(key, part):
    key = jax.random.fold_in(key, 12)
    fresh = jax.random.normal(key, (TOKENS, H * DH), jnp.float32)
    return fresh.astype(jnp.bfloat16)


def draw_ratios(key, part):
    key = jax.random.fold_in(key, 13)
    left_key, right_key = jax.random.split(key)
    powers = jax.random.randint(left_key, (N_CTX,), 1, 6)
    result = jnp.left_shift(jnp.ones((N_CTX,), jnp.int32), powers.astype(jnp.int32))
    chosen = jax.random.randint(right_key, (), 0, N_CTX - 1)
    return jnp.where(jnp.arange(N_CTX) == chosen, 2, result).astype(jnp.int32)


def steps_of(key, shape, shards, low, largest):
    loudness = 1.0
    for axis_at, blocks in shards:
        draws = jax.random.uniform(jax.random.fold_in(jax.random.fold_in(key, 6), axis_at), (blocks,), jnp.float32, low / len(shards), largest / len(shards))
        loudness = loudness * jnp.repeat(jnp.exp(draws), shape[axis_at] // blocks).reshape((-1,) + (1,) * (len(shape) - 1 - axis_at))
    return loudness


def bell_draw(own_key, extent, deviation, reach, cuts=(), held_as=jnp.bfloat16):
    gain = steps_of(own_key, extent, cuts, -0.22, 0.18) if cuts else 1.0
    values = jax.random.normal(own_key, extent, jnp.float32) * deviation * gain
    return jnp.minimum(jnp.maximum(values, -reach), reach).astype(held_as)


def setup_inputs(seed: int = 0, part: int = 0) -> dict:
    seeds = jax.random.split(jax.random.key(seed), 8)
    own_keys = jax.random.split(jax.random.fold_in(seeds[7], part), 8)
    queries = draw_queries(jax.random.fold_in(jax.random.fold_in(seeds[7], part), 71), part)
    keys = draw_keys(jax.random.fold_in(jax.random.fold_in(seeds[7], part), 71), part)
    values = bell_draw(own_keys[2], (TOKENS, KVH * DH), 1.0, 6.0, ((0, 8), (1, 2)))
    beacon_keys = bell_draw(own_keys[3], (BEACONS, KVH * DH), 1.0, 6.0, ((0, 8), (1, 2)))
    beacon_values = bell_draw(own_keys[4], (BEACONS, KVH * DH), 1.0, 6.0, ((0, 8), (1, 2)))
    grad_out = bell_draw(own_keys[5], (TOKENS, H * DH), 1.0, 6.0, ((0, 8), (1, 2)))
    ratios = draw_ratios(jax.random.fold_in(jax.random.fold_in(seeds[7], part), 71), part)
    return {"queries": queries, "keys": keys, "values": values, "beacon_keys": beacon_keys, "beacon_values": beacon_values, "grad_out": grad_out, "ratios": ratios}


def to_bfloat(values_in):
    rounded = lax.optimization_barrier(values_in.astype(jnp.bfloat16))
    return rounded.astype(jnp.float32)


def reference(queries, keys, values, beacon_keys, beacon_values, grad_out, ratios):
    count_spans = ratios.shape[0]
    slots = SPAN // 2
    group = H // KVH
    softmax_scale = DH ** -0.5
    query_all = queries.reshape(count_spans, SPAN, KVH, group, DH)
    grad_all = grad_out.reshape(count_spans, SPAN, KVH, group, DH)
    key_all = keys.reshape(count_spans, SPAN, KVH, DH)
    value_all = values.reshape(count_spans, SPAN, KVH, DH)
    distant_key_rows = beacon_keys.reshape(count_spans * slots, KVH, DH).astype(jnp.float32)
    distant_value_rows = beacon_values.reshape(count_spans * slots, KVH, DH).astype(jnp.float32)
    live_counts = SPAN // ratios
    slot_index = jnp.arange(count_spans * slots, dtype=jnp.int32)
    owner = slot_index // slots
    live_slot = (slot_index % slots) < live_counts[owner]
    positions = jnp.arange(SPAN, dtype=jnp.int32)
    causal = positions[None, :] <= positions[:, None]
    distant_key_running = jnp.zeros((count_spans * slots, KVH, DH), jnp.float32)
    distant_value_running = jnp.zeros((count_spans * slots, KVH, DH), jnp.float32)
    grad_query_list = []
    grad_key_list = []
    grad_value_list = []
    for span_index in range(count_spans):
        visible = live_slot & (owner < span_index)
        current_query = query_all[span_index].astype(jnp.float32)
        current_gradient = grad_all[span_index].astype(jnp.float32)
        current_key = key_all[span_index].astype(jnp.float32)
        current_value = value_all[span_index].astype(jnp.float32)
        near_scores = jnp.einsum('rkgd,ukd->kgru', current_query, current_key) * softmax_scale
        near_scores = jnp.where(causal, near_scores, -jnp.inf)
        distant_score_grid = jnp.einsum('fmpi,ymi->mpfy', current_query, distant_key_rows) * softmax_scale
        distant_score_grid = jnp.where(visible, distant_score_grid, -jnp.inf)
        top = jnp.maximum(jnp.max(near_scores, -1), jnp.max(distant_score_grid, -1))
        total = jnp.sum(jnp.exp(near_scores - top[..., None]), -1) + jnp.sum(jnp.exp(distant_score_grid - top[..., None]), -1)
        logsumexp = top + jnp.log(total)
        near_probs = jnp.exp(near_scores - logsumexp[..., None])
        far_probs = jnp.exp(distant_score_grid - logsumexp[..., None])
        nearby_weight_grid = to_bfloat(near_probs)
        distant_weight_grid = to_bfloat(far_probs)
        result_output = jnp.einsum('jpxi,ije->xjpe', nearby_weight_grid, current_value) + jnp.einsum('tuxs,sto->xtuo', distant_weight_grid, distant_value_rows)
        deltas = jnp.einsum('rkgd,rkgd->kgr', current_gradient, result_output)
        near_signal = jnp.einsum('rkgd,ukd->kgru', current_gradient, current_value)
        distant_gradient_signal = jnp.einsum('fmpi,ymi->mpfy', current_gradient, distant_value_rows)
        nearby_bias_slopes = to_bfloat(near_probs * (near_signal - deltas[..., None]))
        distant_bias_slopes = to_bfloat(far_probs * (distant_gradient_signal - deltas[..., None]))
        query_gradient = softmax_scale * (jnp.einsum('jpxi,ije->xjpe', nearby_bias_slopes, current_key) + jnp.einsum('tuxs,sto->xtuo', distant_bias_slopes, distant_key_rows))
        grad_query_list.append(query_gradient.reshape(SPAN, H * DH).astype(jnp.bfloat16))
        grad_key = softmax_scale * jnp.einsum('kgru,rkgd->ukd', nearby_bias_slopes, current_query)
        grad_value = jnp.einsum('kgru,rkgd->ukd', nearby_weight_grid, current_gradient)
        grad_key_list.append(grad_key.reshape(SPAN, KVH * DH).astype(jnp.bfloat16))
        grad_value_list.append(grad_value.reshape(SPAN, KVH * DH).astype(jnp.bfloat16))
        distant_key_running = distant_key_running + softmax_scale * jnp.einsum('jmch,cjmu->hju', distant_bias_slopes, current_query)
        distant_value_running = distant_value_running + jnp.einsum('jmch,cjmu->hju', distant_weight_grid, current_gradient)
    grad_queries = jnp.concatenate(grad_query_list, 0)
    grad_keys = jnp.concatenate(grad_key_list, 0)
    grad_values = jnp.concatenate(grad_value_list, 0)
    grad_beacon_keys = distant_key_running.reshape(count_spans * slots, KVH * DH).astype(jnp.bfloat16)
    grad_beacon_values = distant_value_running.reshape(count_spans * slots, KVH * DH).astype(jnp.bfloat16)
    return (grad_queries, grad_keys, grad_values, grad_beacon_keys, grad_beacon_values)
```

```python
import functools
import math

import jax
import jax.numpy as jnp
from jax import lax
from jax.experimental import pallas as pl
from jax.experimental.pallas import tpu as pltpu
from jax.sharding import PartitionSpec as P

DH = 128
SPAN = 256
SLOTS = SPAN // 2


def attention_kernel(shifts, group, info, q_ref, g_ref, *refs):
    ins, refs = refs[: 4 + 4 * shifts], refs[4 + 4 * shifts :]
    outs, (key_buf, value_buf, weight_buf, slope_buf) = refs[: 3 + 2 * shifts], refs[3 + 2 * shifts :]
    rows = q_ref.shape[0]
    half = SLOTS // 2
    scale = DH ** (-0.5)
    log_scale = scale * math.log2(math.e)
    sub = info[0]

    at = 0
    for index in range(2 + 2 * shifts):
        key_piece, value_piece = ins[2 * index], ins[2 * index + 1]
        size = key_piece.shape[0]
        key_buf[at : at + size, :] = key_piece[...]
        value_buf[at : at + size, :] = value_piece[...]
        at += size
    key_all, value_all = key_buf[...], value_buf[...]

    width = 2 * rows
    nt = (((1,), (1,)), ((), ()))
    tn = (((0,), (0,)), ((), ()))
    key_at = lax.broadcasted_iota(jnp.int32, (rows, rows), 0)
    token_at = lax.broadcasted_iota(jnp.int32, (rows, rows), 1)
    causal = jnp.concatenate([key_at <= token_at] * 2, axis=1)
    slot_at = lax.broadcasted_iota(jnp.int32, (half, width), 0)
    minus = -jnp.inf

    for chunk in range(group // 2):
        cols = [slice((2 * chunk + i) * DH, (2 * chunk + i + 1) * DH) for i in range(2)]
        q_pair = jnp.concatenate([q_ref[:, c] for c in cols], axis=0)
        g_pair = jnp.concatenate([g_ref[:, c] for c in cols], axis=0)
        scores = lax.dot_general(key_all, q_pair, nt, preferred_element_type=jnp.float32)
        signal = lax.dot_general(value_all, g_pair, nt, preferred_element_type=jnp.float32)
        pieces = [
            jnp.where(causal, scores[:rows], minus),
            jnp.where(sub > 0, scores[rows : 2 * rows], minus),
        ]
        at = 2 * rows
        for shift in range(shifts):
            live = info[1 + shift]
            for first in (sub * half, (1 - sub) * half):
                pieces.append(jnp.where(slot_at < live - first, scores[at : at + half], minus))
                at += half
        scores = jnp.concatenate(pieces, axis=0)
        top = jnp.max(scores, axis=0, keepdims=True)
        grown = jnp.exp2(scores * log_scale - top * log_scale)
        total = jnp.sum(grown, axis=0, keepdims=True)
        probs = grown * (1.0 / total)
        weights = probs.astype(jnp.bfloat16)
        delta = jnp.sum(weights.astype(jnp.float32) * signal, axis=0, keepdims=True)
        slopes = (probs * (signal - delta)).astype(jnp.bfloat16)
        weight_buf[:, chunk * width : (chunk + 1) * width] = weights
        slope_buf[:, chunk * width : (chunk + 1) * width] = slopes
        dq = lax.dot_general(slopes, key_all, tn, preferred_element_type=jnp.float32) * scale
        outs[0][:, cols[0]] = dq[:rows].astype(jnp.bfloat16)
        outs[0][:, cols[1]] = dq[rows:].astype(jnp.bfloat16)

    q_all = jnp.concatenate([q_ref[:, i * DH : (i + 1) * DH] for i in range(group)], axis=0)
    g_all = jnp.concatenate([g_ref[:, i * DH : (i + 1) * DH] for i in range(group)], axis=0)
    dk = jnp.dot(slope_buf[...], q_all, preferred_element_type=jnp.float32) * scale
    dv = jnp.dot(weight_buf[...], g_all, preferred_element_type=jnp.float32)
    at = 0
    for out in outs[1:]:
        size = out.shape[0]
        out[:, :DH] = dk[at : at + size].astype(out.dtype)
        out[:, DH:] = dv[at : at + size].astype(out.dtype)
        at += size


def attention(info, queries, grad_out, mine, other, far_mine, far_other):
    shifts = len(far_mine)
    rows = queries.shape[0]
    heads = mine.shape[1] // (2 * DH)
    group = queries.shape[1] // (heads * DH)
    half = SLOTS // 2
    columns = 2 * rows + SLOTS * shifts
    wide = pl.BlockSpec((rows, group * DH), lambda h, info: (0, h))
    in_specs = [wide, wide]
    operands = [queries, grad_out]

    def add(array):
        size = array.shape[0]
        in_specs.append(pl.BlockSpec((size, DH), lambda h, info: (0, h)))
        in_specs.append(pl.BlockSpec((size, DH), lambda h, info: (0, heads + h)))
        operands.extend([array, array])

    add(mine)
    add(other)
    for own, sibling in zip(far_mine, far_other):
        add(own)
        add(sibling)
    sizes = [(rows, jnp.float32), (rows, jnp.bfloat16)]
    sizes += [(half, jnp.float32), (half, jnp.bfloat16)] * shifts
    out_shape = [jax.ShapeDtypeStruct(queries.shape, jnp.bfloat16)]
    out_specs = [wide]
    for size, dtype in sizes:
        out_shape.append(jax.ShapeDtypeStruct((size, heads * 2 * DH), dtype))
        out_specs.append(pl.BlockSpec((size, 2 * DH), lambda h, info: (0, h)))
    products = queries.shape[1] * rows * columns
    return pl.pallas_call(
        functools.partial(attention_kernel, shifts, group),
        out_shape=out_shape,
        grid_spec=pltpu.PrefetchScalarGridSpec(
            num_scalar_prefetch=1,
            grid=(heads,),
            in_specs=in_specs,
            out_specs=out_specs,
            scratch_shapes=[
                pltpu.VMEM((columns, DH), jnp.bfloat16),
                pltpu.VMEM((columns, DH), jnp.bfloat16),
                pltpu.VMEM((columns, group * rows), jnp.bfloat16),
                pltpu.VMEM((columns, group * rows), jnp.bfloat16),
            ],
        ),
        compiler_params=pltpu.CompilerParams(vmem_limit_bytes=40 * 1024 * 1024),
        cost_estimate=pl.CostEstimate(
            flops=10 * products, bytes_accessed=6 * queries.size, transcendentals=products // DH
        ),
    )(info, *operands)


def local(queries, keys, values, beacon_keys, beacon_values, grad_out, ratios):
    spans = ratios.shape[0]
    here = lax.axis_index("ctx")
    sub = lax.axis_index("sub")
    swap = [(0, 1), (1, 0)]
    beacons = jnp.concatenate([beacon_keys, beacon_values], axis=1)
    mine = jnp.concatenate([keys, values], axis=1)
    other = lax.ppermute(mine, "sub", [(0, 1)])
    shifts = range(1, spans)
    far_mine = [
        lax.ppermute(beacons, "ctx", [(i, i + k) for i in range(spans - k)]) for k in shifts
    ]
    far_other = [lax.ppermute(array, "sub", swap) for array in far_mine]
    live = SPAN // ratios
    seen = [jnp.where(here >= k, live[jnp.maximum(here - k, 0)], 0) for k in shifts]
    info = jnp.stack([sub.astype(jnp.int32)] + [x.astype(jnp.int32) for x in seen])
    grad_queries, near_mine, near_other, *far = attention(
        info, queries, grad_out, mine, other, far_mine, far_other
    )
    sums = []
    for k in shifts:
        own, sent = far[2 * (k - 1)], far[2 * (k - 1) + 1]
        pair = (own + lax.ppermute(sent, "sub", swap).astype(jnp.float32)).astype(jnp.bfloat16)
        sums.append(lax.ppermute(pair, "ctx", [(i + k, i) for i in range(spans - k)]))
    near = near_mine + lax.ppermute(near_other, "sub", [(1, 0)]).astype(jnp.float32)
    beacon = functools.reduce(jnp.add, [x.astype(jnp.float32) for x in sums])

    def split(array):
        parts = array.reshape(array.shape[0], -1, 2, DH).astype(jnp.bfloat16)
        return [parts[:, :, i].reshape(array.shape[0], -1) for i in range(2)]

    grad_keys, grad_values = split(near)
    grad_beacon_keys, grad_beacon_values = split(beacon)
    return grad_queries, grad_keys, grad_values, grad_beacon_keys, grad_beacon_values


def solution(mesh):
    rows = P(("grp", "ctx", "sub"), "tp")
    return jax.shard_map(
        local,
        mesh=mesh,
        in_specs=(rows,) * 6 + (P("grp"),),
        out_specs=(rows,) * 5,
        check_vma=False,
    )
```

```python
import functools
import math

import jax
import jax.numpy as jnp
from jax import lax
from jax.experimental import pallas as pl
from jax.experimental.pallas import tpu as pltpu
from jax.sharding import PartitionSpec as P

DH = 128
SPAN = 256
SLOTS = SPAN // 2


def attention_kernel(
    shifts, group, ratios, q_ref, g_ref, near_key, near_value, near_other, far_mine, far_other,
    dq_ref, mine_out, other_out, key_buf, value_buf, weight_buf, slope_buf,
):
    head = pl.program_id(0)
    here = lax.axis_index("ctx")
    sub = lax.axis_index("sub")
    spans = shifts + 1
    rows = q_ref.shape[0]
    half = SLOTS // 2
    wide = near_key.shape[1]
    scale = DH ** (-0.5)
    log_scale = scale * math.log2(math.e)
    key_cols = pl.ds(pl.multiple_of(head * DH, DH), DH)
    value_cols = pl.ds(pl.multiple_of(wide + head * DH, DH), DH)
    owners = [lax.rem(here - k + spans, spans) for k in range(1, spans)]

    key_buf[:rows, :] = near_key[:, key_cols]
    value_buf[:rows, :] = near_value[:, key_cols]
    key_buf[rows : 2 * rows, :] = near_other[:, key_cols]
    value_buf[rows : 2 * rows, :] = near_other[:, value_cols]
    at = 2 * rows
    for owner in owners:
        for far in (far_mine, far_other):
            key_buf[at : at + half, :] = far[owner, :, key_cols]
            value_buf[at : at + half, :] = far[owner, :, value_cols]
            at += half
    key_all, value_all = key_buf[...], value_buf[...]

    width = 2 * rows
    nt = (((1,), (1,)), ((), ()))
    tn = (((0,), (0,)), ((), ()))
    key_at = lax.broadcasted_iota(jnp.int32, (rows, rows), 0)
    token_at = lax.broadcasted_iota(jnp.int32, (rows, rows), 1)
    causal = jnp.concatenate([key_at <= token_at] * 2, axis=1)
    slot_at = lax.broadcasted_iota(jnp.int32, (half, width), 0)
    minus = -jnp.inf

    for chunk in range(group // 2):
        cols = [slice((2 * chunk + i) * DH, (2 * chunk + i + 1) * DH) for i in range(2)]
        q_pair = jnp.concatenate([q_ref[:, c] for c in cols], axis=0)
        g_pair = jnp.concatenate([g_ref[:, c] for c in cols], axis=0)
        scores = lax.dot_general(key_all, q_pair, nt, preferred_element_type=jnp.float32)
        signal = lax.dot_general(value_all, g_pair, nt, preferred_element_type=jnp.float32)
        pieces = [
            jnp.where(causal, scores[:rows], minus),
            jnp.where(sub > 0, scores[rows : 2 * rows], minus),
        ]
        at = 2 * rows
        for shift, owner in enumerate(owners):
            live = jnp.where(here > shift, SPAN // ratios[owner], 0)
            for first in (sub * half, (1 - sub) * half):
                pieces.append(jnp.where(slot_at < live - first, scores[at : at + half], minus))
                at += half
        scores = jnp.concatenate(pieces, axis=0)
        top = jnp.max(scores, axis=0, keepdims=True)
        grown = jnp.exp2(scores * log_scale - top * log_scale)
        total = jnp.sum(grown, axis=0, keepdims=True)
        probs = grown * (1.0 / total)
        weights = probs.astype(jnp.bfloat16)
        delta = jnp.sum(weights.astype(jnp.float32) * signal, axis=0, keepdims=True)
        slopes = (probs * (signal - delta)).astype(jnp.bfloat16)
        weight_buf[:, chunk * width : (chunk + 1) * width] = weights
        slope_buf[:, chunk * width : (chunk + 1) * width] = slopes
        dq = lax.dot_general(slopes, key_all, tn, preferred_element_type=jnp.float32) * scale
        dq_ref[:, cols[0]] = dq[:rows].astype(jnp.bfloat16)
        dq_ref[:, cols[1]] = dq[rows:].astype(jnp.bfloat16)

    q_all = jnp.concatenate([q_ref[:, i * DH : (i + 1) * DH] for i in range(group)], axis=0)
    g_all = jnp.concatenate([g_ref[:, i * DH : (i + 1) * DH] for i in range(group)], axis=0)
    dk = jnp.dot(slope_buf[...], q_all, preferred_element_type=jnp.float32) * scale
    dv = jnp.dot(weight_buf[...], g_all, preferred_element_type=jnp.float32)

    def put(out, row, size, at):
        out[pl.ds(row, size), key_cols] = dk[at : at + size].astype(out.dtype)
        out[pl.ds(row, size), value_cols] = dv[at : at + size].astype(out.dtype)

    put(mine_out, 0, rows, 0)
    put(other_out, 0, rows, rows)
    at = 2 * rows
    for owner in owners:
        for out in (mine_out, other_out):
            put(out, pl.multiple_of(rows + owner * half, half), half, at)
            at += half
    own = pl.ds(pl.multiple_of(rows + here * half, half), half)
    for out in (mine_out, other_out):
        out[own, key_cols] = jnp.zeros((half, DH), out.dtype)
        out[own, value_cols] = jnp.zeros((half, DH), out.dtype)


def attention(ratios, queries, grad_out, near_key, near_value, near_other, far_mine, far_other):
    spans = far_mine.shape[0]
    rows = queries.shape[0]
    heads = near_key.shape[1] // DH
    group = queries.shape[1] // (heads * DH)
    columns = 2 * rows + SLOTS * (spans - 1)
    wide = pl.BlockSpec((rows, group * DH), lambda h, r: (0, h))

    def full(array):
        return pl.BlockSpec(array.shape, lambda h, r: (0,) * len(array.shape))

    fixed = [near_key, near_value, near_other, far_mine, far_other]
    out_rows = rows + spans * SLOTS // 2
    outs = [
        jax.ShapeDtypeStruct((out_rows, 2 * heads * DH), jnp.float32),
        jax.ShapeDtypeStruct((out_rows, 2 * heads * DH), jnp.bfloat16),
    ]
    products = queries.shape[1] * rows * columns
    return pl.pallas_call(
        functools.partial(attention_kernel, spans - 1, group),
        out_shape=[jax.ShapeDtypeStruct(queries.shape, jnp.bfloat16)] + outs,
        grid_spec=pltpu.PrefetchScalarGridSpec(
            num_scalar_prefetch=1,
            grid=(heads,),
            in_specs=[wide, wide] + [full(x) for x in fixed],
            out_specs=[wide] + [full(x) for x in outs],
            scratch_shapes=[
                pltpu.VMEM((columns, DH), jnp.bfloat16),
                pltpu.VMEM((columns, DH), jnp.bfloat16),
                pltpu.VMEM((columns, group * rows), jnp.bfloat16),
                pltpu.VMEM((columns, group * rows), jnp.bfloat16),
            ],
        ),
        compiler_params=pltpu.CompilerParams(vmem_limit_bytes=48 * 1024 * 1024),
        cost_estimate=pl.CostEstimate(
            flops=10 * products, bytes_accessed=6 * queries.size, transcendentals=products // DH
        ),
    )(ratios, queries, grad_out, *fixed)


def local(queries, keys, values, beacon_keys, beacon_values, grad_out, ratios):
    spans = ratios.shape[0]
    rows, wide = keys.shape
    half = SLOTS // 2
    swap = [(0, 1), (1, 0)]
    beacons = jnp.concatenate([beacon_keys, beacon_values], axis=1)
    near_other = lax.ppermute(jnp.concatenate([keys, values], axis=1), "sub", [(0, 1)])
    far_mine = lax.all_gather(beacons, "ctx", axis=0)
    far_other = lax.ppermute(far_mine, "sub", swap)
    grad_queries, mine, other = attention(
        ratios, queries, grad_out, keys, values, near_other, far_mine, far_other
    )
    both = mine + lax.ppermute(other, "sub", swap).astype(jnp.float32)
    near = both[:rows].astype(jnp.bfloat16)
    sent = both[rows:].astype(jnp.bfloat16).reshape(spans, half, 2 * wide)
    got = lax.all_to_all(sent, "ctx", split_axis=0, concat_axis=0)
    beacon = jnp.sum(got.astype(jnp.float32), axis=0).astype(jnp.bfloat16)
    return grad_queries, near[:, :wide], near[:, wide:], beacon[:, :wide], beacon[:, wide:]


def solution(mesh):
    rows = P(("grp", "ctx", "sub"), "tp")
    return jax.shard_map(
        local,
        mesh=mesh,
        in_specs=(rows,) * 6 + (P("grp"),),
        out_specs=(rows,) * 5,
        check_vma=False,
    )
```

```python
import functools
import math

import jax
import jax.numpy as jnp
from jax import lax
from jax.experimental import pallas as pl
from jax.experimental.pallas import tpu as pltpu
from jax.sharding import PartitionSpec as P

DH = 128
SPAN = 256
SLOTS = SPAN // 2
NT = (((1,), (1,)), ((), ()))


def attention_kernel(shifts, heads, group, ratios, q_hbm, g_hbm, *refs):
    pieces = 2 + 2 * shifts
    ins, refs = refs[: 2 * pieces], refs[2 * pieces :]
    dq_hbm, outs, refs = refs[0], refs[1 : 1 + 2 * pieces], refs[1 + 2 * pieces :]
    (q_buf, g_buf, dq_buf, key_buf, value_buf, turned_buf, bias_buf, dk_buf, dv_buf) = refs[:9]
    sets, (in_sem, out_sem) = (refs[9:14], refs[14:19]), refs[19:]
    rows = q_buf.shape[0]
    half = SLOTS // 2
    columns = key_buf.shape[1]
    width = 2 * rows
    per_head = group // 2
    scale = DH ** (-0.5)
    log_scale = scale * math.log2(math.e)
    here = lax.axis_index("ctx")
    sub = lax.axis_index("sub")

    loads = [pltpu.make_async_copy(q_hbm, q_buf, in_sem.at[0]), pltpu.make_async_copy(g_hbm, g_buf, in_sem.at[1])]
    for load in loads:
        load.start()

    at = 0
    for index in range(pieces):
        size = ins[2 * index].shape[0]
        for head in range(heads):
            cols = slice(head * DH, (head + 1) * DH)
            key_buf[head, at : at + size, :] = ins[2 * index][:, cols]
            value_buf[head, at : at + size, :] = ins[2 * index + 1][:, cols]
        at += size
    for head in range(heads):
        turned_buf[head] = key_buf[head].T

    def bias_of(seen):
        return jnp.where(seen, 0.0, -jnp.inf).astype(jnp.float32)

    key_at = lax.broadcasted_iota(jnp.int32, (rows, DH), 0)
    token_at = lax.broadcasted_iota(jnp.int32, (rows, DH), 1)
    slot_at = lax.broadcasted_iota(jnp.int32, (half, DH), 0)
    bias_buf[:rows, :] = bias_of(key_at <= token_at)
    bias_buf[rows : 2 * rows, :] = bias_of(key_at < sub * rows)
    at = 2 * rows
    for shift in range(shifts):
        owner = jnp.maximum(here - 1 - shift, 0)
        live = jnp.where(here > shift, SPAN // ratios[owner], 0)
        for first in (sub * half, (1 - sub) * half):
            bias_buf[at : at + half, :] = bias_of(slot_at < live - first)
            at += half
    dk_buf[...] = jnp.zeros_like(dk_buf)
    dv_buf[...] = jnp.zeros_like(dv_buf)
    for _, _, _, weights, slopes in sets:
        weights[...] = jnp.zeros_like(weights)
        slopes[...] = jnp.zeros_like(slopes)
    for load in loads:
        load.wait()

    def pair(buf, chunk):
        first = pl.multiple_of(chunk * width, width)
        return jnp.concatenate(
            [buf[:, pl.ds(first, DH)], buf[:, pl.ds(pl.multiple_of(first + DH, DH), DH)]], axis=0
        )

    def products(chunk, buffers):
        score_ref, signal_ref, top_ref, _, _ = buffers
        head = chunk // per_head
        scores = lax.dot_general(key_buf[head], pair(q_buf, chunk), NT, preferred_element_type=jnp.float32)
        bias = bias_buf[...]
        scores = scores + jnp.concatenate([bias, bias], axis=1)
        score_ref[...] = scores
        top_ref[...] = jnp.max(scores, axis=0, keepdims=True)
        signal_ref[...] = lax.dot_general(
            value_buf[head], pair(g_buf, chunk), NT, preferred_element_type=jnp.float32
        )

    def softmax(buffers):
        score_ref, signal_ref, top_ref, weight_ref, slope_ref = buffers
        grown = jnp.exp2((score_ref[...] - top_ref[...]) * log_scale)
        total = jnp.sum(grown, axis=0, keepdims=True)
        probs = grown * (1.0 / total)
        weights = probs.astype(jnp.bfloat16)
        weight_ref[...] = weights
        signal = signal_ref[...]
        delta = jnp.sum(weights.astype(jnp.float32) * signal, axis=0, keepdims=True)
        slope_ref[...] = (probs * (signal - delta)).astype(jnp.bfloat16)

    def gradients(chunk, buffers):
        _, _, _, weight_ref, slope_ref = buffers
        head = chunk // per_head
        slopes = slope_ref[...]
        dk_buf[head] += jnp.dot(slopes, pair(q_buf, chunk), preferred_element_type=jnp.float32)
        dv_buf[head] += jnp.dot(weight_ref[...], pair(g_buf, chunk), preferred_element_type=jnp.float32)
        turned = jnp.dot(turned_buf[head], slopes, preferred_element_type=jnp.float32)
        dq = (turned.T * scale).astype(jnp.bfloat16)
        first = pl.multiple_of(chunk * width, width)
        dq_buf[:, pl.ds(first, DH)] = dq[:rows]
        dq_buf[:, pl.ds(pl.multiple_of(first + DH, DH), DH)] = dq[rows:]

    chunks = heads * per_head
    even, odd = sets
    products(0, even)

    def body(step, carry):
        chunk = 2 * step
        products(chunk + 1, odd)
        softmax(even)
        gradients(jnp.maximum(chunk - 1, 0), odd)
        products(jnp.minimum(chunk + 2, chunks - 1), even)
        softmax(odd)
        gradients(chunk, even)
        return carry

    lax.fori_loop(0, chunks // 2, body, 0)
    gradients(chunks - 1, odd)
    store = pltpu.make_async_copy(dq_buf, dq_hbm, out_sem)
    store.start()

    at = 0
    for index in range(pieces):
        key_out, value_out = outs[2 * index], outs[2 * index + 1]
        size = key_out.shape[0]
        for head in range(heads):
            cols = slice(head * DH, (head + 1) * DH)
            key_out[:, cols] = (dk_buf[head, at : at + size, :] * scale).astype(key_out.dtype)
            value_out[:, cols] = dv_buf[head, at : at + size, :].astype(value_out.dtype)
        at += size
    store.wait()


def attention(ratios, queries, grad_out, pieces):
    rows = queries.shape[0]
    wide = pieces[0][0].shape[1]
    heads = wide // DH
    group = queries.shape[1] // wide
    columns = sum(keys.shape[0] for keys, _ in pieces)
    shifts = len(pieces) // 2 - 1
    width = 2 * rows
    flat = [array for piece in pieces for array in piece]
    out_shape = [jax.ShapeDtypeStruct(queries.shape, jnp.bfloat16)]
    for index, piece in enumerate(pieces):
        dtype = jnp.bfloat16 if index % 2 else jnp.float32
        out_shape += [jax.ShapeDtypeStruct(array.shape, dtype) for array in piece]
    hbm = pl.BlockSpec(memory_space=pltpu.HBM)
    vmem = pl.BlockSpec(memory_space=pltpu.VMEM)
    buffers = [
        pltpu.VMEM((columns, width), jnp.float32),
        pltpu.VMEM((columns, width), jnp.float32),
        pltpu.VMEM((1, width), jnp.float32),
        pltpu.VMEM((columns, width), jnp.bfloat16),
        pltpu.VMEM((columns, width), jnp.bfloat16),
    ]
    products = queries.shape[1] * rows * columns
    return pl.pallas_call(
        functools.partial(attention_kernel, shifts, heads, group),
        out_shape=out_shape,
        in_specs=[pl.BlockSpec(memory_space=pltpu.SMEM), hbm, hbm] + [vmem] * len(flat),
        out_specs=[hbm] + [vmem] * len(flat),
        scratch_shapes=[
            pltpu.VMEM(queries.shape, jnp.bfloat16),
            pltpu.VMEM(queries.shape, jnp.bfloat16),
            pltpu.VMEM(queries.shape, jnp.bfloat16),
            pltpu.VMEM((heads, columns, DH), jnp.bfloat16),
            pltpu.VMEM((heads, columns, DH), jnp.bfloat16),
            pltpu.VMEM((heads, DH, columns), jnp.bfloat16),
            pltpu.VMEM((columns, DH), jnp.float32),
            pltpu.VMEM((heads, columns, DH), jnp.float32),
            pltpu.VMEM((heads, columns, DH), jnp.float32),
        ]
        + buffers * 2
        + [pltpu.SemaphoreType.DMA((2,)), pltpu.SemaphoreType.DMA],
        compiler_params=pltpu.CompilerParams(vmem_limit_bytes=48 * 1024 * 1024),
        cost_estimate=pl.CostEstimate(
            flops=10 * products, bytes_accessed=6 * queries.size, transcendentals=products // DH
        ),
    )(ratios, queries, grad_out, *flat)


def local(queries, keys, values, beacon_keys, beacon_values, grad_out, ratios):
    spans = ratios.shape[0]
    swap = [(0, 1), (1, 0)]
    up = [(i, i + 1) for i in range(spans - 1)]
    down = [(i + 1, i) for i in range(spans - 1)]
    near = (keys, values)
    pieces = [near, tuple(lax.ppermute(x, "sub", [(0, 1)]) for x in near)]
    held = (beacon_keys, beacon_values)
    for _ in range(spans - 1):
        held = tuple(lax.ppermute(x, "ctx", up) for x in held)
        pieces += [held, tuple(lax.ppermute(x, "sub", swap) for x in held)]
    grad_queries, *grads = attention(ratios, queries, grad_out, pieces)
    held = (None, None)
    for k in range(spans - 1, 0, -1):
        own, sent = grads[4 * k : 4 * k + 2], grads[4 * k + 2 : 4 * k + 4]
        sums = [x + lax.ppermute(y, "sub", swap).astype(jnp.float32) for x, y in zip(own, sent)]
        sums = [x if y is None else x + y.astype(jnp.float32) for x, y in zip(sums, held)]
        held = tuple(lax.ppermute(x.astype(jnp.bfloat16), "ctx", down) for x in sums)
    near = [
        (x + lax.ppermute(y, "sub", [(1, 0)]).astype(jnp.float32)).astype(jnp.bfloat16)
        for x, y in zip(grads[:2], grads[2:4])
    ]
    return grad_queries, near[0], near[1], held[0], held[1]


def solution(mesh):
    rows = P(("grp", "ctx", "sub"), "tp")
    return jax.shard_map(
        local,
        mesh=mesh,
        in_specs=(rows,) * 6 + (P("grp"),),
        out_specs=(rows,) * 5,
        check_vma=False,
    )
```

```python
import functools
import math

import jax
import jax.numpy as jnp
from jax import lax
from jax.experimental import pallas as pl
from jax.experimental.pallas import tpu as pltpu
from jax.sharding import PartitionSpec as P

DH = 128
SPAN = 256
SLOTS = SPAN // 2
NT = (((1,), (1,)), ((), ()))
HIDDEN = -3e38
JOIN = 4
BLOCK = 16


def attention_kernel(shifts, heads, group, ratios, q_hbm, g_hbm, key_hbm, value_hbm, near_other, *refs):
    far, refs = refs[: 2 * shifts], refs[2 * shifts :]
    dq_hbm, outs, refs = refs[0], refs[1 : 3 + 2 * shifts], refs[3 + 2 * shifts :]
    (q_buf, g_buf, dq_buf, near_key, near_value, key_buf, value_buf, turned_buf, dk_buf, dv_buf) = refs[:10]
    sets, (in_sem, out_sem) = (refs[10:14], refs[14:18]), refs[18:]
    rows = q_buf.shape[0]
    wide = heads * DH
    half = SLOTS // 2
    columns = key_buf.shape[1]
    width = JOIN * rows
    per_head = group // JOIN
    scale = DH ** (-0.5)
    log_scale = scale * math.log2(math.e)
    here = lax.axis_index("ctx")
    sub = lax.axis_index("sub")

    loads = [
        pltpu.make_async_copy(source, target, in_sem.at[index])
        for index, (source, target) in enumerate(
            [(key_hbm, near_key), (value_hbm, near_value), (q_hbm, q_buf), (g_hbm, g_buf)]
        )
    ]
    for load in loads:
        load.start()

    def place(at, keys, values, seen):
        mask = jnp.where(seen, 0.0, HIDDEN).astype(jnp.bfloat16)
        size = mask.shape[0]
        for head in range(heads):
            cols = slice(head * DH, (head + 1) * DH)
            key_buf[head, at : at + size, :DH] = keys[:, cols]
            key_buf[head, at : at + size, DH:] = mask
            value_buf[head, at : at + size, :] = values[:, cols]

    key_at = lax.broadcasted_iota(jnp.int32, (rows, DH), 0)
    token_at = lax.broadcasted_iota(jnp.int32, (rows, DH), 1)
    slot_at = lax.broadcasted_iota(jnp.int32, (half, DH), 0)
    place(rows, near_other.at[:, :wide], near_other.at[:, wide:], key_at < sub * rows)
    at = 2 * rows
    for shift in range(shifts):
        owner = jnp.maximum(here - 1 - shift, 0)
        live = jnp.where(here > shift, SPAN // ratios[owner], 0)
        for side, first in enumerate((sub * half, (1 - sub) * half)):
            source = far[2 * shift + side]
            place(at, source.at[:, :wide], source.at[:, wide:], slot_at < live - first)
            at += half
    dk_buf[...] = jnp.zeros_like(dk_buf)
    dv_buf[...] = jnp.zeros_like(dv_buf)
    for _, _, weights, slopes in sets:
        weights[...] = jnp.zeros_like(weights)
        slopes[...] = jnp.zeros_like(slopes)
    loads[0].wait()
    loads[1].wait()
    place(0, near_key, near_value, key_at <= token_at)
    for head in range(heads):
        turned_buf[head] = key_buf[head, :, :DH].T
    loads[2].wait()
    loads[3].wait()

    def columns_of(chunk, index):
        return pl.ds(pl.multiple_of((chunk * JOIN + index) * DH, DH), DH)

    def joined(buf, chunk):
        return jnp.concatenate([buf[:, columns_of(chunk, i)] for i in range(JOIN)], axis=0)

    def products(chunk, buffers):
        score_ref, signal_ref, _, _ = buffers
        head = chunk // per_head
        one_hot = jnp.where(key_at == token_at, 1.0, 0.0).astype(jnp.bfloat16)
        queries = jnp.concatenate([joined(q_buf, chunk), jnp.concatenate([one_hot] * JOIN, axis=0)], axis=1)
        score_ref[...] = lax.dot_general(key_buf[head], queries, NT, preferred_element_type=jnp.float32)
        signal_ref[...] = lax.dot_general(
            value_buf[head], joined(g_buf, chunk), NT, preferred_element_type=jnp.float32
        )

    def softmax(buffers):
        score_ref, signal_ref, weight_ref, slope_ref = buffers
        blocks = [slice(at, at + BLOCK) for at in range(0, columns, BLOCK)]
        fold = lambda x: x.reshape(BLOCK // 8, 8, width)
        top = jnp.full((8, width), HIDDEN, jnp.float32)
        for block in blocks:
            top = jnp.maximum(top, jnp.max(fold(score_ref[block, :]), axis=0))
        top = jnp.max(top, axis=0, keepdims=True)
        total = jnp.zeros((8, width), jnp.float32)
        for block in blocks:
            grown = jnp.exp2((score_ref[block, :] - top) * log_scale)
            score_ref[block, :] = grown
            total = total + jnp.sum(fold(grown), axis=0)
        share = 1.0 / jnp.sum(total, axis=0, keepdims=True)
        delta = jnp.zeros((8, width), jnp.float32)
        for block in blocks:
            weights = (score_ref[block, :] * share).astype(jnp.bfloat16)
            weight_ref[block, :] = weights
            delta = delta + jnp.sum(fold(weights.astype(jnp.float32) * signal_ref[block, :]), axis=0)
        delta = jnp.sum(delta, axis=0, keepdims=True)
        for block in blocks:
            probs = score_ref[block, :] * share
            slope_ref[block, :] = (probs * (signal_ref[block, :] - delta)).astype(jnp.bfloat16)

    def gradients(chunk, buffers):
        _, _, weight_ref, slope_ref = buffers
        head = chunk // per_head
        slopes = slope_ref[...]
        dk_buf[head] += jnp.dot(slopes, joined(q_buf, chunk), preferred_element_type=jnp.float32)
        dv_buf[head] += jnp.dot(weight_ref[...], joined(g_buf, chunk), preferred_element_type=jnp.float32)
        turned = jnp.dot(turned_buf[head], slopes, preferred_element_type=jnp.float32)
        for i in range(JOIN):
            piece = turned[:, i * rows : (i + 1) * rows].T
            dq_buf[:, columns_of(chunk, i)] = (piece * scale).astype(jnp.bfloat16)

    chunks = heads * per_head
    even, odd = sets
    products(0, even)

    def body(step, carry):
        chunk = 2 * step
        products(chunk + 1, odd)
        softmax(even)
        gradients(jnp.maximum(chunk - 1, 0), odd)
        products(jnp.minimum(chunk + 2, chunks - 1), even)
        softmax(odd)
        gradients(chunk, even)
        return carry

    lax.fori_loop(0, chunks // 2, body, 0)
    gradients(chunks - 1, odd)
    store = pltpu.make_async_copy(dq_buf, dq_hbm, out_sem)
    store.start()

    at = 0
    for out in outs:
        size = out.shape[0]
        for head in range(heads):
            cols = slice(head * DH, (head + 1) * DH)
            out[:, cols] = (dk_buf[head, at : at + size, :] * scale).astype(out.dtype)
            cols = slice(wide + head * DH, wide + (head + 1) * DH)
            out[:, cols] = dv_buf[head, at : at + size, :].astype(out.dtype)
        at += size
    store.wait()


def attention(ratios, queries, grad_out, keys, values, near_other, far):
    rows, wide = keys.shape
    heads = wide // DH
    group = queries.shape[1] // wide
    shifts = len(far) // 2
    columns = 2 * rows + SLOTS * shifts
    width = JOIN * rows
    out_shape = [jax.ShapeDtypeStruct(queries.shape, jnp.bfloat16)]
    for index, size in enumerate([rows] * 2 + [SLOTS // 2] * (2 * shifts)):
        out_shape.append(jax.ShapeDtypeStruct((size, 2 * wide), jnp.bfloat16 if index % 2 else jnp.float32))
    hbm = pl.BlockSpec(memory_space=pltpu.HBM)
    vmem = pl.BlockSpec(memory_space=pltpu.VMEM)
    buffers = [
        pltpu.VMEM((columns, width), jnp.float32),
        pltpu.VMEM((columns, width), jnp.float32),
        pltpu.VMEM((columns, width), jnp.bfloat16),
        pltpu.VMEM((columns, width), jnp.bfloat16),
    ]
    products = queries.shape[1] * rows * columns
    fixed = [pltpu.with_memory_space_constraint(x, pltpu.HBM) for x in (queries, grad_out, keys, values)]
    return pl.pallas_call(
        functools.partial(attention_kernel, shifts, heads, group),
        out_shape=out_shape,
        in_specs=[pl.BlockSpec(memory_space=pltpu.SMEM)] + [hbm] * 4 + [vmem] * (1 + 2 * shifts),
        out_specs=[hbm] + [vmem] * (2 + 2 * shifts),
        scratch_shapes=[
            pltpu.VMEM(queries.shape, jnp.bfloat16),
            pltpu.VMEM(queries.shape, jnp.bfloat16),
            pltpu.VMEM(queries.shape, jnp.bfloat16),
            pltpu.VMEM(keys.shape, jnp.bfloat16),
            pltpu.VMEM(keys.shape, jnp.bfloat16),
            pltpu.VMEM((heads, columns, 2 * DH), jnp.bfloat16),
            pltpu.VMEM((heads, columns, DH), jnp.bfloat16),
            pltpu.VMEM((heads, DH, columns), jnp.bfloat16),
            pltpu.VMEM((heads, columns, DH), jnp.float32),
            pltpu.VMEM((heads, columns, DH), jnp.float32),
        ]
        + buffers * 2
        + [pltpu.SemaphoreType.DMA((4,)), pltpu.SemaphoreType.DMA],
        compiler_params=pltpu.CompilerParams(vmem_limit_bytes=48 * 1024 * 1024),
        cost_estimate=pl.CostEstimate(
            flops=10 * products, bytes_accessed=6 * queries.size, transcendentals=products // DH
        ),
    )(ratios, *fixed, near_other, *far)


def local(queries, keys, values, beacon_keys, beacon_values, grad_out, ratios):
    spans = ratios.shape[0]
    wide = keys.shape[1]
    swap = [(0, 1), (1, 0)]
    shifts = range(1, spans)

    def up(k):
        return [(i, (i + k) % spans) for i in range(spans)]

    beacons = jnp.concatenate([beacon_keys, beacon_values], axis=1)
    near_other = lax.ppermute(jnp.concatenate([keys, values], axis=1), "sub", swap)
    order = sorted(shifts, key=lambda k: abs(2 * k - spans))
    own = {k: lax.ppermute(beacons, "ctx", up(k)) for k in reversed(order)}
    other = {k: lax.ppermute(own[k], "sub", swap) for k in order}
    far = [x[k] for k in shifts for x in (own, other)]
    grad_queries, near_own, near_sent, *grads = attention(
        ratios, queries, grad_out, keys, values, near_other, far
    )
    sums = []
    for k in order:
        own, sent = grads[2 * k - 2 : 2 * k]
        pair = own + lax.ppermute(sent, "sub", swap).astype(jnp.float32)
        sums.append(lax.ppermute(pair.astype(jnp.bfloat16), "ctx", up(-k)).astype(jnp.float32))
    near = near_own + lax.ppermute(near_sent, "sub", swap).astype(jnp.float32)
    beacon = functools.reduce(jnp.add, sums)
    outs = [x.astype(jnp.bfloat16) for y in (near, beacon) for x in (y[:, :wide], y[:, wide:])]
    return (grad_queries, *outs)


def solution(mesh):
    rows = P(("grp", "ctx", "sub"), "tp")
    return jax.shard_map(
        local,
        mesh=mesh,
        in_specs=(rows,) * 6 + (P("grp"),),
        out_specs=(rows,) * 5,
        check_vma=False,
    )
```

```python
import functools
import math

import jax
import jax.numpy as jnp
from jax import lax
from jax.experimental import pallas as pl
from jax.experimental.pallas import tpu as pltpu
from jax.sharding import PartitionSpec as P

DH = 128
SPAN = 256
SLOTS = SPAN // 2
NT = (((1,), (1,)), ((), ()))
HIDDEN = -3e38
JOIN = 4
BLOCK = 16


def interleave(first, second):
    few, many = sorted((first, second), key=len)
    done = 0
    for index, step in enumerate(few):
        step()
        upto = len(many) * (index + 1) // len(few)
        for other in many[done:upto]:
            other()
        done = upto
    for other in many[done:]:
        other()


def attention_kernel(shifts, heads, group, ratios, q_hbm, g_hbm, key_hbm, value_hbm, near_other, *refs):
    far, refs = refs[: 2 * shifts], refs[2 * shifts :]
    dq_hbm, outs, refs = refs[0], refs[1 : 3 + 2 * shifts], refs[3 + 2 * shifts :]
    (q_buf, g_buf, dq_buf, near_key, near_value, key_buf, value_buf, turned_buf, dk_buf, dv_buf) = refs[:10]
    sets, (near_sem, in_sem, out_sem) = (refs[10:14], refs[14:18]), refs[18:]
    rows = q_buf.shape[0]
    wide = heads * DH
    half = SLOTS // 2
    columns = key_buf.shape[1]
    width = JOIN * rows
    per_head = group // JOIN
    chunks = heads * per_head
    scale = DH ** (-0.5)
    log_scale = scale * math.log2(math.e)
    here = lax.axis_index("ctx")
    sub = lax.axis_index("sub")

    near_loads = [
        pltpu.make_async_copy(key_hbm, near_key, near_sem.at[0]),
        pltpu.make_async_copy(value_hbm, near_value, near_sem.at[1]),
    ]
    loads, stores = [], []
    for head in range(heads):
        cols = slice(head * group * DH, (head + 1) * group * DH)
        loads.append(
            [
                pltpu.make_async_copy(q_hbm.at[:, cols], q_buf.at[:, cols], in_sem.at[2 * head]),
                pltpu.make_async_copy(g_hbm.at[:, cols], g_buf.at[:, cols], in_sem.at[2 * head + 1]),
            ]
        )
        stores.append(pltpu.make_async_copy(dq_buf.at[:, cols], dq_hbm.at[:, cols], out_sem.at[head]))
    for load in near_loads + loads[0]:
        load.start()
    for load in sum(loads[1:], []):
        load.start()

    def place(at, keys, values, seen):
        mask = jnp.where(seen, 0.0, HIDDEN).astype(jnp.bfloat16)
        size = mask.shape[0]
        for head in range(heads):
            cols = slice(head * DH, (head + 1) * DH)
            key_buf[head, at : at + size, :DH] = keys[:, cols]
            key_buf[head, at : at + size, DH:] = mask
            value_buf[head, at : at + size, :] = values[:, cols]

    key_at = lax.broadcasted_iota(jnp.int32, (rows, DH), 0)
    token_at = lax.broadcasted_iota(jnp.int32, (rows, DH), 1)
    slot_at = lax.broadcasted_iota(jnp.int32, (half, DH), 0)
    place(rows, near_other.at[:, :wide], near_other.at[:, wide:], key_at < sub * rows)
    at = 2 * rows
    for shift in range(shifts):
        owner = jnp.maximum(here - 1 - shift, 0)
        live = jnp.where(here > shift, SPAN // ratios[owner], 0)
        for side, first in enumerate((sub * half, (1 - sub) * half)):
            source = far[2 * shift + side]
            place(at, source.at[:, :wide], source.at[:, wide:], slot_at < live - first)
            at += half
    for load in near_loads:
        load.wait()
    place(0, near_key, near_value, key_at <= token_at)
    one_hot = jnp.where(key_at == token_at, 1.0, 0.0).astype(jnp.bfloat16)

    def joined(buf, chunk, start, count):
        first = (chunk * JOIN + start) * DH
        return jnp.concatenate([buf[:, first + i * DH : first + (i + 1) * DH] for i in range(count)], axis=0)

    def products(chunk):
        score_ref, signal_ref, _, _ = sets[chunk % 2]
        head = chunk // per_head

        def score(start):
            cols = slice(start * rows, (start + 2) * rows)
            queries = jnp.concatenate(
                [joined(q_buf, chunk, start, 2), jnp.concatenate([one_hot] * 2, axis=0)], axis=1
            )
            score_ref[:, cols] = lax.dot_general(key_buf[head], queries, NT, preferred_element_type=jnp.float32)

        def signal(start):
            cols = slice(start * rows, (start + 2) * rows)
            signal_ref[:, cols] = lax.dot_general(
                value_buf[head], joined(g_buf, chunk, start, 2), NT, preferred_element_type=jnp.float32
            )

        def begin():
            if chunk % per_head == 0:
                for load in loads[head]:
                    load.wait()
                turned_buf[head] = key_buf[head, :, :DH].T

        begin()
        return [functools.partial(f, start) for f in (score, signal) for start in range(0, JOIN, 2)]

    def softmax(chunk):
        score_ref, signal_ref, weight_ref, slope_ref = sets[chunk % 2]
        state = {}

        def spread(x):
            return jnp.broadcast_to(x, (8, width))

        def begin_top():
            state["top"] = jnp.full((8, width), HIDDEN, jnp.float32)

        def top(at):
            for i in range(at, at + BLOCK, 8):
                state["top"] = jnp.maximum(state["top"], score_ref[i : i + 8, :])

        def end_top():
            state["top"] = spread(jnp.max(state["top"], axis=0, keepdims=True))
            state["total"] = jnp.zeros((8, width), jnp.float32)

        def grow(at):
            for i in range(at, at + BLOCK, 8):
                grown = jnp.exp2((score_ref[i : i + 8, :] - state["top"]) * log_scale)
                score_ref[i : i + 8, :] = grown
                state["total"] = state["total"] + grown

        def end_grow():
            state["share"] = spread(1.0 / jnp.sum(state["total"], axis=0, keepdims=True))
            state["delta"] = jnp.zeros((8, width), jnp.float32)

        def weigh(at):
            probs = [score_ref[i : i + 8, :] * state["share"] for i in range(at, at + BLOCK, 8)]
            weights = jnp.concatenate(probs, axis=0).astype(jnp.bfloat16)
            weight_ref[at : at + BLOCK, :] = weights
            terms = weights.astype(jnp.float32) * signal_ref[at : at + BLOCK, :]
            for i in range(0, BLOCK, 8):
                state["delta"] = state["delta"] + terms[i : i + 8]

        def end_weigh():
            state["delta"] = spread(jnp.sum(state["delta"], axis=0, keepdims=True))

        def slope(at):
            slopes = []
            for i in range(at, at + BLOCK, 8):
                probs = score_ref[i : i + 8, :] * state["share"]
                slopes.append(probs * (signal_ref[i : i + 8, :] - state["delta"]))
            slope_ref[at : at + BLOCK, :] = jnp.concatenate(slopes, axis=0).astype(jnp.bfloat16)

        steps = [begin_top]
        for work, end in ((top, end_top), (grow, end_grow), (weigh, end_weigh), (slope, None)):
            steps += [functools.partial(work, at) for at in range(0, columns, BLOCK)]
            steps += [end] if end else []
        return steps

    def gradients(chunk):
        _, _, weight_ref, slope_ref = sets[chunk % 2]
        head = chunk // per_head
        last = chunk % per_head == per_head - 1

        def piece(buf, start, left_ref):
            cols = slice(start * rows, (start + 2) * rows)
            return jnp.dot(left_ref[:, cols], joined(buf, chunk, start, 2), preferred_element_type=jnp.float32)

        def collect(total_ref, buf, left_ref, side, factor):
            total = piece(buf, 0, left_ref)
            for start in range(2, JOIN, 2):
                total = total + piece(buf, start, left_ref)
            if chunk % per_head:
                total = total + total_ref[...]
            if not last:
                total_ref[...] = total
                return
            cols = slice(side * wide + head * DH, side * wide + (head + 1) * DH)
            at = 0
            for out in outs:
                size = out.shape[0]
                out[:, cols] = (total[at : at + size] * factor).astype(out.dtype)
                at += size

        def turn(start):
            cols = slice(start * rows, (start + 2) * rows)
            turned = jnp.dot(turned_buf[head], slope_ref[:, cols], preferred_element_type=jnp.float32)
            for i in range(2):
                first = (chunk * JOIN + start + i) * DH
                dq = turned[:, i * rows : (i + 1) * rows].T * scale
                dq_buf[:, first : first + DH] = dq.astype(jnp.bfloat16)

        steps = [
            functools.partial(collect, dk_buf, q_buf, slope_ref, 0, scale),
            functools.partial(collect, dv_buf, g_buf, weight_ref, 1, 1.0),
        ]
        steps += [functools.partial(turn, start) for start in range(0, JOIN, 2)]
        if last:
            steps.append(stores[head].start)
        return steps

    for step in products(0):
        step()
    for chunk in range(chunks):
        matrix = gradients(chunk - 1) if chunk > 0 else []
        matrix = matrix + (products(chunk + 1) if chunk + 1 < chunks else [])
        interleave(matrix, softmax(chunk))
    for step in gradients(chunks - 1):
        step()
    for store in stores:
        store.wait()


def attention(ratios, queries, grad_out, keys, values, near_other, far):
    rows, wide = keys.shape
    heads = wide // DH
    group = queries.shape[1] // wide
    shifts = len(far) // 2
    columns = 2 * rows + SLOTS * shifts
    width = JOIN * rows
    out_shape = [jax.ShapeDtypeStruct(queries.shape, jnp.bfloat16)]
    for index, size in enumerate([rows] * 2 + [SLOTS // 2] * (2 * shifts)):
        out_shape.append(jax.ShapeDtypeStruct((size, 2 * wide), jnp.bfloat16 if index % 2 else jnp.float32))
    hbm = pl.BlockSpec(memory_space=pltpu.HBM)
    vmem = pl.BlockSpec(memory_space=pltpu.VMEM)
    buffers = [
        pltpu.VMEM((columns, width), jnp.float32),
        pltpu.VMEM((columns, width), jnp.float32),
        pltpu.VMEM((columns, width), jnp.bfloat16),
        pltpu.VMEM((columns, width), jnp.bfloat16),
    ]
    products = queries.shape[1] * rows * columns
    fixed = [pltpu.with_memory_space_constraint(x, pltpu.HBM) for x in (queries, grad_out, keys, values)]
    return pl.pallas_call(
        functools.partial(attention_kernel, shifts, heads, group),
        out_shape=out_shape,
        in_specs=[pl.BlockSpec(memory_space=pltpu.SMEM)] + [hbm] * 4 + [vmem] * (1 + 2 * shifts),
        out_specs=[hbm] + [vmem] * (2 + 2 * shifts),
        scratch_shapes=[
            pltpu.VMEM(queries.shape, jnp.bfloat16),
            pltpu.VMEM(queries.shape, jnp.bfloat16),
            pltpu.VMEM(queries.shape, jnp.bfloat16),
            pltpu.VMEM(keys.shape, jnp.bfloat16),
            pltpu.VMEM(keys.shape, jnp.bfloat16),
            pltpu.VMEM((heads, columns, 2 * DH), jnp.bfloat16),
            pltpu.VMEM((heads, columns, DH), jnp.bfloat16),
            pltpu.VMEM((heads, DH, columns), jnp.bfloat16),
            pltpu.VMEM((columns, DH), jnp.float32),
            pltpu.VMEM((columns, DH), jnp.float32),
        ]
        + buffers * 2
        + [
            pltpu.SemaphoreType.DMA((2,)),
            pltpu.SemaphoreType.DMA((2 * heads,)),
            pltpu.SemaphoreType.DMA((heads,)),
        ],
        compiler_params=pltpu.CompilerParams(vmem_limit_bytes=48 * 1024 * 1024),
        cost_estimate=pl.CostEstimate(
            flops=10 * products, bytes_accessed=6 * queries.size, transcendentals=products // DH
        ),
    )(ratios, *fixed, near_other, *far)


def local(queries, keys, values, beacon_keys, beacon_values, grad_out, ratios):
    spans = ratios.shape[0]
    wide = keys.shape[1]
    swap = [(0, 1), (1, 0)]
    shifts = range(1, spans)

    def up(k):
        return [(i, (i + k) % spans) for i in range(spans)]

    beacons = jnp.concatenate([beacon_keys, beacon_values], axis=1)
    near_other = lax.ppermute(jnp.concatenate([keys, values], axis=1), "sub", swap)
    order = sorted(shifts, key=lambda k: abs(2 * k - spans))
    own = {k: lax.ppermute(beacons, "ctx", up(k)) for k in reversed(order)}
    other = {k: lax.ppermute(own[k], "sub", swap) for k in order}
    far = [x[k] for k in shifts for x in (own, other)]
    grad_queries, near_own, near_sent, *grads = attention(
        ratios, queries, grad_out, keys, values, near_other, far
    )
    sums = []
    for k in order:
        own, sent = grads[2 * k - 2 : 2 * k]
        pair = own + lax.ppermute(sent, "sub", swap).astype(jnp.float32)
        sums.append(lax.ppermute(pair.astype(jnp.bfloat16), "ctx", up(-k)).astype(jnp.float32))
    near = near_own + lax.ppermute(near_sent, "sub", swap).astype(jnp.float32)
    beacon = functools.reduce(jnp.add, sums)
    outs = [x.astype(jnp.bfloat16) for y in (near, beacon) for x in (y[:, :wide], y[:, wide:])]
    return (grad_queries, *outs)


def solution(mesh):
    rows = P(("grp", "ctx", "sub"), "tp")
    return jax.shard_map(
        local,
        mesh=mesh,
        in_specs=(rows,) * 6 + (P("grp"),),
        out_specs=(rows,) * 5,
        check_vma=False,
    )
```

```python
import functools
import math

import jax
import jax.numpy as jnp
from jax import lax
from jax.experimental import pallas as pl
from jax.experimental.pallas import tpu as pltpu
from jax.sharding import PartitionSpec as P

DH = 128
SPAN = 256
SLOTS = SPAN // 2
NT = (((1,), (1,)), ((), ()))
HIDDEN = -3e38
JOIN = 4
BLOCK = 16


def interleave(first, second):
    few, many = sorted((first, second), key=len)
    done = 0
    for index, step in enumerate(few):
        step()
        upto = len(many) * (index + 1) // len(few)
        for other in many[done:upto]:
            other()
        done = upto
    for other in many[done:]:
        other()


def attention_kernel(shifts, heads, group, base, extra, ratios, q_hbm, g_hbm, near_own, near_other, *refs):
    far, refs = refs[: 2 * shifts], refs[2 * shifts + extra :]
    dq_hbm, own_outs, sent_out, refs = refs[0], refs[1 : 2 + shifts], refs[2 + shifts], refs[3 + shifts :]
    (q_buf, g_buf, dq_buf, key_buf, value_buf, turned_buf, dk_buf, dv_buf) = refs[:8]
    sets, (in_sem, out_sem) = (refs[8:12], refs[12:16]), refs[16:]
    rows = q_buf.shape[0]
    wide = heads * DH
    half = SLOTS // 2
    columns = key_buf.shape[1]
    width = JOIN * rows
    per_head = group // JOIN
    chunks = heads * per_head
    scale = DH ** (-0.5)
    log_scale = scale * math.log2(math.e)
    here = lax.axis_index("ctx")
    sub = lax.axis_index("sub")

    loads, stores = [], []
    for head in range(heads):
        cols = slice(head * group * DH, (head + 1) * group * DH)
        far_cols = slice((base + head) * group * DH, (base + head + 1) * group * DH)
        loads.append(
            [
                pltpu.make_async_copy(q_hbm.at[:, far_cols], q_buf.at[:, cols], in_sem.at[2 * head]),
                pltpu.make_async_copy(g_hbm.at[:, far_cols], g_buf.at[:, cols], in_sem.at[2 * head + 1]),
            ]
        )
        stores.append(pltpu.make_async_copy(dq_buf.at[:, cols], dq_hbm.at[:, far_cols], out_sem.at[head]))
    for load in sum(loads, []):
        load.start()

    def place(at, keys, values, seen):
        mask = jnp.where(seen, 0.0, HIDDEN).astype(jnp.bfloat16)
        size = mask.shape[0]
        for head in range(heads):
            cols = slice(head * DH, (head + 1) * DH)
            key_buf[head, at : at + size, :DH] = keys[:, cols]
            key_buf[head, at : at + size, DH:] = mask
            value_buf[head, at : at + size, :] = values[:, cols]

    key_at = lax.broadcasted_iota(jnp.int32, (rows, DH), 0)
    token_at = lax.broadcasted_iota(jnp.int32, (rows, DH), 1)
    slot_at = lax.broadcasted_iota(jnp.int32, (half, DH), 0)
    place(rows, near_other.at[:, :wide], near_other.at[:, wide:], key_at < sub * rows)
    at = 2 * rows
    for shift in range(shifts):
        owner = jnp.maximum(here - 1 - shift, 0)
        live = jnp.where(here > shift, SPAN // ratios[owner], 0)
        for side, first in enumerate((sub * half, (1 - sub) * half)):
            source = far[2 * shift + side]
            place(at, source.at[:, :wide], source.at[:, wide:], slot_at < live - first)
            at += half
    place(0, near_own.at[:, :wide], near_own.at[:, wide:], key_at <= token_at)
    one_hot = jnp.where(key_at == token_at, 1.0, 0.0).astype(jnp.bfloat16)

    def joined(buf, chunk, start, count):
        first = (chunk * JOIN + start) * DH
        return jnp.concatenate([buf[:, first + i * DH : first + (i + 1) * DH] for i in range(count)], axis=0)

    def products(chunk):
        score_ref, signal_ref, _, _ = sets[chunk % 2]
        head = chunk // per_head

        def score(start):
            cols = slice(start * rows, (start + 2) * rows)
            queries = jnp.concatenate(
                [joined(q_buf, chunk, start, 2), jnp.concatenate([one_hot] * 2, axis=0)], axis=1
            )
            score_ref[:, cols] = lax.dot_general(key_buf[head], queries, NT, preferred_element_type=jnp.float32)

        def signal(start):
            cols = slice(start * rows, (start + 2) * rows)
            signal_ref[:, cols] = lax.dot_general(
                value_buf[head], joined(g_buf, chunk, start, 2), NT, preferred_element_type=jnp.float32
            )

        def begin():
            if chunk % per_head == 0:
                for load in loads[head]:
                    load.wait()
                turned_buf[head] = key_buf[head, :, :DH].T

        begin()
        return [functools.partial(f, start) for f in (score, signal) for start in range(0, JOIN, 2)]

    def softmax(chunk):
        score_ref, signal_ref, weight_ref, slope_ref = sets[chunk % 2]
        state = {}

        def spread(x):
            return jnp.broadcast_to(x, (8, width))

        def begin_top():
            state["top"] = jnp.full((8, width), HIDDEN, jnp.float32)

        def top(at):
            for i in range(at, at + BLOCK, 8):
                state["top"] = jnp.maximum(state["top"], score_ref[i : i + 8, :])

        def end_top():
            state["top"] = spread(jnp.max(state["top"], axis=0, keepdims=True))
            state["total"] = jnp.zeros((8, width), jnp.float32)

        def grow(at):
            for i in range(at, at + BLOCK, 8):
                grown = jnp.exp2((score_ref[i : i + 8, :] - state["top"]) * log_scale)
                score_ref[i : i + 8, :] = grown
                state["total"] = state["total"] + grown

        def end_grow():
            state["share"] = spread(1.0 / jnp.sum(state["total"], axis=0, keepdims=True))
            state["delta"] = jnp.zeros((8, width), jnp.float32)

        def weigh(at):
            probs = [score_ref[i : i + 8, :] * state["share"] for i in range(at, at + BLOCK, 8)]
            weights = jnp.concatenate(probs, axis=0).astype(jnp.bfloat16)
            weight_ref[at : at + BLOCK, :] = weights
            terms = weights.astype(jnp.float32) * signal_ref[at : at + BLOCK, :]
            for i in range(0, BLOCK, 8):
                state["delta"] = state["delta"] + terms[i : i + 8]

        def end_weigh():
            state["delta"] = spread(jnp.sum(state["delta"], axis=0, keepdims=True))

        def slope(at):
            slopes = []
            for i in range(at, at + BLOCK, 8):
                probs = score_ref[i : i + 8, :] * state["share"]
                slopes.append(probs * (signal_ref[i : i + 8, :] - state["delta"]))
            slope_ref[at : at + BLOCK, :] = jnp.concatenate(slopes, axis=0).astype(jnp.bfloat16)

        steps = [begin_top]
        for work, end in ((top, end_top), (grow, end_grow), (weigh, end_weigh), (slope, None)):
            steps += [functools.partial(work, at) for at in range(0, columns, BLOCK)]
            steps += [end] if end else []
        return steps

    def gradients(chunk):
        _, _, weight_ref, slope_ref = sets[chunk % 2]
        head = chunk // per_head
        last = chunk % per_head == per_head - 1

        def piece(buf, start, left_ref):
            cols = slice(start * rows, (start + 2) * rows)
            return jnp.dot(left_ref[:, cols], joined(buf, chunk, start, 2), preferred_element_type=jnp.float32)

        def collect(total_ref, buf, left_ref, side, factor):
            total = piece(buf, 0, left_ref)
            for start in range(2, JOIN, 2):
                total = total + piece(buf, start, left_ref)
            if chunk % per_head:
                total = total + total_ref[...]
            if not last:
                total_ref[...] = total
                return
            cols = slice(side * wide + head * DH, side * wide + (head + 1) * DH)
            at, sent = 0, 0
            for out in own_outs:
                size = out.shape[0]
                out[:, cols] = total[at : at + size] * factor
                at += size
                sent_out[sent : sent + size, cols] = (total[at : at + size] * factor).astype(sent_out.dtype)
                at += size
                sent += size

        def turn(start):
            cols = slice(start * rows, (start + 2) * rows)
            turned = jnp.dot(turned_buf[head], slope_ref[:, cols], preferred_element_type=jnp.float32)
            for i in range(2):
                first = (chunk * JOIN + start + i) * DH
                dq = turned[:, i * rows : (i + 1) * rows].T * scale
                dq_buf[:, first : first + DH] = dq.astype(jnp.bfloat16)

        steps = [
            functools.partial(collect, dk_buf, q_buf, slope_ref, 0, scale),
            functools.partial(collect, dv_buf, g_buf, weight_ref, 1, 1.0),
        ]
        steps += [functools.partial(turn, start) for start in range(0, JOIN, 2)]
        if last:
            steps.append(stores[head].start)
        return steps

    for step in products(0):
        step()
    for chunk in range(chunks):
        matrix = gradients(chunk - 1) if chunk > 0 else []
        matrix = matrix + (products(chunk + 1) if chunk + 1 < chunks else [])
        interleave(matrix, softmax(chunk))
    for step in gradients(chunks - 1):
        step()
    for store in stores:
        store.wait()


def attention(ratios, queries, grad_out, near_own, near_other, far, base, group, before):
    rows, wide = near_own.shape[0], near_own.shape[1] // 2
    heads = wide // DH
    shifts = len(far) // 2
    half = SLOTS // 2
    columns = 2 * rows + SLOTS * shifts
    width = JOIN * rows
    out_shape = [jax.ShapeDtypeStruct(queries.shape, jnp.bfloat16)]
    out_shape += [jax.ShapeDtypeStruct((size, 2 * wide), jnp.float32) for size in [rows] + [half] * shifts]
    out_shape.append(jax.ShapeDtypeStruct((rows + half * shifts, 2 * wide), jnp.bfloat16))
    hbm = pl.BlockSpec(memory_space=pltpu.HBM)
    vmem = pl.BlockSpec(memory_space=pltpu.VMEM)
    buffers = [
        pltpu.VMEM((columns, width), jnp.float32),
        pltpu.VMEM((columns, width), jnp.float32),
        pltpu.VMEM((columns, width), jnp.bfloat16),
        pltpu.VMEM((columns, width), jnp.bfloat16),
    ]
    part = (rows, heads * group * DH)
    products = heads * group * DH * rows * columns
    fixed = [pltpu.with_memory_space_constraint(x, pltpu.HBM) for x in (queries, grad_out)]
    extra = [] if before is None else [pltpu.with_memory_space_constraint(before, pltpu.HBM)]
    operands = [ratios, *fixed, near_own, near_other, *far, *extra]
    return pl.pallas_call(
        functools.partial(attention_kernel, shifts, heads, group, base, len(extra)),
        out_shape=out_shape,
        in_specs=[pl.BlockSpec(memory_space=pltpu.SMEM)]
        + [hbm] * 2
        + [vmem] * (2 + 2 * shifts)
        + [hbm] * len(extra),
        out_specs=[hbm] + [vmem] * (2 + shifts),
        input_output_aliases={len(operands) - 1: 0} if extra else {},
        scratch_shapes=[
            pltpu.VMEM(part, jnp.bfloat16),
            pltpu.VMEM(part, jnp.bfloat16),
            pltpu.VMEM(part, jnp.bfloat16),
            pltpu.VMEM((heads, columns, 2 * DH), jnp.bfloat16),
            pltpu.VMEM((heads, columns, DH), jnp.bfloat16),
            pltpu.VMEM((heads, DH, columns), jnp.bfloat16),
            pltpu.VMEM((columns, DH), jnp.float32),
            pltpu.VMEM((columns, DH), jnp.float32),
        ]
        + buffers * 2
        + [pltpu.SemaphoreType.DMA((2 * heads,)), pltpu.SemaphoreType.DMA((heads,))],
        compiler_params=pltpu.CompilerParams(vmem_limit_bytes=40 * 1024 * 1024),
        cost_estimate=pl.CostEstimate(
            flops=10 * products, bytes_accessed=6 * queries.size, transcendentals=products // DH
        ),
    )(*operands)


def pack_kernel(parts, near_key, near_value, far_key, far_value, *refs):
    outs, buffers, sem = refs[: 2 * parts], refs[2 * parts : -1], refs[-1]
    sources = (far_key, far_value, near_key, near_value)
    loads = [pltpu.make_async_copy(*pair, sem.at[i]) for i, pair in enumerate(zip(sources, buffers))]
    for load in loads:
        load.start()
    for index in range(2):
        loads[2 * index].wait()
        loads[2 * index + 1].wait()
        keys, values = buffers[2 * index], buffers[2 * index + 1]
        size = keys.shape[1] // parts
        for part in range(parts):
            out = outs[index * parts + part]
            out[:, :size] = keys[:, part * size : (part + 1) * size]
            out[:, size:] = values[:, part * size : (part + 1) * size]


def pack(parts, keys, values, beacon_keys, beacon_values):
    shapes = [(x.shape[0], 2 * x.shape[1] // parts) for x in (beacon_keys, keys) for _ in range(parts)]
    inputs = [pltpu.with_memory_space_constraint(x, pltpu.HBM) for x in (keys, values, beacon_keys, beacon_values)]
    outs = pl.pallas_call(
        functools.partial(pack_kernel, parts),
        out_shape=[jax.ShapeDtypeStruct(shape, jnp.bfloat16) for shape in shapes],
        in_specs=[pl.BlockSpec(memory_space=pltpu.HBM)] * 4,
        scratch_shapes=[pltpu.VMEM(x.shape, jnp.bfloat16) for x in (beacon_keys, beacon_values, keys, values)]
        + [pltpu.SemaphoreType.DMA((4,))],
    )(*inputs)
    return outs[parts:], outs[:parts]


def total_kernel(counts, *refs):
    terms, (key_out, value_out) = refs[:-2], refs[-2:]
    size = terms[0].shape[1] // 2
    at = 0
    for part, count in enumerate(counts):
        total = functools.reduce(jnp.add, [x[...].astype(jnp.float32) for x in terms[at : at + count]])
        at += count
        cols = slice(part * size, (part + 1) * size)
        key_out[:, cols] = total[:, :size].astype(key_out.dtype)
        value_out[:, cols] = total[:, size:].astype(value_out.dtype)


def total(parts):
    rows, wide = parts[0][0].shape
    shape = jax.ShapeDtypeStruct((rows, wide // 2 * len(parts)), jnp.bfloat16)
    return pl.pallas_call(
        functools.partial(total_kernel, [len(x) for x in parts]),
        out_shape=[shape, shape],
    )(*[x for terms in parts for x in terms])


def local(queries, keys, values, beacon_keys, beacon_values, grad_out, ratios):
    spans = ratios.shape[0]
    rows, wide = keys.shape
    heads = wide // DH
    group = queries.shape[1] // wide
    half = SLOTS // 2
    parts = 2 if heads % 2 == 0 else 1
    swap = [(0, 1), (1, 0)]
    shifts = range(1, spans)
    order = sorted(shifts, key=lambda k: abs(2 * k - spans))

    def up(k):
        return [(i, (i + k) % spans) for i in range(spans)]

    near_own, beacons = pack(parts, keys, values, beacon_keys, beacon_values)
    near_other = [lax.ppermute(x, "sub", swap) for x in near_own]
    far_own = [{k: lax.ppermute(x, "ctx", up(k)) for k in reversed(order)} for x in beacons]

    grad_queries, near, beacon = None, [], []
    for part in range(parts):
        far_other = {k: lax.ppermute(far_own[part][k], "sub", swap) for k in order}
        far = [x[k] for k in shifts for x in (far_own[part], far_other)]
        grad_queries, near_grad, *own, sent = attention(
            ratios, queries, grad_out, near_own[part], near_other[part], far, part * heads // parts, group, grad_queries
        )
        sent, far_own[part + 1 :], beacon = lax.optimization_barrier((sent, far_own[part + 1 :], beacon))
        got = lax.ppermute(sent, "sub", swap)
        pairs = {}
        for k in order:
            at = rows + half * (k - 1)
            pairs[k] = (own[k - 1] + got[at : at + half].astype(jnp.float32)).astype(jnp.bfloat16)
        if part + 1 < parts:
            pairs, far_own[part + 1] = lax.optimization_barrier((pairs, far_own[part + 1]))
        beacon.append([lax.ppermute(pairs[k], "ctx", up(-k)) for k in order])
        near.append([near_grad, got[:rows]])
    return (grad_queries, *total(near), *total(beacon))


def solution(mesh):
    rows = P(("grp", "ctx", "sub"), "tp")
    return jax.shard_map(
        local,
        mesh=mesh,
        in_specs=(rows,) * 6 + (P("grp"),),
        out_specs=(rows,) * 5,
        check_vma=False,
    )
```

```python
import functools
import math

import jax
import jax.numpy as jnp
from jax import lax
from jax.experimental import pallas as pl
from jax.experimental.pallas import tpu as pltpu
from jax.sharding import PartitionSpec as P

DH = 128
SPAN = 256
SLOTS = SPAN // 2
HALF = SLOTS // 2
NT = (((1,), (1,)), ((), ()))
HIDDEN = -3e38
JOIN = 4
BLOCK = 16
SCALE = DH ** (-0.5)
LOG_SCALE = SCALE * math.log2(math.e)


def interleave(first, second):
    few, many = sorted((first, second), key=len)
    done = 0
    for index, step in enumerate(few):
        step()
        upto = len(many) * (index + 1) // len(few)
        for other in many[done:upto]:
            other()
        done = upto
    for other in many[done:]:
        other()


def pipeline(chunks, products, softmax, gradients):
    for step in products(0):
        step()
    for chunk in range(chunks):
        matrix = gradients(chunk - 1) if chunk > 0 else []
        matrix = matrix + (products(chunk + 1) if chunk + 1 < chunks else [])
        interleave(matrix, softmax(chunk))
    for step in gradients(chunks - 1):
        step()


def head_cols(head):
    return slice(head * DH, (head + 1) * DH)


def joined(buf, chunk, start, count):
    first = chunk * JOIN + start
    return jnp.concatenate([buf[:, head_cols(first + i)] for i in range(count)], axis=0)


def pair_products(key_buf, value_buf, q_buf, g_buf, chunk, head, score_ref, signal_ref):
    rows = q_buf.shape[0]
    at = [lax.broadcasted_iota(jnp.int32, (rows, DH), axis) for axis in range(2)]
    one_hot = jnp.where(at[0] == at[1], 1.0, 0.0).astype(jnp.bfloat16)
    one_hot = jnp.concatenate([one_hot] * 2, axis=0)

    def score(start):
        queries = jnp.concatenate([joined(q_buf, chunk, start, 2), one_hot], axis=1)
        cols = slice(start * rows, (start + 2) * rows)
        score_ref[:, cols] = lax.dot_general(key_buf[head], queries, NT, preferred_element_type=jnp.float32)

    def signal(start):
        cols = slice(start * rows, (start + 2) * rows)
        signal_ref[:, cols] = lax.dot_general(
            value_buf[head], joined(g_buf, chunk, start, 2), NT, preferred_element_type=jnp.float32
        )

    return [functools.partial(f, start) for f in (score, signal) for start in range(0, JOIN, 2)]


def mask_of(seen):
    return jnp.where(seen, 0.0, HIDDEN).astype(jnp.bfloat16)


def place(key_buf, value_buf, at, keys, values, mask):
    size = mask.shape[0]
    for head in range(key_buf.shape[0]):
        key_buf[head, at : at + size, :DH] = keys[:, head_cols(head)]
        key_buf[head, at : at + size, DH:] = mask
        value_buf[head, at : at + size, :] = values[:, head_cols(head)]


def spread(x):
    return jnp.broadcast_to(x, (8, x.shape[1]))


def near_kernel(
    shifts, group, ratios, q_hbm, g_hbm, key_hbm, value_hbm, other_key, other_value, q_buf, g_buf, mask_out, grown_out,
    signal_out, top_out, total_out, own_key, own_value, key_buf, value_buf, sem,
):
    rows = q_buf.shape[0]
    heads = key_buf.shape[0]
    per_head = group // JOIN
    chunks = heads * per_head
    width = JOIN * rows
    sub = lax.axis_index("sub")
    pairs = [(key_hbm, own_key), (value_hbm, own_value)]
    for head in range(heads):
        cols = slice(head * group * DH, (head + 1) * group * DH)
        pairs += [(q_hbm.at[:, cols], q_buf.at[:, cols]), (g_hbm.at[:, cols], g_buf.at[:, cols])]
    loads = [pltpu.make_async_copy(*pair, sem.at[i]) for i, pair in enumerate(pairs)]
    for load in loads:
        load.start()
    key_at = lax.broadcasted_iota(jnp.int32, (rows, DH), 0)
    token_at = lax.broadcasted_iota(jnp.int32, (rows, DH), 1)
    place(key_buf, value_buf, rows, other_key, other_value, mask_of(key_at < sub * rows))
    here = lax.axis_index("ctx")
    slot_at = lax.broadcasted_iota(jnp.int32, (HALF, DH), 0)
    for shift in range(shifts):
        owner = jnp.maximum(here - 1 - shift, 0)
        live = jnp.where(here > shift, SPAN // ratios[owner], 0)
        for side, first in enumerate((sub * HALF, (1 - sub) * HALF)):
            at = (2 * shift + side) * HALF
            mask_out[at : at + HALF, :] = mask_of(slot_at < live - first)
    loads[0].wait()
    loads[1].wait()
    place(key_buf, value_buf, 0, own_key, own_value, mask_of(key_at <= token_at))

    def products(chunk):
        head = chunk // per_head
        if chunk % per_head == 0:
            loads[2 + 2 * head].wait()
            loads[3 + 2 * head].wait()
        return pair_products(
            key_buf, value_buf, q_buf, g_buf, chunk, head, grown_out.at[chunk], signal_out.at[chunk]
        )

    def softmax(chunk):
        score_ref = grown_out.at[chunk]
        state = {"top": jnp.full((8, width), HIDDEN, jnp.float32)}

        def top(at):
            for i in range(at, at + BLOCK, 8):
                state["top"] = jnp.maximum(state["top"], score_ref[i : i + 8, :])

        def end_top():
            state["top"] = spread(jnp.max(state["top"], axis=0, keepdims=True))
            top_out[chunk] = state["top"]
            state["total"] = jnp.zeros((8, width), jnp.float32)

        def grow(at):
            for i in range(at, at + BLOCK, 8):
                grown = jnp.exp2((score_ref[i : i + 8, :] - state["top"]) * LOG_SCALE)
                score_ref[i : i + 8, :] = grown
                state["total"] = state["total"] + grown

        def end_grow():
            total_out[chunk] = spread(jnp.sum(state["total"], axis=0, keepdims=True))

        blocks = range(0, 2 * rows, BLOCK)
        return [functools.partial(top, at) for at in blocks] + [end_top] + [functools.partial(grow, at) for at in blocks] + [end_grow]

    pipeline(chunks, products, softmax, lambda chunk: [])


def far_kernel(shifts, group, q_buf, g_buf, far_mask, near_grown, near_signal, near_top, near_total, *refs):
    far, refs = refs[: 2 * shifts], refs[2 * shifts :]
    near_weights, slopes_out, own_outs, sent_out = refs[0], refs[1], refs[2 : 2 + shifts], refs[2 + shifts]
    refs = refs[3 + shifts :]
    (key_buf, value_buf, dk_buf, dv_buf), sets = refs[:4], (refs[4:7], refs[7:10])
    rows = q_buf.shape[0]
    heads, columns = key_buf.shape[:2]
    wide = heads * DH
    per_head = group // JOIN
    chunks = heads * per_head
    width = JOIN * rows
    near = 2 * rows
    for index, source in enumerate(far):
        at = index * HALF
        place(key_buf, value_buf, at, source.at[:, :wide], source.at[:, wide:], far_mask[at : at + HALF, :])

    def products(chunk):
        score_ref, signal_ref, _ = sets[chunk % 2]
        return pair_products(key_buf, value_buf, q_buf, g_buf, chunk, chunk // per_head, score_ref, signal_ref)

    def softmax(chunk):
        score_ref, signal_ref, weight_ref = sets[chunk % 2]
        slope_ref = slopes_out.at[chunk]
        state = {"top": near_top[chunk]}

        def top(at):
            for i in range(at, at + BLOCK, 8):
                state["top"] = jnp.maximum(state["top"], score_ref[i : i + 8, :])

        def end_top():
            state["top"] = spread(jnp.max(state["top"], axis=0, keepdims=True))
            state["total"] = jnp.zeros((8, width), jnp.float32)

        def grow(at):
            for i in range(at, at + BLOCK, 8):
                grown = jnp.exp2((score_ref[i : i + 8, :] - state["top"]) * LOG_SCALE)
                score_ref[i : i + 8, :] = grown
                state["total"] = state["total"] + grown

        def end_grow():
            shrink = jnp.exp2((near_top[chunk] - state["top"]) * LOG_SCALE)
            total = near_total[chunk] * shrink + spread(jnp.sum(state["total"], axis=0, keepdims=True))
            state["far"] = 1.0 / total
            state["near"] = shrink * state["far"]
            state["delta"] = jnp.zeros((8, width), jnp.float32)

        def weigh(grown, signal, out, share, at):
            probs = [grown[i : i + 8, :] * state[share] for i in range(at, at + BLOCK, 8)]
            weights = jnp.concatenate(probs, axis=0).astype(jnp.bfloat16)
            out[at : at + BLOCK, :] = weights
            terms = weights.astype(jnp.float32) * signal[at : at + BLOCK, :]
            for i in range(0, BLOCK, 8):
                state["delta"] = state["delta"] + terms[i : i + 8]

        def end_weigh():
            state["delta"] = spread(jnp.sum(state["delta"], axis=0, keepdims=True))

        def slope(grown, signal, share, offset, at):
            slopes = []
            for i in range(at, at + BLOCK, 8):
                slopes.append(grown[i : i + 8, :] * state[share] * (signal[i : i + 8, :] - state["delta"]))
            slope_ref[offset + at : offset + at + BLOCK, :] = jnp.concatenate(slopes, axis=0).astype(jnp.bfloat16)

        far_blocks, near_blocks = range(0, columns, BLOCK), range(0, near, BLOCK)
        grown, signal = near_grown.at[chunk], near_signal.at[chunk]
        steps = [functools.partial(top, at) for at in far_blocks] + [end_top]
        steps += [functools.partial(grow, at) for at in far_blocks] + [end_grow]
        steps += [functools.partial(weigh, score_ref, signal_ref, weight_ref, "far", at) for at in far_blocks]
        steps += [functools.partial(weigh, grown, signal, near_weights.at[chunk], "near", at) for at in near_blocks]
        steps += [end_weigh]
        steps += [functools.partial(slope, score_ref, signal_ref, "far", near, at) for at in far_blocks]
        steps += [functools.partial(slope, grown, signal, "near", 0, at) for at in near_blocks]
        return steps

    def gradients(chunk):
        weight_ref = sets[chunk % 2][2]
        head = chunk // per_head
        last = chunk % per_head == per_head - 1

        def collect(total_ref, buf, left, side, factor):
            total = None
            for start in range(0, JOIN, 2):
                cols = slice(start * rows, (start + 2) * rows)
                part = jnp.dot(left(cols), joined(buf, chunk, start, 2), preferred_element_type=jnp.float32)
                total = part if total is None else total + part
            if chunk % per_head:
                total = total + total_ref[...]
            if not last:
                total_ref[...] = total
                return
            cols = slice(side * wide + head * DH, side * wide + (head + 1) * DH)
            for shift, out in enumerate(own_outs):
                at = shift * SLOTS
                out[:, cols] = total[at : at + HALF] * factor
                sent = total[at + HALF : at + SLOTS] * factor
                sent_out[shift * HALF : (shift + 1) * HALF, cols] = sent.astype(sent_out.dtype)

        return [
            functools.partial(collect, dk_buf, q_buf, lambda cols: slopes_out[chunk, near:, cols], 0, SCALE),
            functools.partial(collect, dv_buf, g_buf, lambda cols: weight_ref[:, cols], 1, 1.0),
        ]

    pipeline(chunks, products, softmax, gradients)


def finish_kernel(shifts, group, q_buf, g_buf, slopes, weights, key_hbm, other_key, *refs):
    far, refs = refs[: 2 * shifts], refs[2 * shifts :]
    dq_hbm, own_out, sent_out, own_key, key_buf, turned_buf, dq_buf, in_sem, out_sem = refs
    rows = q_buf.shape[0]
    heads = key_buf.shape[0]
    wide = heads * DH
    near = 2 * rows
    per_head = group // JOIN
    load = pltpu.make_async_copy(key_hbm, own_key, in_sem)
    load.start()
    at = rows
    for piece in (other_key, *far):
        size = piece.shape[0]
        for head in range(heads):
            key_buf[head, at : at + size, :] = piece[:, head_cols(head)]
        at += size
    load.wait()
    stores = []
    for head in range(heads):
        key_buf[head, :rows, :] = own_key[:, head_cols(head)]
        turned_buf[head] = key_buf[head].T
        chunks = range(head * per_head, (head + 1) * per_head)
        for side, left, right, factor in ((0, slopes, q_buf, SCALE), (1, weights, g_buf, 1.0)):
            total = None
            for chunk in chunks:
                for start in range(0, JOIN, 2):
                    cols = slice(start * rows, (start + 2) * rows)
                    part = jnp.dot(
                        left[chunk, :near, cols], joined(right, chunk, start, 2), preferred_element_type=jnp.float32
                    )
                    total = part if total is None else total + part
            cols = slice(side * wide + head * DH, side * wide + (head + 1) * DH)
            own_out[:, cols] = total[:rows] * factor
            sent_out[:, cols] = (total[rows:] * factor).astype(sent_out.dtype)
        for chunk in chunks:
            for start in range(0, JOIN, 2):
                cols = slice(start * rows, (start + 2) * rows)
                turned = jnp.dot(turned_buf[head], slopes[chunk, :, cols], preferred_element_type=jnp.float32)
                for i in range(2):
                    dq = turned[:, i * rows : (i + 1) * rows].T * SCALE
                    dq_buf[:, head_cols(chunk * JOIN + start + i)] = dq.astype(jnp.bfloat16)
        cols = slice(head * group * DH, (head + 1) * group * DH)
        stores.append(pltpu.make_async_copy(dq_buf.at[:, cols], dq_hbm.at[:, cols], out_sem.at[head]))
        stores[-1].start()
    for store in stores:
        store.wait()


def in_hbm(x):
    return pltpu.with_memory_space_constraint(x, pltpu.HBM)


def call(kernel, operands, spaces, outs, out_spaces, scratch, limit, products):
    return pl.pallas_call(
        kernel,
        out_shape=[jax.ShapeDtypeStruct(*x) for x in outs],
        in_specs=[pl.BlockSpec(memory_space=x) for x in spaces],
        out_specs=[pl.BlockSpec(memory_space=x) for x in out_spaces],
        scratch_shapes=scratch,
        compiler_params=pltpu.CompilerParams(vmem_limit_bytes=limit * 1024 * 1024),
        cost_estimate=pl.CostEstimate(flops=products, bytes_accessed=products // 256, transcendentals=products // 512),
    )(*operands)


def local(queries, keys, values, beacon_keys, beacon_values, grad_out, ratios):
    bf16, f32 = jnp.bfloat16, jnp.float32
    hbm, vmem = pltpu.HBM, pltpu.VMEM
    spans = ratios.shape[0]
    rows, wide = keys.shape
    heads = wide // DH
    group = queries.shape[1] // wide
    chunks = heads * group // JOIN
    width = JOIN * rows
    shift_count = spans - 1
    near, columns = 2 * rows, SLOTS * shift_count
    swap = [(0, 1), (1, 0)]
    shifts = range(1, spans)
    order = sorted(shifts, key=lambda k: abs(2 * k - spans))

    def up(k):
        return [(i, (i + k) % spans) for i in range(spans)]

    side_by_side = lax.broadcasted_iota(jnp.int32, (beacon_keys.shape[0], 2 * wide), 1) < wide
    beacons = jnp.where(
        side_by_side, jnp.pad(beacon_keys, ((0, 0), (0, wide))), jnp.pad(beacon_values, ((0, 0), (wide, 0)))
    )
    other_key, other_value = (lax.ppermute(x, "sub", swap) for x in (keys, values))
    own = {k: lax.ppermute(beacons, "ctx", up(k)) for k in reversed(order)}

    product = queries.shape[1] * rows * 2
    near_shape = ((chunks, near, width), f32)
    stat_shape = ((chunks, 8, width), f32)
    q_in, g_in, *stats = call(
        functools.partial(near_kernel, shift_count, group),
        [ratios, in_hbm(queries), in_hbm(grad_out), in_hbm(keys), in_hbm(values), other_key, other_value],
        [pltpu.SMEM] + [hbm] * 4 + [vmem] * 2,
        [(queries.shape, bf16)] * 2 + [((columns, DH), bf16)] + [near_shape] * 2 + [stat_shape] * 2,
        [vmem] * 7,
        [vmem(keys.shape, bf16)] * 2
        + [vmem((heads, near, 2 * DH), bf16), vmem((heads, near, DH), bf16)]
        + [pltpu.SemaphoreType.DMA((2 + 2 * heads,))],
        8,
        2 * product * near,
    )
    own, stats = lax.optimization_barrier((own, stats))
    other = {k: lax.ppermute(own[k], "sub", swap) for k in order}
    far = [x[k] for k in shifts for x in (own, other)]
    sets = [vmem((columns, width), f32)] * 2 + [vmem((columns, width), bf16)]
    weights, slopes, *grads, sent = call(
        functools.partial(far_kernel, shift_count, group),
        [q_in, g_in, *stats, *far],
        [vmem] * (7 + len(far)),
        [((chunks, near, width), bf16), ((chunks, near + columns, width), bf16)]
        + [((HALF, 2 * wide), f32)] * shift_count
        + [((HALF * shift_count, 2 * wide), bf16)],
        [vmem] * (3 + shift_count),
        [vmem((heads, columns, 2 * DH), bf16), vmem((heads, columns, DH), bf16)]
        + [vmem((columns, DH), f32)] * 2
        + sets * 2,
        16,
        4 * product * columns,
    )
    got = lax.ppermute(sent, "sub", swap)
    pairs = {k: (grads[k - 1] + got[HALF * (k - 1) : HALF * k].astype(f32)).astype(bf16) for k in order}
    pairs, other_key = lax.optimization_barrier((pairs, other_key))
    sums = [lax.ppermute(pairs[k], "ctx", up(-k)) for k in order]
    grad_queries, near_grad, near_sent = call(
        functools.partial(finish_kernel, shift_count, group),
        [q_in, g_in, slopes, weights, in_hbm(keys), other_key, *far],
        [vmem] * 4 + [hbm] + [vmem] * (1 + len(far)),
        [(queries.shape, bf16), ((rows, 2 * wide), f32), ((rows, 2 * wide), bf16)],
        [hbm, vmem, vmem],
        [
            vmem(keys.shape, bf16),
            vmem((heads, near + columns, DH), bf16),
            vmem((heads, DH, near + columns), bf16),
            vmem(queries.shape, bf16),
            pltpu.SemaphoreType.DMA,
            pltpu.SemaphoreType.DMA((heads,)),
        ],
        12,
        2 * product * (near + columns),
    )
    sums, grad_queries = lax.optimization_barrier((sums, grad_queries))
    near_total = near_grad + lax.ppermute(near_sent, "sub", swap).astype(f32)
    beacon_total = functools.reduce(jnp.add, [x.astype(f32) for x in sums])
    outs = [x.astype(bf16) for y in (near_total, beacon_total) for x in (y[:, :wide], y[:, wide:])]
    return (grad_queries, *outs)


def solution(mesh):
    rows = P(("grp", "ctx", "sub"), "tp")
    return jax.shard_map(
        local,
        mesh=mesh,
        in_specs=(rows,) * 6 + (P("grp"),),
        out_specs=(rows,) * 5,
        check_vma=False,
    )
```

```python
import functools
import math

import jax
import jax.numpy as jnp
from jax import lax
from jax.experimental import pallas as pl
from jax.experimental.pallas import tpu as pltpu
from jax.sharding import PartitionSpec as P

DH = 128
SPAN = 256
SLOTS = SPAN // 2
HALF = SLOTS // 2
NT = (((1,), (1,)), ((), ()))
HIDDEN = -3e38
JOIN = 4
BLOCK = 16
SCALE = DH ** (-0.5)
LOG_SCALE = SCALE * math.log2(math.e)


def interleave(first, second):
    few, many = sorted((first, second), key=len)
    done = 0
    for index, step in enumerate(few):
        step()
        upto = len(many) * (index + 1) // len(few)
        for other in many[done:upto]:
            other()
        done = upto
    for other in many[done:]:
        other()


def pipeline(chunks, products, softmax, gradients):
    for step in products(0):
        step()
    for chunk in range(chunks):
        matrix = gradients(chunk - 1) if chunk > 0 else []
        matrix = matrix + (products(chunk + 1) if chunk + 1 < chunks else [])
        interleave(matrix, softmax(chunk))
    for step in gradients(chunks - 1):
        step()


def head_cols(head):
    return slice(head * DH, (head + 1) * DH)


def joined(buf, chunk, start, count):
    first = chunk * JOIN + start
    return jnp.concatenate([buf[:, head_cols(first + i)] for i in range(count)], axis=0)


def pair_products(key_buf, value_buf, q_buf, g_buf, chunk, head, score_ref, signal_ref):
    rows = q_buf.shape[0]
    at = [lax.broadcasted_iota(jnp.int32, (rows, DH), axis) for axis in range(2)]
    one_hot = jnp.where(at[0] == at[1], 1.0, 0.0).astype(jnp.bfloat16)
    one_hot = jnp.concatenate([one_hot] * 2, axis=0)

    def score(start):
        queries = jnp.concatenate([joined(q_buf, chunk, start, 2), one_hot], axis=1)
        cols = slice(start * rows, (start + 2) * rows)
        score_ref[:, cols] = lax.dot_general(key_buf[head], queries, NT, preferred_element_type=jnp.float32)

    def signal(start):
        cols = slice(start * rows, (start + 2) * rows)
        signal_ref[:, cols] = lax.dot_general(
            value_buf[head], joined(g_buf, chunk, start, 2), NT, preferred_element_type=jnp.float32
        )

    return [functools.partial(f, start) for f in (score, signal) for start in range(0, JOIN, 2)]


def mask_of(seen):
    return jnp.where(seen, 0.0, HIDDEN).astype(jnp.bfloat16)


def place(key_buf, value_buf, at, keys, values, mask):
    size = mask.shape[0]
    for head in range(key_buf.shape[0]):
        key_buf[head, at : at + size, :DH] = keys[:, head_cols(head)]
        key_buf[head, at : at + size, DH:] = mask
        value_buf[head, at : at + size, :] = values[:, head_cols(head)]


def spread(x):
    return jnp.broadcast_to(x, (8, x.shape[1]))


def exponentials(chunk, grown_out, top_out, total_out):
    score_ref = grown_out.at[chunk]
    columns, width = score_ref.shape
    state = {"top": jnp.full((8, width), HIDDEN, jnp.float32)}

    def top(at):
        for i in range(at, at + BLOCK, 8):
            state["top"] = jnp.maximum(state["top"], score_ref[i : i + 8, :])

    def end_top():
        state["top"] = spread(jnp.max(state["top"], axis=0, keepdims=True))
        top_out[chunk] = state["top"]
        state["total"] = jnp.zeros((8, width), jnp.float32)

    def grow(at):
        for i in range(at, at + BLOCK, 8):
            grown = jnp.exp2((score_ref[i : i + 8, :] - state["top"]) * LOG_SCALE)
            score_ref[i : i + 8, :] = grown
            state["total"] = state["total"] + grown

    def end_grow():
        total_out[chunk] = spread(jnp.sum(state["total"], axis=0, keepdims=True))

    blocks = range(0, columns, BLOCK)
    return [functools.partial(top, at) for at in blocks] + [end_top] + [functools.partial(grow, at) for at in blocks] + [end_grow]


def near_kernel(
    shifts, group, ratios, q_hbm, g_hbm, key_hbm, value_hbm, other_key, other_value, q_buf, g_buf, mask_out, grown_out,
    signal_out, top_out, total_out, own_key, own_value, key_buf, value_buf, sem,
):
    rows = q_buf.shape[0]
    heads = key_buf.shape[0]
    per_head = group // JOIN
    sub = lax.axis_index("sub")
    pairs = [(key_hbm, own_key), (value_hbm, own_value)]
    for head in range(heads):
        cols = slice(head * group * DH, (head + 1) * group * DH)
        pairs += [(q_hbm.at[:, cols], q_buf.at[:, cols]), (g_hbm.at[:, cols], g_buf.at[:, cols])]
    loads = [pltpu.make_async_copy(*pair, sem.at[i]) for i, pair in enumerate(pairs)]
    for load in loads:
        load.start()
    key_at = lax.broadcasted_iota(jnp.int32, (rows, DH), 0)
    token_at = lax.broadcasted_iota(jnp.int32, (rows, DH), 1)
    place(key_buf, value_buf, rows, other_key, other_value, mask_of(key_at < sub * rows))
    here = lax.axis_index("ctx")
    slot_at = lax.broadcasted_iota(jnp.int32, (HALF, DH), 0)
    for shift in range(shifts):
        owner = jnp.maximum(here - 1 - shift, 0)
        live = jnp.where(here > shift, SPAN // ratios[owner], 0)
        for side, first in enumerate((sub * HALF, (1 - sub) * HALF)):
            at = (2 * shift + side) * HALF
            mask_out[at : at + HALF, :] = mask_of(slot_at < live - first)
    loads[0].wait()
    loads[1].wait()
    place(key_buf, value_buf, 0, own_key, own_value, mask_of(key_at <= token_at))

    def products(chunk):
        head = chunk // per_head
        if chunk % per_head == 0:
            loads[2 + 2 * head].wait()
            loads[3 + 2 * head].wait()
        return pair_products(
            key_buf, value_buf, q_buf, g_buf, chunk, head, grown_out.at[chunk], signal_out.at[chunk]
        )

    pipeline(
        heads * per_head,
        products,
        lambda chunk: exponentials(chunk, grown_out, top_out, total_out),
        lambda chunk: [],
    )


def place_far(key_buf, value_buf, far, mask):
    wide = far[0].shape[1] // 2
    for index, source in enumerate(far):
        at = index * HALF
        place(key_buf, value_buf, at, source.at[:, :wide], source.at[:, wide:], mask[at : at + HALF, :])


def middle_kernel(group, q_buf, g_buf, far_mask, *refs):
    far, (grown_out, signal_out, top_out, total_out, key_buf, value_buf) = refs[:-6], refs[-6:]
    heads = key_buf.shape[0]
    per_head = group // JOIN
    place_far(key_buf, value_buf, far, far_mask)

    def products(chunk):
        return pair_products(
            key_buf, value_buf, q_buf, g_buf, chunk, chunk // per_head, grown_out.at[chunk], signal_out.at[chunk]
        )

    pipeline(
        heads * per_head,
        products,
        lambda chunk: exponentials(chunk, grown_out, top_out, total_out),
        lambda chunk: [],
    )


def far_kernel(shifts, group, held, q_buf, g_buf, far_mask, *refs):
    groups, refs = [refs[4 * i : 4 * i + 4] for i in range(held)], refs[4 * held :]
    far, refs = refs[:2], refs[2:]
    share_out, delta_out, slopes_out, own_outs, sent_out = refs[0], refs[1], refs[2], refs[3 : 3 + shifts], refs[3 + shifts]
    refs = refs[4 + shifts :]
    (key_buf, value_buf, dk_buf, dv_buf), sets = refs[:4], (refs[4:7], refs[7:10])
    rows = q_buf.shape[0]
    heads, fresh = key_buf.shape[:2]
    wide = heads * DH
    per_head = group // JOIN
    chunks = heads * per_head
    width = JOIN * rows
    middle = (shifts - 1) * SLOTS
    place_far(key_buf, value_buf, far, far_mask.at[middle:, :])

    def products(chunk):
        score_ref, signal_ref, _ = sets[chunk % 2]
        return pair_products(key_buf, value_buf, q_buf, g_buf, chunk, chunk // per_head, score_ref, signal_ref)

    def softmax(chunk):
        score_ref, signal_ref, weight_ref = sets[chunk % 2]
        slope_ref = slopes_out.at[chunk]
        tops = [group[2][chunk] for group in groups]
        state = {"top": functools.reduce(jnp.maximum, tops)}

        def top(at):
            for i in range(at, at + BLOCK, 8):
                state["top"] = jnp.maximum(state["top"], score_ref[i : i + 8, :])

        def end_top():
            state["top"] = spread(jnp.max(state["top"], axis=0, keepdims=True))
            state["total"] = jnp.zeros((8, width), jnp.float32)

        def grow(at):
            for i in range(at, at + BLOCK, 8):
                grown = jnp.exp2((score_ref[i : i + 8, :] - state["top"]) * LOG_SCALE)
                score_ref[i : i + 8, :] = grown
                state["total"] = state["total"] + grown

        def end_grow():
            total = spread(jnp.sum(state["total"], axis=0, keepdims=True))
            shrinks = [jnp.exp2((group[2][chunk] - state["top"]) * LOG_SCALE) for group in groups]
            for group, shrink in zip(groups, shrinks):
                total = total + group[3][chunk] * shrink
            share = 1.0 / total
            state["shares"] = [shrink * share for shrink in shrinks] + [share]
            share_out[chunk] = state["shares"][0]
            state["delta"] = jnp.zeros((8, width), jnp.float32)

        def weigh(grown, signal, index, offset, at):
            probs = [grown[i : i + 8, :] * state["shares"][index] for i in range(at, at + BLOCK, 8)]
            weights = jnp.concatenate(probs, axis=0).astype(jnp.bfloat16)
            if index:
                weight_ref[offset + at : offset + at + BLOCK, :] = weights
            terms = weights.astype(jnp.float32) * signal[at : at + BLOCK, :]
            for i in range(0, BLOCK, 8):
                state["delta"] = state["delta"] + terms[i : i + 8]

        def end_weigh():
            state["delta"] = spread(jnp.sum(state["delta"], axis=0, keepdims=True))
            delta_out[chunk] = state["delta"]

        def slope(grown, signal, index, offset, at):
            slopes = []
            for i in range(at, at + BLOCK, 8):
                probs = grown[i : i + 8, :] * state["shares"][index]
                slopes.append(probs * (signal[i : i + 8, :] - state["delta"]))
            slope_ref[offset + at : offset + at + BLOCK, :] = jnp.concatenate(slopes, axis=0).astype(jnp.bfloat16)

        parts = [(group[0].at[chunk], group[1].at[chunk], index, 0) for index, group in enumerate(groups)]
        parts.append((score_ref, signal_ref, held, middle))
        blocks = range(0, fresh, BLOCK)
        steps = [functools.partial(top, at) for at in blocks] + [end_top]
        steps += [functools.partial(grow, at) for at in blocks] + [end_grow]
        for work, chosen, end in ((weigh, parts, end_weigh), (slope, parts[1:], None)):
            steps += [functools.partial(work, *x, at) for x in chosen for at in range(0, x[0].shape[0], BLOCK)]
            steps += [end] if end else []
        return steps

    def gradients(chunk):
        weight_ref = sets[chunk % 2][2]
        head = chunk // per_head
        last = chunk % per_head == per_head - 1

        def collect(total_ref, buf, left, side, factor):
            total = None
            for start in range(0, JOIN, 2):
                cols = slice(start * rows, (start + 2) * rows)
                part = jnp.dot(left(cols), joined(buf, chunk, start, 2), preferred_element_type=jnp.float32)
                total = part if total is None else total + part
            if chunk % per_head:
                total = total + total_ref[...]
            if not last:
                total_ref[...] = total
                return
            cols = slice(side * wide + head * DH, side * wide + (head + 1) * DH)
            for shift, out in enumerate(own_outs):
                at = shift * SLOTS
                out[:, cols] = total[at : at + HALF] * factor
                sent = total[at + HALF : at + SLOTS] * factor
                sent_out[shift * HALF : (shift + 1) * HALF, cols] = sent.astype(sent_out.dtype)

        return [
            functools.partial(collect, dk_buf, q_buf, lambda cols: slopes_out[chunk, :, cols], 0, SCALE),
            functools.partial(collect, dv_buf, g_buf, lambda cols: weight_ref[:, cols], 1, 1.0),
        ]

    pipeline(chunks, products, softmax, gradients)


def near_gradients_kernel(group, q_buf, g_buf, grown, signal, share, delta, slopes_out, own_out, sent_out, *sets):
    rows = q_buf.shape[0]
    wide = own_out.shape[1] // 2
    per_head = group // JOIN
    chunks = wide // DH * per_head
    near = 2 * rows
    totals = {}

    def softmax(chunk):
        weight_ref = sets[chunk % 2]

        def work(at):
            weights, slopes = [], []
            for i in range(at, at + BLOCK, 8):
                probs = grown[chunk, i : i + 8, :] * share[chunk]
                weights.append(probs)
                slopes.append(probs * (signal[chunk, i : i + 8, :] - delta[chunk]))
            weight_ref[at : at + BLOCK, :] = jnp.concatenate(weights, axis=0).astype(jnp.bfloat16)
            slopes_out[chunk, at : at + BLOCK, :] = jnp.concatenate(slopes, axis=0).astype(jnp.bfloat16)

        return [functools.partial(work, at) for at in range(0, near, BLOCK)]

    def gradients(chunk):
        weight_ref = sets[chunk % 2]
        head = chunk // per_head

        def collect(left, buf, side, factor):
            total = totals.pop(side, None)
            for start in range(0, JOIN, 2):
                cols = slice(start * rows, (start + 2) * rows)
                part = jnp.dot(left(cols), joined(buf, chunk, start, 2), preferred_element_type=jnp.float32)
                total = part if total is None else total + part
            if chunk % per_head < per_head - 1:
                totals[side] = total
                return
            cols = slice(side * wide + head * DH, side * wide + (head + 1) * DH)
            own_out[:, cols] = total[:rows] * factor
            sent_out[:, cols] = (total[rows:] * factor).astype(sent_out.dtype)

        return [
            functools.partial(collect, lambda cols: slopes_out[chunk, :, cols], q_buf, 0, SCALE),
            functools.partial(collect, lambda cols: weight_ref[:, cols], g_buf, 1, 1.0),
        ]

    pipeline(chunks, lambda chunk: [], softmax, gradients)


def query_gradients_kernel(group, near_slopes, far_slopes, key_hbm, other_key, *refs):
    far, (dq_hbm, own_key, key_buf, turned_buf, dq_buf, in_sem, out_sem) = refs[:-7], refs[-7:]
    rows = dq_buf.shape[0]
    heads = key_buf.shape[0]
    near = 2 * rows
    per_head = group // JOIN
    load = pltpu.make_async_copy(key_hbm, own_key, in_sem)
    load.start()
    at = rows
    for piece in (other_key, *far):
        size = piece.shape[0]
        for head in range(heads):
            key_buf[head, at : at + size, :] = piece[:, head_cols(head)]
        at += size
    load.wait()
    stores = []
    for head in range(heads):
        key_buf[head, :rows, :] = own_key[:, head_cols(head)]
        turned_buf[head] = key_buf[head].T
        for chunk in range(head * per_head, (head + 1) * per_head):
            for start in range(0, JOIN, 2):
                cols = slice(start * rows, (start + 2) * rows)
                turned = jnp.dot(
                    turned_buf[head, :, :near], near_slopes[chunk, :, cols], preferred_element_type=jnp.float32
                ) + jnp.dot(turned_buf[head, :, near:], far_slopes[chunk, :, cols], preferred_element_type=jnp.float32)
                for i in range(2):
                    dq = turned[:, i * rows : (i + 1) * rows].T * SCALE
                    dq_buf[:, head_cols(chunk * JOIN + start + i)] = dq.astype(jnp.bfloat16)
        cols = slice(head * group * DH, (head + 1) * group * DH)
        stores.append(pltpu.make_async_copy(dq_buf.at[:, cols], dq_hbm.at[:, cols], out_sem.at[head]))
        stores[-1].start()
    for store in stores:
        store.wait()


def in_hbm(x):
    return pltpu.with_memory_space_constraint(x, pltpu.HBM)


def call(kernel, operands, spaces, outs, out_spaces, scratch, limit, products):
    return list(pl.pallas_call(
        kernel,
        out_shape=[jax.ShapeDtypeStruct(*x) for x in outs],
        in_specs=[pl.BlockSpec(memory_space=x) for x in spaces],
        out_specs=[pl.BlockSpec(memory_space=x) for x in out_spaces],
        scratch_shapes=scratch,
        compiler_params=pltpu.CompilerParams(vmem_limit_bytes=limit * 1024 * 1024),
        cost_estimate=pl.CostEstimate(flops=products, bytes_accessed=products // 256, transcendentals=products // 512),
    )(*operands))


def local(queries, keys, values, beacon_keys, beacon_values, grad_out, ratios):
    bf16, f32 = jnp.bfloat16, jnp.float32
    hbm, vmem = pltpu.HBM, pltpu.VMEM
    spans = ratios.shape[0]
    rows, wide = keys.shape
    heads = wide // DH
    group = queries.shape[1] // wide
    chunks = heads * group // JOIN
    width = JOIN * rows
    last = spans - 1
    near, middle, columns = 2 * rows, SLOTS * (last - 1), SLOTS * last
    swap = [(0, 1), (1, 0)]
    neighbour = [(i, i ^ 1 if spans % 2 == 0 or i < spans - 1 else i) for i in range(spans)]
    order = sorted(range(1, last), key=lambda k: (k != last - 1, abs(2 * k - spans)))

    def up(k):
        return [(i, (i + k) % spans) for i in range(spans)]

    left = lax.broadcasted_iota(jnp.int32, (beacon_keys.shape[0], 2 * wide), 1) < wide
    beacons = jnp.where(left, jnp.pad(beacon_keys, ((0, 0), (0, wide))), jnp.pad(beacon_values, ((0, 0), (wide, 0))))
    own = {k: lax.ppermute(beacons, "ctx", up(k)) for k in reversed(order)}
    other_key, other_value = (lax.ppermute(x, "sub", swap) for x in (keys, values))

    product = queries.shape[1] * rows * 2

    def stats_of(size):
        return [((chunks, size, width), f32)] * 2 + [((chunks, 8, width), f32)] * 2

    q_in, g_in, far_mask, *near_stats = call(
        functools.partial(near_kernel, last, group),
        [ratios, in_hbm(queries), in_hbm(grad_out), in_hbm(keys), in_hbm(values), other_key, other_value],
        [pltpu.SMEM] + [hbm] * 4 + [vmem] * 2,
        [(queries.shape, bf16)] * 2 + [((columns, DH), bf16)] + stats_of(near),
        [vmem] * 7,
        [vmem(keys.shape, bf16)] * 2
        + [vmem((heads, near, 2 * DH), bf16), vmem((heads, near, DH), bf16)]
        + [pltpu.SemaphoreType.DMA((2 + 2 * heads,))],
        8,
        2 * product * near,
    )
    groups = [near_stats]
    if middle:
        own[last - 1], near_stats[2] = lax.optimization_barrier((own[last - 1], near_stats[2]))
        own[last] = lax.ppermute(own[last - 1], "ctx", neighbour)
        other = {k: lax.ppermute(own[k], "sub", swap) for k in order}
        far = [x[k] for k in range(1, last) for x in (own, other)]
        middle_stats = call(
            functools.partial(middle_kernel, group),
            [q_in, g_in, far_mask, *far],
            [vmem] * (3 + len(far)),
            stats_of(middle),
            [vmem] * 4,
            [vmem((heads, middle, 2 * DH), bf16), vmem((heads, middle, DH), bf16)],
            8,
            2 * product * middle,
        )
        own[last], middle_stats[2] = lax.optimization_barrier((own[last], middle_stats[2]))
        groups.append(middle_stats)
    else:
        far = []
        own[last] = lax.ppermute(beacons, "ctx", up(last))
    ending = [own[last], lax.ppermute(own[last], "sub", swap)]
    sets = [vmem((SLOTS, width), f32)] * 2 + [vmem((columns, width), bf16)]
    share, delta, far_slopes, *grads, sent = call(
        functools.partial(far_kernel, last, group, len(groups)),
        [q_in, g_in, far_mask, *[x for stats in groups for x in stats], *ending],
        [vmem] * (5 + 4 * len(groups)),
        [((chunks, 8, width), f32)] * 2
        + [((chunks, columns, width), bf16)]
        + [((HALF, 2 * wide), f32)] * last
        + [((HALF * last, 2 * wide), bf16)],
        [vmem] * (4 + last),
        [vmem((heads, SLOTS, 2 * DH), bf16), vmem((heads, SLOTS, DH), bf16)]
        + [vmem((columns, DH), f32)] * 2
        + sets * 2,
        16,
        2 * product * (columns + SLOTS),
    )
    got = lax.ppermute(sent, "sub", swap)
    pairs = {k: grads[k - 1] + got[HALF * (k - 1) : HALF * k].astype(f32) for k in range(1, spans)}
    rounded = {k: x.astype(bf16) for k, x in pairs.items()}
    rounded, delta = lax.optimization_barrier((rounded, delta))
    if middle:
        stepped = lax.ppermute(rounded[last], "ctx", neighbour)
        sums = [lax.ppermute(rounded[k], "ctx", up(-k)) for k in order if k != last - 1]
    else:
        sums = [lax.ppermute(rounded[last], "ctx", up(-last))]
    near_slopes, near_grad, near_sent = call(
        functools.partial(near_gradients_kernel, group),
        [q_in, g_in, near_stats[0], near_stats[1], share, delta],
        [vmem] * 6,
        [((chunks, near, width), bf16), ((rows, 2 * wide), f32), ((rows, 2 * wide), bf16)],
        [vmem] * 3,
        [vmem((near, width), bf16)] * 2,
        8,
        2 * product * near,
    )
    if middle:
        stepped, near_slopes = lax.optimization_barrier((stepped, near_slopes))
        joint = (pairs[last - 1] + stepped.astype(f32)).astype(bf16)
        joint, other_key = lax.optimization_barrier((joint, other_key))
        sums.append(lax.ppermute(joint, "ctx", up(1 - last)))
    (grad_queries,) = call(
        functools.partial(query_gradients_kernel, group),
        [near_slopes, far_slopes, in_hbm(keys), other_key, *far, *ending],
        [vmem] * 2 + [hbm] + [vmem] * (1 + 2 * last),
        [(queries.shape, bf16)],
        [hbm],
        [
            vmem(keys.shape, bf16),
            vmem((heads, near + columns, DH), bf16),
            vmem((heads, DH, near + columns), bf16),
            vmem(queries.shape, bf16),
            pltpu.SemaphoreType.DMA,
            pltpu.SemaphoreType.DMA((heads,)),
        ],
        12,
        product * (near + columns),
    )
    near_total = (near_grad + lax.ppermute(near_sent, "sub", swap).astype(f32)).astype(bf16)
    near_outs = near_total[:, :wide], near_total[:, wide:]
    sums, grad_queries, near_outs = lax.optimization_barrier((sums, grad_queries, near_outs))
    beacon_total = functools.reduce(jnp.add, [x.astype(f32) for x in sums]).astype(bf16)
    return grad_queries, *near_outs, beacon_total[:, :wide], beacon_total[:, wide:]


def solution(mesh):
    rows = P(("grp", "ctx", "sub"), "tp")
    return jax.shard_map(
        local,
        mesh=mesh,
        in_specs=(rows,) * 6 + (P("grp"),),
        out_specs=(rows,) * 5,
        check_vma=False,
    )
```

```python
import functools
import math

import jax
import jax.numpy as jnp
from jax import lax
from jax.experimental import pallas as pl
from jax.experimental.pallas import tpu as pltpu
from jax.sharding import PartitionSpec as P

DH = 128
SPAN = 256
SLOTS = SPAN // 2
HALF = SLOTS // 2
NT = (((1,), (1,)), ((), ()))
HIDDEN = -3e38
JOIN = 4
BLOCK = 16
SCALE = DH ** (-0.5)
LOG_SCALE = SCALE * math.log2(math.e)


def interleave(first, second):
    few, many = sorted((first, second), key=len)
    done = 0
    for index, step in enumerate(few):
        step()
        upto = len(many) * (index + 1) // len(few)
        for other in many[done:upto]:
            other()
        done = upto
    for other in many[done:]:
        other()


def pipeline(chunks, products, softmax, gradients):
    for step in products(0):
        step()
    for chunk in range(chunks):
        matrix = gradients(chunk - 1) if chunk > 0 else []
        matrix = matrix + (products(chunk + 1) if chunk + 1 < chunks else [])
        interleave(matrix, softmax(chunk))
    for step in gradients(chunks - 1):
        step()


def head_cols(head):
    return slice(head * DH, (head + 1) * DH)


def joined(buf, chunk, start, count):
    first = chunk * JOIN + start
    return jnp.concatenate([buf[:, head_cols(first + i)] for i in range(count)], axis=0)


def pair_products(key_buf, value_buf, q_buf, g_buf, chunk, head, score_ref, signal_ref):
    rows = q_buf.shape[0]
    at = [lax.broadcasted_iota(jnp.int32, (rows, DH), axis) for axis in range(2)]
    one_hot = jnp.where(at[0] == at[1], 1.0, 0.0).astype(jnp.bfloat16)
    one_hot = jnp.concatenate([one_hot] * 2, axis=0)

    def score(start):
        queries = jnp.concatenate([joined(q_buf, chunk, start, 2), one_hot], axis=1)
        cols = slice(start * rows, (start + 2) * rows)
        score_ref[:, cols] = lax.dot_general(key_buf[head], queries, NT, preferred_element_type=jnp.float32)

    def signal(start):
        cols = slice(start * rows, (start + 2) * rows)
        signal_ref[:, cols] = lax.dot_general(
            value_buf[head], joined(g_buf, chunk, start, 2), NT, preferred_element_type=jnp.float32
        )

    return [functools.partial(f, start) for f in (score, signal) for start in range(0, JOIN, 2)]


def mask_of(seen):
    return jnp.where(seen, 0.0, HIDDEN).astype(jnp.bfloat16)


def place(key_buf, value_buf, at, keys, values, mask):
    size = mask.shape[0]
    for head in range(key_buf.shape[0]):
        key_buf[head, at : at + size, :DH] = keys[:, head_cols(head)]
        key_buf[head, at : at + size, DH:] = mask
        value_buf[head, at : at + size, :] = values[:, head_cols(head)]


def spread(x):
    return jnp.broadcast_to(x, (8, x.shape[1]))


def exponentials(chunk, grown_out, top_out, total_out):
    score_ref = grown_out.at[chunk]
    columns, width = score_ref.shape
    state = {"top": jnp.full((8, width), HIDDEN, jnp.float32)}

    def top(at):
        for i in range(at, at + BLOCK, 8):
            state["top"] = jnp.maximum(state["top"], score_ref[i : i + 8, :])

    def end_top():
        state["top"] = spread(jnp.max(state["top"], axis=0, keepdims=True))
        top_out[chunk] = state["top"]
        state["total"] = jnp.zeros((8, width), jnp.float32)

    def grow(at):
        for i in range(at, at + BLOCK, 8):
            grown = jnp.exp2((score_ref[i : i + 8, :] - state["top"]) * LOG_SCALE)
            score_ref[i : i + 8, :] = grown
            state["total"] = state["total"] + grown

    def end_grow():
        total_out[chunk] = spread(jnp.sum(state["total"], axis=0, keepdims=True))

    blocks = range(0, columns, BLOCK)
    return [functools.partial(top, at) for at in blocks] + [end_top] + [functools.partial(grow, at) for at in blocks] + [end_grow]


def near_kernel(
    shifts, group, ratios, q_hbm, g_hbm, key_hbm, value_hbm, other_key, other_value, q_buf, g_buf, mask_out, grown_out,
    signal_out, top_out, total_out, own_key, own_value, key_buf, value_buf, sem,
):
    rows = q_buf.shape[0]
    heads = key_buf.shape[0]
    per_head = group // JOIN
    sub = lax.axis_index("sub")
    pairs = [(key_hbm, own_key), (value_hbm, own_value)]
    for head in range(heads):
        cols = slice(head * group * DH, (head + 1) * group * DH)
        pairs += [(q_hbm.at[:, cols], q_buf.at[:, cols]), (g_hbm.at[:, cols], g_buf.at[:, cols])]
    loads = [pltpu.make_async_copy(*pair, sem.at[i]) for i, pair in enumerate(pairs)]
    for load in loads:
        load.start()
    key_at = lax.broadcasted_iota(jnp.int32, (rows, DH), 0)
    token_at = lax.broadcasted_iota(jnp.int32, (rows, DH), 1)
    place(key_buf, value_buf, rows, other_key, other_value, mask_of(key_at < sub * rows))
    here = lax.axis_index("ctx")
    slot_at = lax.broadcasted_iota(jnp.int32, (HALF, DH), 0)
    for shift in range(shifts):
        owner = jnp.maximum(here - 1 - shift, 0)
        live = jnp.where(here > shift, SPAN // ratios[owner], 0)
        for side, first in enumerate((sub * HALF, (1 - sub) * HALF)):
            at = (2 * shift + side) * HALF
            mask_out[at : at + HALF, :] = mask_of(slot_at < live - first)
    loads[0].wait()
    loads[1].wait()
    place(key_buf, value_buf, 0, own_key, own_value, mask_of(key_at <= token_at))

    def products(chunk):
        head = chunk // per_head
        if chunk % per_head == 0:
            loads[2 + 2 * head].wait()
            loads[3 + 2 * head].wait()
        return pair_products(
            key_buf, value_buf, q_buf, g_buf, chunk, head, grown_out.at[chunk], signal_out.at[chunk]
        )

    pipeline(
        heads * per_head,
        products,
        lambda chunk: exponentials(chunk, grown_out, top_out, total_out),
        lambda chunk: [],
    )


def place_far(key_buf, value_buf, far, mask):
    wide = far[0].shape[1] // 2
    for index, source in enumerate(far):
        at = index * HALF
        place(key_buf, value_buf, at, source.at[:, :wide], source.at[:, wide:], mask[at : at + HALF, :])


def far_kernel(shifts, group, q_buf, g_buf, far_mask, near_grown, near_signal, near_top, near_total, *refs):
    far, refs = refs[: 2 * shifts], refs[2 * shifts :]
    share_out, delta_out, slopes_out, own_outs, sent_out = refs[0], refs[1], refs[2], refs[3 : 3 + shifts], refs[3 + shifts]
    refs = refs[4 + shifts :]
    (key_buf, value_buf, dk_buf, dv_buf), sets = refs[:4], (refs[4:7], refs[7:10])
    rows = q_buf.shape[0]
    heads, columns = key_buf.shape[:2]
    wide = heads * DH
    per_head = group // JOIN
    chunks = heads * per_head
    width = JOIN * rows
    place_far(key_buf, value_buf, far, far_mask)

    def products(chunk):
        score_ref, signal_ref, _ = sets[chunk % 2]
        return pair_products(key_buf, value_buf, q_buf, g_buf, chunk, chunk // per_head, score_ref, signal_ref)

    def softmax(chunk):
        score_ref, signal_ref, weight_ref = sets[chunk % 2]
        slope_ref = slopes_out.at[chunk]
        state = {"top": near_top[chunk]}

        def top(at):
            for i in range(at, at + BLOCK, 8):
                state["top"] = jnp.maximum(state["top"], score_ref[i : i + 8, :])

        def end_top():
            state["top"] = spread(jnp.max(state["top"], axis=0, keepdims=True))
            state["total"] = jnp.zeros((8, width), jnp.float32)

        def grow(at):
            for i in range(at, at + BLOCK, 8):
                grown = jnp.exp2((score_ref[i : i + 8, :] - state["top"]) * LOG_SCALE)
                score_ref[i : i + 8, :] = grown
                state["total"] = state["total"] + grown

        def end_grow():
            total = spread(jnp.sum(state["total"], axis=0, keepdims=True))
            shrink = jnp.exp2((near_top[chunk] - state["top"]) * LOG_SCALE)
            state["far"] = 1.0 / (near_total[chunk] * shrink + total)
            state["near"] = shrink * state["far"]
            share_out[chunk] = state["near"]
            state["delta"] = jnp.zeros((8, width), jnp.float32)

        def weigh(grown, signal, share, at):
            probs = [grown[i : i + 8, :] * state[share] for i in range(at, at + BLOCK, 8)]
            weights = jnp.concatenate(probs, axis=0).astype(jnp.bfloat16)
            if share == "far":
                weight_ref[at : at + BLOCK, :] = weights
            terms = weights.astype(jnp.float32) * signal[at : at + BLOCK, :]
            for i in range(0, BLOCK, 8):
                state["delta"] = state["delta"] + terms[i : i + 8]

        def end_weigh():
            state["delta"] = spread(jnp.sum(state["delta"], axis=0, keepdims=True))
            delta_out[chunk] = state["delta"]

        def slope(at):
            slopes = []
            for i in range(at, at + BLOCK, 8):
                probs = score_ref[i : i + 8, :] * state["far"]
                slopes.append(probs * (signal_ref[i : i + 8, :] - state["delta"]))
            slope_ref[at : at + BLOCK, :] = jnp.concatenate(slopes, axis=0).astype(jnp.bfloat16)

        grown, signal = near_grown.at[chunk], near_signal.at[chunk]
        blocks = range(0, columns, BLOCK)
        steps = [functools.partial(top, at) for at in blocks] + [end_top]
        steps += [functools.partial(grow, at) for at in blocks] + [end_grow]
        steps += [functools.partial(weigh, score_ref, signal_ref, "far", at) for at in blocks]
        steps += [functools.partial(weigh, grown, signal, "near", at) for at in range(0, 2 * rows, BLOCK)] + [end_weigh]
        return steps + [functools.partial(slope, at) for at in blocks]

    def gradients(chunk):
        weight_ref = sets[chunk % 2][2]
        head = chunk // per_head
        last = chunk % per_head == per_head - 1

        def collect(total_ref, buf, left, side, factor):
            total = None
            for start in range(0, JOIN, 2):
                cols = slice(start * rows, (start + 2) * rows)
                part = jnp.dot(left(cols), joined(buf, chunk, start, 2), preferred_element_type=jnp.float32)
                total = part if total is None else total + part
            if chunk % per_head:
                total = total + total_ref[...]
            if not last:
                total_ref[...] = total
                return
            cols = slice(side * wide + head * DH, side * wide + (head + 1) * DH)
            for shift, out in enumerate(own_outs):
                at = shift * SLOTS
                out[:, cols] = total[at : at + HALF] * factor
                sent = total[at + HALF : at + SLOTS] * factor
                sent_out[shift * HALF : (shift + 1) * HALF, cols] = sent.astype(sent_out.dtype)

        return [
            functools.partial(collect, dk_buf, q_buf, lambda cols: slopes_out[chunk, :, cols], 0, SCALE),
            functools.partial(collect, dv_buf, g_buf, lambda cols: weight_ref[:, cols], 1, 1.0),
        ]

    pipeline(chunks, products, softmax, gradients)


def near_gradients_kernel(group, q_buf, g_buf, grown, signal, share, delta, slopes_out, own_out, sent_out, *sets):
    rows = q_buf.shape[0]
    wide = own_out.shape[1] // 2
    per_head = group // JOIN
    chunks = wide // DH * per_head
    near = 2 * rows
    totals = {}

    def softmax(chunk):
        weight_ref = sets[chunk % 2]

        def work(at):
            weights, slopes = [], []
            for i in range(at, at + BLOCK, 8):
                probs = grown[chunk, i : i + 8, :] * share[chunk]
                weights.append(probs)
                slopes.append(probs * (signal[chunk, i : i + 8, :] - delta[chunk]))
            weight_ref[at : at + BLOCK, :] = jnp.concatenate(weights, axis=0).astype(jnp.bfloat16)
            slopes_out[chunk, at : at + BLOCK, :] = jnp.concatenate(slopes, axis=0).astype(jnp.bfloat16)

        return [functools.partial(work, at) for at in range(0, near, BLOCK)]

    def gradients(chunk):
        weight_ref = sets[chunk % 2]
        head = chunk // per_head

        def collect(left, buf, side, factor):
            total = totals.pop(side, None)
            for start in range(0, JOIN, 2):
                cols = slice(start * rows, (start + 2) * rows)
                part = jnp.dot(left(cols), joined(buf, chunk, start, 2), preferred_element_type=jnp.float32)
                total = part if total is None else total + part
            if chunk % per_head < per_head - 1:
                totals[side] = total
                return
            cols = slice(side * wide + head * DH, side * wide + (head + 1) * DH)
            own_out[:, cols] = total[:rows] * factor
            sent_out[:, cols] = (total[rows:] * factor).astype(sent_out.dtype)

        return [
            functools.partial(collect, lambda cols: slopes_out[chunk, :, cols], q_buf, 0, SCALE),
            functools.partial(collect, lambda cols: weight_ref[:, cols], g_buf, 1, 1.0),
        ]

    pipeline(chunks, lambda chunk: [], softmax, gradients)


def query_gradients_kernel(group, near_slopes, far_slopes, key_hbm, other_key, *refs):
    far, (dq_hbm, own_key, key_buf, turned_buf, dq_buf, in_sem, out_sem) = refs[:-7], refs[-7:]
    rows = dq_buf.shape[0]
    heads = key_buf.shape[0]
    near = 2 * rows
    per_head = group // JOIN
    load = pltpu.make_async_copy(key_hbm, own_key, in_sem)
    load.start()
    at = rows
    for piece in (other_key, *far):
        size = piece.shape[0]
        for head in range(heads):
            key_buf[head, at : at + size, :] = piece[:, head_cols(head)]
        at += size
    load.wait()
    stores = []
    for head in range(heads):
        key_buf[head, :rows, :] = own_key[:, head_cols(head)]
        turned_buf[head] = key_buf[head].T
        for chunk in range(head * per_head, (head + 1) * per_head):
            for start in range(0, JOIN, 2):
                cols = slice(start * rows, (start + 2) * rows)
                turned = jnp.dot(
                    turned_buf[head, :, :near], near_slopes[chunk, :, cols], preferred_element_type=jnp.float32
                ) + jnp.dot(turned_buf[head, :, near:], far_slopes[chunk, :, cols], preferred_element_type=jnp.float32)
                for i in range(2):
                    dq = turned[:, i * rows : (i + 1) * rows].T * SCALE
                    dq_buf[:, head_cols(chunk * JOIN + start + i)] = dq.astype(jnp.bfloat16)
        cols = slice(head * group * DH, (head + 1) * group * DH)
        stores.append(pltpu.make_async_copy(dq_buf.at[:, cols], dq_hbm.at[:, cols], out_sem.at[head]))
        stores[-1].start()
    for store in stores:
        store.wait()


def in_hbm(x):
    return pltpu.with_memory_space_constraint(x, pltpu.HBM)


def call(kernel, operands, spaces, outs, out_spaces, scratch, limit, products):
    return list(pl.pallas_call(
        kernel,
        out_shape=[jax.ShapeDtypeStruct(*x) for x in outs],
        in_specs=[pl.BlockSpec(memory_space=x) for x in spaces],
        out_specs=[pl.BlockSpec(memory_space=x) for x in out_spaces],
        scratch_shapes=scratch,
        compiler_params=pltpu.CompilerParams(vmem_limit_bytes=limit * 1024 * 1024),
        cost_estimate=pl.CostEstimate(flops=products, bytes_accessed=products // 256, transcendentals=products // 512),
    )(*operands))


def local(queries, keys, values, beacon_keys, beacon_values, grad_out, ratios):
    bf16, f32 = jnp.bfloat16, jnp.float32
    hbm, vmem = pltpu.HBM, pltpu.VMEM
    spans = ratios.shape[0]
    rows, wide = keys.shape
    heads = wide // DH
    group = queries.shape[1] // wide
    chunks = heads * group // JOIN
    width = JOIN * rows
    last = spans - 1
    near, columns = 2 * rows, SLOTS * last
    swap = [(0, 1), (1, 0)]
    shifts = range(1, spans)
    order = sorted(shifts, key=lambda k: abs(2 * k - spans))

    def up(k):
        return [(i, (i + k) % spans) for i in range(spans)]

    left = lax.broadcasted_iota(jnp.int32, (beacon_keys.shape[0], 2 * wide), 1) < wide
    beacons = jnp.where(left, jnp.pad(beacon_keys, ((0, 0), (0, wide))), jnp.pad(beacon_values, ((0, 0), (wide, 0))))
    near_keys, near_values, beacons = lax.optimization_barrier((keys, values, beacons))
    own = {k: lax.ppermute(beacons, "ctx", up(k)) for k in reversed(order)}
    other_key, other_value = (lax.ppermute(x, "sub", swap) for x in (near_keys, near_values))

    product = queries.shape[1] * rows * 2

    def stats_of(size):
        return [((chunks, size, width), f32)] * 2 + [((chunks, 8, width), f32)] * 2

    q_in, g_in, far_mask, *near_stats = call(
        functools.partial(near_kernel, last, group),
        [ratios, in_hbm(queries), in_hbm(grad_out), in_hbm(keys), in_hbm(values), other_key, other_value],
        [pltpu.SMEM] + [hbm] * 4 + [vmem] * 2,
        [(queries.shape, bf16)] * 2 + [((columns, DH), bf16)] + stats_of(near),
        [vmem] * 7,
        [vmem(keys.shape, bf16)] * 2
        + [vmem((heads, near, 2 * DH), bf16), vmem((heads, near, DH), bf16)]
        + [pltpu.SemaphoreType.DMA((2 + 2 * heads,))],
        8,
        2 * product * near,
    )
    first = order[0]
    own[first], near_stats[2] = lax.optimization_barrier((own[first], near_stats[2]))
    other = {k: lax.ppermute(own[k], "sub", swap) for k in order}
    far = [x[k] for k in shifts for x in (own, other)]
    sets = [vmem((columns, width), f32)] * 2 + [vmem((columns, width), bf16)]
    share, delta, far_slopes, *grads, sent = call(
        functools.partial(far_kernel, last, group),
        [q_in, g_in, far_mask, *near_stats, *far],
        [vmem] * (7 + len(far)),
        [((chunks, 8, width), f32)] * 2
        + [((chunks, columns, width), bf16)]
        + [((HALF, 2 * wide), f32)] * last
        + [((HALF * last, 2 * wide), bf16)],
        [vmem] * (4 + last),
        [vmem((heads, columns, 2 * DH), bf16), vmem((heads, columns, DH), bf16)]
        + [vmem((columns, DH), f32)] * 2
        + sets * 2,
        16,
        4 * product * columns,
    )
    got = lax.ppermute(sent, "sub", swap)
    pairs = {k: grads[k - 1] + got[HALF * (k - 1) : HALF * k].astype(f32) for k in range(1, spans)}
    pairs = {k: x.astype(bf16) for k, x in pairs.items()}
    pairs, delta = lax.optimization_barrier((pairs, delta))
    sums = [lax.ppermute(pairs[k], "ctx", up(-k)) for k in order]
    near_slopes, near_grad, near_sent = call(
        functools.partial(near_gradients_kernel, group),
        [q_in, g_in, near_stats[0], near_stats[1], share, delta],
        [vmem] * 6,
        [((chunks, near, width), bf16), ((rows, 2 * wide), f32), ((rows, 2 * wide), bf16)],
        [vmem] * 3,
        [vmem((near, width), bf16)] * 2,
        8,
        product,
    )
    (grad_queries,) = call(
        functools.partial(query_gradients_kernel, group),
        [near_slopes, far_slopes, in_hbm(keys), other_key, *far],
        [vmem] * 2 + [hbm] + [vmem] * (1 + 2 * last),
        [(queries.shape, bf16)],
        [hbm],
        [
            vmem(keys.shape, bf16),
            vmem((heads, near + columns, DH), bf16),
            vmem((heads, DH, near + columns), bf16),
            vmem(queries.shape, bf16),
            pltpu.SemaphoreType.DMA,
            pltpu.SemaphoreType.DMA((heads,)),
        ],
        12,
        product,
    )
    near_total = (near_grad + lax.ppermute(near_sent, "sub", swap).astype(f32)).astype(bf16)
    near_outs = near_total[:, :wide], near_total[:, wide:]
    sums, grad_queries = lax.optimization_barrier((sums, grad_queries))
    beacon_total = functools.reduce(jnp.add, [x.astype(f32) for x in sums]).astype(bf16)
    return grad_queries, *near_outs, beacon_total[:, :wide], beacon_total[:, wide:]


def solution(mesh):
    rows = P(("grp", "ctx", "sub"), "tp")
    return jax.shard_map(
        local,
        mesh=mesh,
        in_specs=(rows,) * 6 + (P("grp"),),
        out_specs=(rows,) * 5,
        check_vma=False,
    )
```

```python
import functools
import math

import jax
import jax.numpy as jnp
from jax import lax
from jax.experimental import pallas as pl
from jax.experimental.pallas import tpu as pltpu
from jax.sharding import PartitionSpec as P

DH = 128
SPAN = 256
SLOTS = SPAN // 2
HALF = SLOTS // 2
NT = (((1,), (1,)), ((), ()))
HIDDEN = -3e38
JOIN = 4
BLOCK = 16
SCALE = DH ** (-0.5)
LOG_SCALE = SCALE * math.log2(math.e)


def interleave(first, second):
    few, many = sorted((first, second), key=len)
    done = 0
    for index, step in enumerate(few):
        step()
        upto = len(many) * (index + 1) // len(few)
        for other in many[done:upto]:
            other()
        done = upto
    for other in many[done:]:
        other()


def pipeline(chunks, products, softmax, gradients):
    for step in products(0):
        step()
    for chunk in range(chunks):
        matrix = gradients(chunk - 1) if chunk > 0 else []
        matrix = matrix + (products(chunk + 1) if chunk + 1 < chunks else [])
        interleave(matrix, softmax(chunk))
    for step in gradients(chunks - 1):
        step()


def head_cols(head):
    return slice(head * DH, (head + 1) * DH)


def joined(buf, chunk, start, count):
    first = chunk * JOIN + start
    return jnp.concatenate([buf[:, head_cols(first + i)] for i in range(count)], axis=0)


def pair_products(key_buf, value_buf, q_buf, g_buf, chunk, head, score_ref, signal_ref):
    rows = q_buf.shape[0]
    at = [lax.broadcasted_iota(jnp.int32, (rows, DH), axis) for axis in range(2)]
    one_hot = jnp.where(at[0] == at[1], 1.0, 0.0).astype(jnp.bfloat16)
    one_hot = jnp.concatenate([one_hot] * 2, axis=0)

    def score(start):
        queries = jnp.concatenate([joined(q_buf, chunk, start, 2), one_hot], axis=1)
        cols = slice(start * rows, (start + 2) * rows)
        score_ref[:, cols] = lax.dot_general(key_buf[head], queries, NT, preferred_element_type=jnp.float32)

    def signal(start):
        cols = slice(start * rows, (start + 2) * rows)
        signal_ref[:, cols] = lax.dot_general(
            value_buf[head], joined(g_buf, chunk, start, 2), NT, preferred_element_type=jnp.float32
        )

    return [functools.partial(f, start) for f in (score, signal) for start in range(0, JOIN, 2)]


def mask_of(seen):
    return jnp.where(seen, 0.0, HIDDEN).astype(jnp.bfloat16)


def place(key_buf, value_buf, at, keys, values, mask):
    size = mask.shape[0]
    for head in range(key_buf.shape[0]):
        key_buf[head, at : at + size, :DH] = keys[:, head_cols(head)]
        key_buf[head, at : at + size, DH:] = mask
        value_buf[head, at : at + size, :] = values[:, head_cols(head)]


def spread(x):
    return jnp.broadcast_to(x, (8, x.shape[1]))


def exponentials(chunk, grown_out, top_out, total_out):
    score_ref = grown_out.at[chunk]
    columns, width = score_ref.shape
    state = {"top": jnp.full((8, width), HIDDEN, jnp.float32)}

    def top(at):
        for i in range(at, at + BLOCK, 8):
            state["top"] = jnp.maximum(state["top"], score_ref[i : i + 8, :])

    def end_top():
        state["top"] = spread(jnp.max(state["top"], axis=0, keepdims=True))
        top_out[chunk] = state["top"]
        state["total"] = jnp.zeros((8, width), jnp.float32)

    def grow(at):
        for i in range(at, at + BLOCK, 8):
            grown = jnp.exp2((score_ref[i : i + 8, :] - state["top"]) * LOG_SCALE)
            score_ref[i : i + 8, :] = grown
            state["total"] = state["total"] + grown

    def end_grow():
        total_out[chunk] = spread(jnp.sum(state["total"], axis=0, keepdims=True))

    blocks = range(0, columns, BLOCK)
    return [functools.partial(top, at) for at in blocks] + [end_top] + [functools.partial(grow, at) for at in blocks] + [end_grow]


def near_kernel(
    shifts, group, ratios, q_hbm, g_hbm, key_hbm, value_hbm, other_key, other_value, q_buf, g_buf, mask_out, grown_out,
    signal_out, top_out, total_out, own_key, own_value, key_buf, value_buf, sem,
):
    rows = q_buf.shape[0]
    heads = key_buf.shape[0]
    per_head = group // JOIN
    sub = lax.axis_index("sub")
    pairs = [(key_hbm, own_key), (value_hbm, own_value)]
    for head in range(heads):
        cols = slice(head * group * DH, (head + 1) * group * DH)
        pairs += [(q_hbm.at[:, cols], q_buf.at[:, cols]), (g_hbm.at[:, cols], g_buf.at[:, cols])]
    loads = [pltpu.make_async_copy(*pair, sem.at[i]) for i, pair in enumerate(pairs)]
    for load in loads:
        load.start()
    key_at = lax.broadcasted_iota(jnp.int32, (rows, DH), 0)
    token_at = lax.broadcasted_iota(jnp.int32, (rows, DH), 1)
    place(key_buf, value_buf, rows, other_key, other_value, mask_of(key_at < sub * rows))
    here = lax.axis_index("ctx")
    slot_at = lax.broadcasted_iota(jnp.int32, (HALF, DH), 0)
    for shift in range(shifts):
        owner = jnp.maximum(here - 1 - shift, 0)
        live = jnp.where(here > shift, SPAN // ratios[owner], 0)
        for side, first in enumerate((sub * HALF, (1 - sub) * HALF)):
            at = (2 * shift + side) * HALF
            mask_out[at : at + HALF, :] = mask_of(slot_at < live - first)
    loads[0].wait()
    loads[1].wait()
    place(key_buf, value_buf, 0, own_key, own_value, mask_of(key_at <= token_at))

    def products(chunk):
        head = chunk // per_head
        if chunk % per_head == 0:
            loads[2 + 2 * head].wait()
            loads[3 + 2 * head].wait()
        return pair_products(
            key_buf, value_buf, q_buf, g_buf, chunk, head, grown_out.at[chunk], signal_out.at[chunk]
        )

    pipeline(
        heads * per_head,
        products,
        lambda chunk: exponentials(chunk, grown_out, top_out, total_out),
        lambda chunk: [],
    )


def place_far(key_buf, value_buf, far, mask):
    wide = far[0].shape[1] // 2
    for index, source in enumerate(far):
        at = index * HALF
        place(key_buf, value_buf, at, source.at[:, :wide], source.at[:, wide:], mask[at : at + HALF, :])


def far_kernel(shifts, group, *refs):
    here = lax.axis_index("ctx")
    levels = sorted({shifts * i // 3 for i in range(4)} | set(range(min(shifts, 4))))
    for low, level in zip([-1, *levels], levels):
        pl.when((here > low) & (here <= level))(functools.partial(far_part, shifts, level, group, *refs))


def far_part(shifts, seen, group, q_buf, g_buf, far_mask, near_grown, near_signal, near_top, near_total, *refs):
    far, refs = refs[: 2 * shifts], refs[2 * shifts :]
    share_out, delta_out, slopes_out, own_outs, sent_outs = refs[0], refs[1], refs[2], refs[3 : 3 + shifts], refs[3 + shifts : 3 + 2 * shifts]
    refs = refs[3 + 2 * shifts :]
    (key_buf, value_buf, dk_buf, dv_buf), sets = refs[:4], (refs[4:7], refs[7:10])
    rows = q_buf.shape[0]
    heads = key_buf.shape[0]
    columns = seen * SLOTS
    wide = heads * DH
    per_head = group // JOIN
    chunks = heads * per_head
    width = JOIN * rows
    if seen:
        place_far(key_buf, value_buf, far[: 2 * seen], far_mask)
    for out in (*own_outs[seen:], *sent_outs[seen:]):
        out[...] = jnp.zeros_like(out)
    key_buf, value_buf = key_buf.at[:, :columns, :], value_buf.at[:, :columns, :]
    sets = [[ref.at[:columns, :] for ref in refs] for refs in sets]

    def products(chunk):
        if not seen:
            return []
        score_ref, signal_ref, _ = sets[chunk % 2]
        return pair_products(key_buf, value_buf, q_buf, g_buf, chunk, chunk // per_head, score_ref, signal_ref)

    def softmax(chunk):
        score_ref, signal_ref, weight_ref = sets[chunk % 2]
        slope_ref = slopes_out.at[chunk]
        state = {"top": near_top[chunk]}

        def top(at):
            for i in range(at, at + BLOCK, 8):
                state["top"] = jnp.maximum(state["top"], score_ref[i : i + 8, :])

        def end_top():
            state["top"] = spread(jnp.max(state["top"], axis=0, keepdims=True))
            state["total"] = jnp.zeros((8, width), jnp.float32)

        def grow(at):
            for i in range(at, at + BLOCK, 8):
                grown = jnp.exp2((score_ref[i : i + 8, :] - state["top"]) * LOG_SCALE)
                score_ref[i : i + 8, :] = grown
                state["total"] = state["total"] + grown

        def end_grow():
            total = spread(jnp.sum(state["total"], axis=0, keepdims=True))
            shrink = jnp.exp2((near_top[chunk] - state["top"]) * LOG_SCALE)
            state["far"] = 1.0 / (near_total[chunk] * shrink + total)
            state["near"] = shrink * state["far"]
            share_out[chunk] = state["near"]
            state["delta"] = jnp.zeros((8, width), jnp.float32)

        def weigh(grown, signal, share, at):
            probs = [grown[i : i + 8, :] * state[share] for i in range(at, at + BLOCK, 8)]
            weights = jnp.concatenate(probs, axis=0).astype(jnp.bfloat16)
            if share == "far":
                weight_ref[at : at + BLOCK, :] = weights
            terms = weights.astype(jnp.float32) * signal[at : at + BLOCK, :]
            for i in range(0, BLOCK, 8):
                state["delta"] = state["delta"] + terms[i : i + 8]

        def end_weigh():
            state["delta"] = spread(jnp.sum(state["delta"], axis=0, keepdims=True))
            delta_out[chunk] = state["delta"]

        def slope(at):
            slopes = []
            for i in range(at, at + BLOCK, 8):
                probs = score_ref[i : i + 8, :] * state["far"]
                slopes.append(probs * (signal_ref[i : i + 8, :] - state["delta"]))
            slope_ref[at : at + BLOCK, :] = jnp.concatenate(slopes, axis=0).astype(jnp.bfloat16)

        grown, signal = near_grown.at[chunk], near_signal.at[chunk]
        blocks = range(0, columns, BLOCK)

        def clear():
            if seen < shifts:
                slope_ref[columns:, :] = jnp.zeros((SLOTS * (shifts - seen), width), jnp.bfloat16)

        steps = [clear] + [functools.partial(top, at) for at in blocks] + [end_top]
        steps += [functools.partial(grow, at) for at in blocks] + [end_grow]
        steps += [functools.partial(weigh, score_ref, signal_ref, "far", at) for at in blocks]
        steps += [functools.partial(weigh, grown, signal, "near", at) for at in range(0, 2 * rows, BLOCK)] + [end_weigh]
        return steps + [functools.partial(slope, at) for at in blocks]

    def gradients(chunk):
        if not seen:
            return []
        weight_ref = sets[chunk % 2][2]
        head = chunk // per_head
        last = chunk % per_head == per_head - 1

        def collect(total_ref, buf, left, side, factor):
            total = None
            for start in range(0, JOIN, 2):
                cols = slice(start * rows, (start + 2) * rows)
                part = jnp.dot(left(cols), joined(buf, chunk, start, 2), preferred_element_type=jnp.float32)
                total = part if total is None else total + part
            if chunk % per_head:
                total = total + total_ref[:columns, :]
            if not last:
                total_ref[:columns, :] = total
                return
            cols = slice(side * wide + head * DH, side * wide + (head + 1) * DH)
            for shift in range(seen):
                at = shift * SLOTS
                own_outs[shift][:, cols] = total[at : at + HALF] * factor
                sent_outs[shift][:, cols] = (total[at + HALF : at + SLOTS] * factor).astype(jnp.bfloat16)

        return [
            functools.partial(collect, dk_buf, q_buf, lambda cols: slopes_out[chunk, :columns, cols], 0, SCALE),
            functools.partial(collect, dv_buf, g_buf, lambda cols: weight_ref[:, cols], 1, 1.0),
        ]

    pipeline(chunks, products, softmax, gradients)


def near_gradients_kernel(group, q_buf, g_buf, grown, signal, share, delta, slopes_out, own_out, sent_out, *sets):
    rows = q_buf.shape[0]
    wide = own_out.shape[1] // 2
    per_head = group // JOIN
    chunks = wide // DH * per_head
    near = 2 * rows
    totals = {}

    def softmax(chunk):
        weight_ref = sets[chunk % 2]

        def work(at):
            weights, slopes = [], []
            for i in range(at, at + BLOCK, 8):
                probs = grown[chunk, i : i + 8, :] * share[chunk]
                weights.append(probs)
                slopes.append(probs * (signal[chunk, i : i + 8, :] - delta[chunk]))
            weight_ref[at : at + BLOCK, :] = jnp.concatenate(weights, axis=0).astype(jnp.bfloat16)
            slopes_out[chunk, at : at + BLOCK, :] = jnp.concatenate(slopes, axis=0).astype(jnp.bfloat16)

        return [functools.partial(work, at) for at in range(0, near, BLOCK)]

    def gradients(chunk):
        weight_ref = sets[chunk % 2]
        head = chunk // per_head

        def collect(left, buf, side, factor):
            total = totals.pop(side, None)
            for start in range(0, JOIN, 2):
                cols = slice(start * rows, (start + 2) * rows)
                part = jnp.dot(left(cols), joined(buf, chunk, start, 2), preferred_element_type=jnp.float32)
                total = part if total is None else total + part
            if chunk % per_head < per_head - 1:
                totals[side] = total
                return
            cols = slice(side * wide + head * DH, side * wide + (head + 1) * DH)
            own_out[:, cols] = total[:rows] * factor
            sent_out[:, cols] = (total[rows:] * factor).astype(sent_out.dtype)

        return [
            functools.partial(collect, lambda cols: slopes_out[chunk, :, cols], q_buf, 0, SCALE),
            functools.partial(collect, lambda cols: weight_ref[:, cols], g_buf, 1, 1.0),
        ]

    pipeline(chunks, lambda chunk: [], softmax, gradients)


def query_gradients_kernel(group, near_slopes, far_slopes, key_hbm, other_key, *refs):
    far, (dq_hbm, own_key, key_buf, turned_buf, dq_buf, in_sem, out_sem) = refs[:-7], refs[-7:]
    rows = dq_buf.shape[0]
    heads = key_buf.shape[0]
    near = 2 * rows
    per_head = group // JOIN
    load = pltpu.make_async_copy(key_hbm, own_key, in_sem)
    load.start()
    at = rows
    for piece in (other_key, *far):
        size = piece.shape[0]
        for head in range(heads):
            key_buf[head, at : at + size, :] = piece[:, head_cols(head)]
        at += size
    load.wait()
    stores = []
    for head in range(heads):
        key_buf[head, :rows, :] = own_key[:, head_cols(head)]
        turned_buf[head] = key_buf[head].T
        for chunk in range(head * per_head, (head + 1) * per_head):
            for start in range(0, JOIN, 2):
                cols = slice(start * rows, (start + 2) * rows)
                turned = jnp.dot(
                    turned_buf[head, :, :near], near_slopes[chunk, :, cols], preferred_element_type=jnp.float32
                ) + jnp.dot(turned_buf[head, :, near:], far_slopes[chunk, :, cols], preferred_element_type=jnp.float32)
                for i in range(2):
                    dq = turned[:, i * rows : (i + 1) * rows].T * SCALE
                    dq_buf[:, head_cols(chunk * JOIN + start + i)] = dq.astype(jnp.bfloat16)
        cols = slice(head * group * DH, (head + 1) * group * DH)
        stores.append(pltpu.make_async_copy(dq_buf.at[:, cols], dq_hbm.at[:, cols], out_sem.at[head]))
        stores[-1].start()
    for store in stores:
        store.wait()


def in_hbm(x):
    return pltpu.with_memory_space_constraint(x, pltpu.HBM)


def call(kernel, operands, spaces, outs, out_spaces, scratch, limit, products):
    return list(pl.pallas_call(
        kernel,
        out_shape=[jax.ShapeDtypeStruct(*x) for x in outs],
        in_specs=[pl.BlockSpec(memory_space=x) for x in spaces],
        out_specs=[pl.BlockSpec(memory_space=x) for x in out_spaces],
        scratch_shapes=scratch,
        compiler_params=pltpu.CompilerParams(vmem_limit_bytes=limit * 1024 * 1024),
        cost_estimate=pl.CostEstimate(flops=products, bytes_accessed=products // 256, transcendentals=products // 512),
    )(*operands))


def local(queries, keys, values, beacon_keys, beacon_values, grad_out, ratios):
    bf16, f32 = jnp.bfloat16, jnp.float32
    hbm, vmem = pltpu.HBM, pltpu.VMEM
    spans = ratios.shape[0]
    rows, wide = keys.shape
    heads = wide // DH
    group = queries.shape[1] // wide
    chunks = heads * group // JOIN
    width = JOIN * rows
    last = spans - 1
    near, columns = 2 * rows, SLOTS * last
    swap = [(0, 1), (1, 0)]
    shifts = range(1, spans)
    order = sorted(shifts, key=lambda k: abs(2 * k - spans))

    def up(k):
        return [(i, (i + k) % spans) for i in range(spans)]

    left = lax.broadcasted_iota(jnp.int32, (beacon_keys.shape[0], 2 * wide), 1) < wide
    beacons = jnp.where(left, jnp.pad(beacon_keys, ((0, 0), (0, wide))), jnp.pad(beacon_values, ((0, 0), (wide, 0))))
    near_keys, near_values, beacons = lax.optimization_barrier((keys, values, beacons))
    own = {k: lax.ppermute(beacons, "ctx", up(k)) for k in reversed(order)}
    other_key, other_value = (lax.ppermute(x, "sub", swap) for x in (near_keys, near_values))

    product = queries.shape[1] * rows * 2

    def stats_of(size):
        return [((chunks, size, width), f32)] * 2 + [((chunks, 8, width), f32)] * 2

    q_in, g_in, far_mask, *near_stats = call(
        functools.partial(near_kernel, last, group),
        [ratios, in_hbm(queries), in_hbm(grad_out), in_hbm(keys), in_hbm(values), other_key, other_value],
        [pltpu.SMEM] + [hbm] * 4 + [vmem] * 2,
        [(queries.shape, bf16)] * 2 + [((columns, DH), bf16)] + stats_of(near),
        [vmem] * 7,
        [vmem(keys.shape, bf16)] * 2
        + [vmem((heads, near, 2 * DH), bf16), vmem((heads, near, DH), bf16)]
        + [pltpu.SemaphoreType.DMA((2 + 2 * heads,))],
        8,
        2 * product * near,
    )
    first = order[0]
    own[first], near_stats[2] = lax.optimization_barrier((own[first], near_stats[2]))
    other = {k: lax.ppermute(own[k], "sub", swap) for k in order}
    far = [x[k] for k in shifts for x in (own, other)]
    sets = [vmem((columns, width), f32)] * 2 + [vmem((columns, width), bf16)]
    share, delta, far_slopes, *grads = call(
        functools.partial(far_kernel, last, group),
        [q_in, g_in, far_mask, *near_stats, *far],
        [vmem] * (7 + len(far)),
        [((chunks, 8, width), f32)] * 2
        + [((chunks, columns, width), bf16)]
        + [((HALF, 2 * wide), f32)] * last
        + [((HALF, 2 * wide), bf16)] * last,
        [vmem] * (3 + 2 * last),
        [vmem((heads, columns, 2 * DH), bf16), vmem((heads, columns, DH), bf16)]
        + [vmem((columns, DH), f32)] * 2
        + sets * 2,
        12 + 30 * columns * width // 2**20,
        4 * product * columns,
    )
    sent = dict(zip(shifts, grads[last:]))

    def pair(k):
        return (grads[k - 1] + lax.ppermute(sent[k], "sub", swap).astype(f32)).astype(bf16)

    pairs = {k: pair(k) for k in order}
    pairs[order[-1]], delta = lax.optimization_barrier((pairs[order[-1]], delta))
    sums = [lax.ppermute(pairs[k], "ctx", up(-k)) for k in order]
    near_slopes, near_grad, near_sent = call(
        functools.partial(near_gradients_kernel, group),
        [q_in, g_in, near_stats[0], near_stats[1], share, delta],
        [vmem] * 6,
        [((chunks, near, width), bf16), ((rows, 2 * wide), f32), ((rows, 2 * wide), bf16)],
        [vmem] * 3,
        [vmem((near, width), bf16)] * 2,
        8,
        product,
    )
    (grad_queries,) = call(
        functools.partial(query_gradients_kernel, group),
        [near_slopes, far_slopes, in_hbm(keys), other_key, *far],
        [vmem] * 2 + [hbm] + [vmem] * (1 + 2 * last),
        [(queries.shape, bf16)],
        [hbm],
        [
            vmem(keys.shape, bf16),
            vmem((heads, near + columns, DH), bf16),
            vmem((heads, DH, near + columns), bf16),
            vmem(queries.shape, bf16),
            pltpu.SemaphoreType.DMA,
            pltpu.SemaphoreType.DMA((heads,)),
        ],
        12,
        product,
    )
    near_total = (near_grad + lax.ppermute(near_sent, "sub", swap).astype(f32)).astype(bf16)
    sums, grad_queries = lax.optimization_barrier((sums, grad_queries))
    beacon_total = functools.reduce(jnp.add, [x.astype(f32) for x in sums]).astype(bf16)
    outs = [x for y in (near_total, beacon_total) for x in (y[:, :wide], y[:, wide:])]
    return (grad_queries, *outs)


def solution(mesh):
    rows = P(("grp", "ctx", "sub"), "tp")
    return jax.shard_map(
        local,
        mesh=mesh,
        in_specs=(rows,) * 6 + (P("grp"),),
        out_specs=(rows,) * 5,
        check_vma=False,
    )
```

```python
import functools
import math

import jax
import jax.numpy as jnp
from jax import lax
from jax.experimental import pallas as pl
from jax.experimental.pallas import tpu as pltpu
from jax.sharding import PartitionSpec as P

DH = 128
SPAN = 256
SLOTS = SPAN // 2
HALF = SLOTS // 2
NT = (((1,), (1,)), ((), ()))
HIDDEN = -3e38
JOIN = 4
BLOCK = 16
SCALE = DH ** (-0.5)
LOG_SCALE = SCALE * math.log2(math.e)


def interleave(first, second):
    few, many = sorted((first, second), key=len)
    done = 0
    for index, step in enumerate(few):
        step()
        upto = len(many) * (index + 1) // len(few)
        for other in many[done:upto]:
            other()
        done = upto
    for other in many[done:]:
        other()


def pipeline(chunks, products, softmax, gradients):
    for step in products(0):
        step()
    for chunk in range(chunks):
        matrix = gradients(chunk - 1) if chunk > 0 else []
        matrix = matrix + (products(chunk + 1) if chunk + 1 < chunks else [])
        interleave(matrix, softmax(chunk))
    for step in gradients(chunks - 1):
        step()


def head_cols(head):
    return slice(head * DH, (head + 1) * DH)


def joined(buf, chunk, start, count):
    first = chunk * JOIN + start
    return jnp.concatenate([buf[:, head_cols(first + i)] for i in range(count)], axis=0)


def pair_products(key_buf, value_buf, q_buf, g_buf, chunk, head, score_ref, signal_ref):
    rows = q_buf.shape[0]
    at = [lax.broadcasted_iota(jnp.int32, (rows, DH), axis) for axis in range(2)]
    one_hot = jnp.where(at[0] == at[1], 1.0, 0.0).astype(jnp.bfloat16)
    one_hot = jnp.concatenate([one_hot] * 2, axis=0)

    def score(start):
        queries = jnp.concatenate([joined(q_buf, chunk, start, 2), one_hot], axis=1)
        cols = slice(start * rows, (start + 2) * rows)
        score_ref[:, cols] = lax.dot_general(key_buf[head], queries, NT, preferred_element_type=jnp.float32)

    def signal(start):
        cols = slice(start * rows, (start + 2) * rows)
        signal_ref[:, cols] = lax.dot_general(
            value_buf[head], joined(g_buf, chunk, start, 2), NT, preferred_element_type=jnp.float32
        )

    return [functools.partial(f, start) for f in (score, signal) for start in range(0, JOIN, 2)]


def mask_of(seen):
    return jnp.where(seen, 0.0, HIDDEN).astype(jnp.bfloat16)


def place(key_buf, value_buf, at, keys, values, mask):
    size = mask.shape[0]
    for head in range(key_buf.shape[0]):
        key_buf[head, at : at + size, :DH] = keys[:, head_cols(head)]
        key_buf[head, at : at + size, DH:] = mask
        value_buf[head, at : at + size, :] = values[:, head_cols(head)]


def spread(x):
    return jnp.broadcast_to(x, (8, x.shape[1]))


def exponentials(chunk, grown_out, top_out, total_out):
    score_ref = grown_out.at[chunk]
    columns, width = score_ref.shape
    state = {"top": jnp.full((8, width), HIDDEN, jnp.float32)}

    def top(at):
        for i in range(at, at + BLOCK, 8):
            state["top"] = jnp.maximum(state["top"], score_ref[i : i + 8, :])

    def end_top():
        state["top"] = spread(jnp.max(state["top"], axis=0, keepdims=True))
        top_out[chunk] = state["top"]
        state["total"] = jnp.zeros((8, width), jnp.float32)

    def grow(at):
        for i in range(at, at + BLOCK, 8):
            grown = jnp.exp2((score_ref[i : i + 8, :] - state["top"]) * LOG_SCALE)
            score_ref[i : i + 8, :] = grown
            state["total"] = state["total"] + grown

    def end_grow():
        total_out[chunk] = spread(jnp.sum(state["total"], axis=0, keepdims=True))

    blocks = range(0, columns, BLOCK)
    return [functools.partial(top, at) for at in blocks] + [end_top] + [functools.partial(grow, at) for at in blocks] + [end_grow]


def piece_of(shifts, shift, side):
    return side * (shifts - 1) + shift if shift < shifts - 1 else 2 * (shifts - 1) + side


def near_kernel(
    shifts, group, ratios, q_hbm, g_hbm, key_hbm, value_hbm, other_key, other_value, q_buf, g_buf, mask_out, grown_out,
    signal_out, top_out, total_out, own_key, own_value, key_buf, value_buf, sem,
):
    rows = q_buf.shape[0]
    heads = key_buf.shape[0]
    per_head = group // JOIN
    sub = lax.axis_index("sub")
    pairs = [(key_hbm, own_key), (value_hbm, own_value)]
    for head in range(heads):
        cols = slice(head * group * DH, (head + 1) * group * DH)
        pairs += [(q_hbm.at[:, cols], q_buf.at[:, cols]), (g_hbm.at[:, cols], g_buf.at[:, cols])]
    loads = [pltpu.make_async_copy(*pair, sem.at[i]) for i, pair in enumerate(pairs)]
    for load in loads:
        load.start()
    key_at = lax.broadcasted_iota(jnp.int32, (rows, DH), 0)
    token_at = lax.broadcasted_iota(jnp.int32, (rows, DH), 1)
    place(key_buf, value_buf, rows, other_key, other_value, mask_of(key_at < sub * rows))
    here = lax.axis_index("ctx")
    slot_at = lax.broadcasted_iota(jnp.int32, (HALF, DH), 0)
    for shift in range(shifts):
        owner = jnp.maximum(here - 1 - shift, 0)
        live = jnp.where(here > shift, SPAN // ratios[owner], 0)
        for side, first in enumerate((sub * HALF, (1 - sub) * HALF)):
            at = piece_of(shifts, shift, side) * HALF
            mask_out[at : at + HALF, :] = mask_of(slot_at < live - first)
    loads[0].wait()
    loads[1].wait()
    place(key_buf, value_buf, 0, own_key, own_value, mask_of(key_at <= token_at))

    def products(chunk):
        head = chunk // per_head
        if chunk % per_head == 0:
            loads[2 + 2 * head].wait()
            loads[3 + 2 * head].wait()
        return pair_products(
            key_buf, value_buf, q_buf, g_buf, chunk, head, grown_out.at[chunk], signal_out.at[chunk]
        )

    pipeline(
        heads * per_head,
        products,
        lambda chunk: exponentials(chunk, grown_out, top_out, total_out),
        lambda chunk: [],
    )


def place_far(key_buf, value_buf, far, mask):
    wide = far[0].shape[1] // 2
    for index, source in enumerate(far):
        at = index * HALF
        place(key_buf, value_buf, at, source.at[:, :wide], source.at[:, wide:], mask[at : at + HALF, :])


def middle_kernel(group, q_buf, g_buf, far_mask, *refs):
    far, (grown_out, signal_out, top_out, total_out, key_buf, value_buf) = refs[:-6], refs[-6:]
    heads = key_buf.shape[0]
    per_head = group // JOIN
    place_far(key_buf, value_buf, far, far_mask)

    def products(chunk):
        return pair_products(
            key_buf, value_buf, q_buf, g_buf, chunk, chunk // per_head, grown_out.at[chunk], signal_out.at[chunk]
        )

    pipeline(
        heads * per_head,
        products,
        lambda chunk: exponentials(chunk, grown_out, top_out, total_out),
        lambda chunk: [],
    )


def far_kernel(shifts, group, *refs):
    here = lax.axis_index("ctx")
    levels = sorted({0, shifts - 1, shifts})
    for low, level in zip([-1, *levels], levels):
        pl.when((here > low) & (here <= level))(functools.partial(far_part, shifts, level, group, *refs))


def far_part(shifts, seen, group, q_buf, g_buf, far_mask, *refs):
    groups, refs = [refs[4 * i : 4 * i + 4] for i in range(min(shifts, 2))], refs[4 * min(shifts, 2) :]
    far, refs = refs[: shifts + 1], refs[shifts + 1 :]
    share_out, delta_out, slopes_out, own_outs, sent_outs = refs[0], refs[1], refs[2], refs[3 : 3 + shifts], refs[3 + shifts : 3 + 2 * shifts]
    refs = refs[3 + 2 * shifts :]
    (key_buf, value_buf, dk_buf, dv_buf), sets = refs[:4], (refs[4:7], refs[7:10])
    rows = q_buf.shape[0]
    heads = key_buf.shape[0]
    middle = (shifts - 1) * HALF if seen else 0
    fresh = middle + (SLOTS if seen == shifts else 0)
    columns = middle + fresh
    wide = heads * DH
    per_head = group // JOIN
    chunks = heads * per_head
    width = JOIN * rows
    if not middle:
        groups = groups[:1]
    if fresh:
        place_far(key_buf, value_buf, far[: fresh // HALF], far_mask.at[middle:, :])
    key_buf, value_buf = key_buf.at[:, :fresh, :], value_buf.at[:, :fresh, :]
    sets = [(score.at[:fresh, :], signal.at[:fresh, :], weight) for score, signal, weight in sets]
    for out in (*own_outs[seen:], *sent_outs[seen:]):
        out[...] = jnp.zeros_like(out)

    def products(chunk):
        if not fresh:
            return []
        score_ref, signal_ref, _ = sets[chunk % 2]
        return pair_products(key_buf, value_buf, q_buf, g_buf, chunk, chunk // per_head, score_ref, signal_ref)

    def softmax(chunk):
        score_ref, signal_ref, weight_ref = sets[chunk % 2]
        slope_ref = slopes_out.at[chunk]
        state = {"top": functools.reduce(jnp.maximum, [group[2][chunk] for group in groups])}

        def clear():
            if seen < shifts:
                slope_ref[columns:, :] = jnp.zeros((SLOTS * shifts - columns, width), jnp.bfloat16)

        def top(at):
            for i in range(at, at + BLOCK, 8):
                state["top"] = jnp.maximum(state["top"], score_ref[i : i + 8, :])

        def end_top():
            state["top"] = spread(jnp.max(state["top"], axis=0, keepdims=True))
            state["total"] = jnp.zeros((8, width), jnp.float32)

        def grow(at):
            for i in range(at, at + BLOCK, 8):
                grown = jnp.exp2((score_ref[i : i + 8, :] - state["top"]) * LOG_SCALE)
                score_ref[i : i + 8, :] = grown
                state["total"] = state["total"] + grown

        def end_grow():
            shrinks = [jnp.exp2((group[2][chunk] - state["top"]) * LOG_SCALE) for group in groups]
            totals = [group[3][chunk] * shrink for group, shrink in zip(groups, shrinks)]
            if fresh:
                totals.append(spread(jnp.sum(state["total"], axis=0, keepdims=True)))
            share = 1.0 / functools.reduce(jnp.add, totals)
            state["shares"] = [shrink * share for shrink in shrinks] + [share]
            share_out[chunk] = state["shares"][0]
            state["delta"] = jnp.zeros((8, width), jnp.float32)

        def weigh(grown, signal, index, offset, at):
            probs = [grown[i : i + 8, :] * state["shares"][index] for i in range(at, at + BLOCK, 8)]
            weights = jnp.concatenate(probs, axis=0).astype(jnp.bfloat16)
            if index:
                weight_ref[offset + at : offset + at + BLOCK, :] = weights
            terms = weights.astype(jnp.float32) * signal[at : at + BLOCK, :]
            for i in range(0, BLOCK, 8):
                state["delta"] = state["delta"] + terms[i : i + 8]

        def end_weigh():
            state["delta"] = spread(jnp.sum(state["delta"], axis=0, keepdims=True))
            delta_out[chunk] = state["delta"]

        def slope(grown, signal, index, offset, at):
            slopes = []
            for i in range(at, at + BLOCK, 8):
                probs = grown[i : i + 8, :] * state["shares"][index]
                slopes.append(probs * (signal[i : i + 8, :] - state["delta"]))
            slope_ref[offset + at : offset + at + BLOCK, :] = jnp.concatenate(slopes, axis=0).astype(jnp.bfloat16)

        parts = [(group[0].at[chunk], group[1].at[chunk], index, 0) for index, group in enumerate(groups)]
        sizes = [2 * rows, middle][: len(groups)]
        steps = [clear]
        if fresh:
            parts.append((score_ref, signal_ref, len(groups), middle))
            sizes.append(fresh)
            steps += [functools.partial(top, at) for at in range(0, fresh, BLOCK)] + [end_top]
            steps += [functools.partial(grow, at) for at in range(0, fresh, BLOCK)]
        steps.append(end_grow)
        for work, first, end in ((weigh, 0, end_weigh), (slope, 1, None)):
            for part, size in list(zip(parts, sizes))[first:]:
                steps += [functools.partial(work, *part, at) for at in range(0, size, BLOCK)]
            steps += [end] if end else []
        return steps

    def gradients(chunk):
        if not seen:
            return []
        weight_ref = sets[chunk % 2][2]
        head = chunk // per_head
        last = chunk % per_head == per_head - 1

        def collect(total_ref, buf, left, side, factor):
            total = None
            for start in range(0, JOIN, 2):
                cols = slice(start * rows, (start + 2) * rows)
                part = jnp.dot(left(cols), joined(buf, chunk, start, 2), preferred_element_type=jnp.float32)
                total = part if total is None else total + part
            if chunk % per_head:
                total = total + total_ref[:columns, :]
            if not last:
                total_ref[:columns, :] = total
                return
            cols = slice(side * wide + head * DH, side * wide + (head + 1) * DH)
            for shift in range(seen):
                at = [piece_of(shifts, shift, side) * HALF for side in range(2)]
                own_outs[shift][:, cols] = total[at[0] : at[0] + HALF] * factor
                sent_outs[shift][:, cols] = (total[at[1] : at[1] + HALF] * factor).astype(jnp.bfloat16)

        return [
            functools.partial(collect, dk_buf, q_buf, lambda cols: slopes_out[chunk, :columns, cols], 0, SCALE),
            functools.partial(collect, dv_buf, g_buf, lambda cols: weight_ref[:columns, cols], 1, 1.0),
        ]

    pipeline(chunks, products, softmax, gradients)


def near_gradients_kernel(group, q_buf, g_buf, grown, signal, share, delta, slopes_out, *refs):
    own_outs, sent_outs, sets = refs[:2], refs[2:4], refs[4:]
    rows = q_buf.shape[0]
    wide = own_outs[0].shape[1]
    per_head = group // JOIN
    chunks = wide // DH * per_head
    near = 2 * rows
    totals = {}

    def softmax(chunk):
        weight_ref = sets[chunk % 2]

        def work(at):
            weights, slopes = [], []
            for i in range(at, at + BLOCK, 8):
                probs = grown[chunk, i : i + 8, :] * share[chunk]
                weights.append(probs)
                slopes.append(probs * (signal[chunk, i : i + 8, :] - delta[chunk]))
            weight_ref[at : at + BLOCK, :] = jnp.concatenate(weights, axis=0).astype(jnp.bfloat16)
            slopes_out[chunk, at : at + BLOCK, :] = jnp.concatenate(slopes, axis=0).astype(jnp.bfloat16)

        return [functools.partial(work, at) for at in range(0, near, BLOCK)]

    def gradients(chunk):
        weight_ref = sets[chunk % 2]
        head = chunk // per_head

        def collect(left, buf, side, factor):
            total = totals.pop(side, None)
            for start in range(0, JOIN, 2):
                cols = slice(start * rows, (start + 2) * rows)
                part = jnp.dot(left(cols), joined(buf, chunk, start, 2), preferred_element_type=jnp.float32)
                total = part if total is None else total + part
            if chunk % per_head < per_head - 1:
                totals[side] = total
                return
            own_outs[side][:, head_cols(head)] = total[:rows] * factor
            sent_outs[side][:, head_cols(head)] = (total[rows:] * factor).astype(jnp.bfloat16)

        return [
            functools.partial(collect, lambda cols: slopes_out[chunk, :, cols], q_buf, 0, SCALE),
            functools.partial(collect, lambda cols: weight_ref[:, cols], g_buf, 1, 1.0),
        ]

    pipeline(chunks, lambda chunk: [], softmax, gradients)


def query_gradients_kernel(group, near_slopes, far_slopes, key_hbm, other_key, *refs):
    far, (dq_hbm, own_key, key_buf, turned_buf, dq_buf, in_sem, out_sem) = refs[:-7], refs[-7:]
    rows = dq_buf.shape[0]
    heads = key_buf.shape[0]
    near = 2 * rows
    per_head = group // JOIN
    load = pltpu.make_async_copy(key_hbm, own_key, in_sem)
    load.start()
    at = rows
    for piece in (other_key, *far):
        size = piece.shape[0]
        for head in range(heads):
            key_buf[head, at : at + size, :] = piece[:, head_cols(head)]
        at += size
    load.wait()
    stores = []
    for head in range(heads):
        key_buf[head, :rows, :] = own_key[:, head_cols(head)]
        turned_buf[head] = key_buf[head].T
        for chunk in range(head * per_head, (head + 1) * per_head):
            for start in range(0, JOIN, 2):
                cols = slice(start * rows, (start + 2) * rows)
                turned = jnp.dot(
                    turned_buf[head, :, :near], near_slopes[chunk, :, cols], preferred_element_type=jnp.float32
                ) + jnp.dot(turned_buf[head, :, near:], far_slopes[chunk, :, cols], preferred_element_type=jnp.float32)
                for i in range(2):
                    dq = turned[:, i * rows : (i + 1) * rows].T * SCALE
                    dq_buf[:, head_cols(chunk * JOIN + start + i)] = dq.astype(jnp.bfloat16)
        cols = slice(head * group * DH, (head + 1) * group * DH)
        stores.append(pltpu.make_async_copy(dq_buf.at[:, cols], dq_hbm.at[:, cols], out_sem.at[head]))
        stores[-1].start()
    for store in stores:
        store.wait()


def total_kernel(own_key, own_value, got_key, got_value, *refs):
    terms, (outs, bufs, sem) = refs[:-9], (refs[-9:-5], refs[-5:-1], refs[-1])
    wide = bufs[0].shape[1]
    near = [own[...] + got[...].astype(jnp.float32) for own, got in ((own_key, got_key), (own_value, got_value))]
    beacon = functools.reduce(jnp.add, [x[...].astype(jnp.float32) for x in terms])
    stores = []
    for at, total in enumerate((*near, beacon[:, :wide], beacon[:, wide:])):
        bufs[at][...] = total.astype(jnp.bfloat16)
        stores.append(pltpu.make_async_copy(bufs[at], outs[at], sem.at[at]))
        stores[-1].start()
    for store in stores:
        store.wait()


def in_hbm(x):
    return pltpu.with_memory_space_constraint(x, pltpu.HBM)


def call(kernel, operands, spaces, outs, out_spaces, scratch, limit, products):
    return list(pl.pallas_call(
        kernel,
        out_shape=[jax.ShapeDtypeStruct(*x) for x in outs],
        in_specs=[pl.BlockSpec(memory_space=x) for x in spaces],
        out_specs=[pl.BlockSpec(memory_space=x) for x in out_spaces],
        scratch_shapes=scratch,
        compiler_params=pltpu.CompilerParams(vmem_limit_bytes=limit * 1024 * 1024),
        cost_estimate=pl.CostEstimate(flops=products, bytes_accessed=products // 256, transcendentals=products // 512),
    )(*operands))


def local(queries, keys, values, beacon_keys, beacon_values, grad_out, ratios):
    bf16, f32 = jnp.bfloat16, jnp.float32
    hbm, vmem = pltpu.HBM, pltpu.VMEM
    spans = ratios.shape[0]
    rows, wide = keys.shape
    heads = wide // DH
    group = queries.shape[1] // wide
    chunks = heads * group // JOIN
    width = JOIN * rows
    last = spans - 1
    near, middle, columns = 2 * rows, HALF * (last - 1), SLOTS * last
    swap = [(0, 1), (1, 0)]
    shifts = range(1, spans)
    order = sorted(shifts, key=lambda k: abs(2 * k - spans))
    starts = [*sorted(range(1, last), key=lambda k: abs(2 * k - spans)), last]

    def up(k):
        return [(i, (i + k) % spans) for i in range(spans)]

    left = lax.broadcasted_iota(jnp.int32, (beacon_keys.shape[0], 2 * wide), 1) < wide
    beacons = jnp.where(left, jnp.pad(beacon_keys, ((0, 0), (0, wide))), jnp.pad(beacon_values, ((0, 0), (wide, 0))))
    near_keys, near_values, beacons = lax.optimization_barrier((keys, values, beacons))
    own = {k: lax.ppermute(beacons, "ctx", up(k)) for k in starts}
    other_key, other_value = (lax.ppermute(x, "sub", swap) for x in (near_keys, near_values))

    product = queries.shape[1] * rows * 2

    def stats_of(size):
        return [((chunks, size, width), f32)] * 2 + [((chunks, 8, width), f32)] * 2

    q_in, g_in, far_mask, *near_stats = call(
        functools.partial(near_kernel, last, group),
        [ratios, in_hbm(queries), in_hbm(grad_out), in_hbm(keys), in_hbm(values), other_key, other_value],
        [pltpu.SMEM] + [hbm] * 4 + [vmem] * 2,
        [(queries.shape, bf16)] * 2 + [((columns, DH), bf16)] + stats_of(near),
        [vmem] * 7,
        [vmem(keys.shape, bf16)] * 2
        + [vmem((heads, near, 2 * DH), bf16), vmem((heads, near, DH), bf16)]
        + [pltpu.SemaphoreType.DMA((2 + 2 * heads,))],
        8,
        2 * product * near,
    )
    groups = [near_stats]
    if middle:
        first = starts[0]
        own[first], near_stats[2] = lax.optimization_barrier((own[first], near_stats[2]))
        groups.append(
            call(
                functools.partial(middle_kernel, group),
                [q_in, g_in, far_mask, *[own[k] for k in range(1, last)]],
                [vmem] * (2 + last),
                stats_of(middle),
                [vmem] * 4,
                [vmem((heads, middle, 2 * DH), bf16), vmem((heads, middle, DH), bf16)],
                8,
                product,
            )
        )
        own[last], groups[1][2] = lax.optimization_barrier((own[last], groups[1][2]))
    other = {k: lax.ppermute(own[k], "sub", swap) for k in starts}
    far = [own[k] for k in range(1, last)] + [other[k] for k in range(1, last)] + [own[last], other[last]]
    fresh = columns - middle
    sets = [vmem((fresh, width), f32)] * 2 + [vmem((columns, width), bf16)]
    share, delta, far_slopes, *grads = call(
        functools.partial(far_kernel, last, group),
        [q_in, g_in, far_mask, *[x for stats in groups for x in stats], *far[last - 1 :]],
        [vmem] * (3 + 4 * len(groups) + last + 1),
        [((chunks, 8, width), f32)] * 2
        + [((chunks, columns, width), bf16)]
        + [((HALF, 2 * wide), f32)] * last
        + [((HALF, 2 * wide), bf16)] * last,
        [vmem] * (3 + 2 * last),
        [vmem((heads, fresh, 2 * DH), bf16), vmem((heads, fresh, DH), bf16)]
        + [vmem((columns, DH), f32)] * 2
        + sets * 2,
        12 + 25 * columns * width // 2**20,
        4 * product * columns,
    )
    sent = dict(zip(shifts, grads[last:]))

    def pair(k):
        return (grads[k - 1] + lax.ppermute(sent[k], "sub", swap).astype(f32)).astype(bf16)

    pairs = {k: pair(k) for k in order}
    pairs, delta = lax.optimization_barrier((pairs, delta))
    sums = [lax.ppermute(pairs[k], "ctx", up(-k)) for k in order]
    near_slopes, *near_grads = call(
        functools.partial(near_gradients_kernel, group),
        [q_in, g_in, near_stats[0], near_stats[1], share, delta],
        [vmem] * 6,
        [((chunks, near, width), bf16)] + [(keys.shape, f32)] * 2 + [(keys.shape, bf16)] * 2,
        [vmem] * 5,
        [vmem((near, width), bf16)] * 2,
        8,
        product,
    )
    (grad_queries,) = call(
        functools.partial(query_gradients_kernel, group),
        [near_slopes, far_slopes, in_hbm(keys), other_key, *far],
        [vmem] * 2 + [hbm] + [vmem] * (1 + 2 * last),
        [(queries.shape, bf16)],
        [hbm],
        [
            vmem(keys.shape, bf16),
            vmem((heads, near + columns, DH), bf16),
            vmem((heads, DH, near + columns), bf16),
            vmem(queries.shape, bf16),
            pltpu.SemaphoreType.DMA,
            pltpu.SemaphoreType.DMA((heads,)),
        ],
        12,
        product,
    )
    near_got = [lax.ppermute(x, "sub", swap) for x in near_grads[2:]]
    sums, grad_queries = lax.optimization_barrier((sums, grad_queries))
    out_shapes = [(x.shape, bf16) for x in (keys, values, beacon_keys, beacon_values)]
    outs = call(
        total_kernel,
        [*near_grads[:2], *near_got, *sums],
        [vmem] * (4 + len(sums)),
        out_shapes,
        [hbm] * 4,
        [vmem(*x) for x in out_shapes] + [pltpu.SemaphoreType.DMA((4,))],
        4,
        product,
    )
    return (grad_queries, *outs)


def solution(mesh):
    rows = P(("grp", "ctx", "sub"), "tp")
    return jax.shard_map(
        local,
        mesh=mesh,
        in_specs=(rows,) * 6 + (P("grp"),),
        out_specs=(rows,) * 5,
        check_vma=False,
    )
```

```python
import functools
import math

import jax
import jax.numpy as jnp
from jax import lax
from jax.experimental import pallas as pl
from jax.experimental.pallas import tpu as pltpu
from jax.sharding import PartitionSpec as P

DH = 128
SPAN = 256
SLOTS = SPAN // 2
HALF = SLOTS // 2
NT = (((1,), (1,)), ((), ()))
HIDDEN = -3e38
JOIN = 4
BLOCK = 16
SCALE = DH ** (-0.5)
LOG_SCALE = SCALE * math.log2(math.e)


def interleave(first, second):
    few, many = sorted((first, second), key=len)
    done = 0
    for index, step in enumerate(few):
        step()
        upto = len(many) * (index + 1) // len(few)
        for other in many[done:upto]:
            other()
        done = upto
    for other in many[done:]:
        other()


def pipeline(chunks, products, softmax, gradients):
    for step in products(0):
        step()
    for chunk in range(chunks):
        matrix = gradients(chunk - 1) if chunk > 0 else []
        matrix = matrix + (products(chunk + 1) if chunk + 1 < chunks else [])
        interleave(matrix, softmax(chunk))
    for step in gradients(chunks - 1):
        step()


def head_cols(head):
    return slice(head * DH, (head + 1) * DH)


def joined(buf, chunk, start, count):
    first = chunk * JOIN + start
    return jnp.concatenate([buf[:, head_cols(first + i)] for i in range(count)], axis=0)


def pair_products(key_buf, value_buf, q_buf, g_buf, chunk, head, score_ref, signal_ref):
    rows = q_buf.shape[0]
    at = [lax.broadcasted_iota(jnp.int32, (rows, DH), axis) for axis in range(2)]
    one_hot = jnp.where(at[0] == at[1], 1.0, 0.0).astype(jnp.bfloat16)
    one_hot = jnp.concatenate([one_hot] * 2, axis=0)

    def score(start):
        queries = jnp.concatenate([joined(q_buf, chunk, start, 2), one_hot], axis=1)
        cols = slice(start * rows, (start + 2) * rows)
        score_ref[:, cols] = lax.dot_general(key_buf[head], queries, NT, preferred_element_type=jnp.float32)

    def signal(start):
        cols = slice(start * rows, (start + 2) * rows)
        signal_ref[:, cols] = lax.dot_general(
            value_buf[head], joined(g_buf, chunk, start, 2), NT, preferred_element_type=jnp.float32
        )

    return [functools.partial(f, start) for f in (score, signal) for start in range(0, JOIN, 2)]


def mask_of(seen):
    return jnp.where(seen, 0.0, HIDDEN).astype(jnp.bfloat16)


def place(key_buf, value_buf, at, keys, values, mask):
    size = mask.shape[0]
    for head in range(key_buf.shape[0]):
        key_buf[head, at : at + size, :DH] = keys[:, head_cols(head)]
        key_buf[head, at : at + size, DH:] = mask
        value_buf[head, at : at + size, :] = values[:, head_cols(head)]


def spread(x):
    return jnp.broadcast_to(x, (8, x.shape[1]))


def exponentials(chunk, grown_out, top_out, total_out):
    score_ref = grown_out.at[chunk]
    columns, width = score_ref.shape
    state = {"top": jnp.full((8, width), HIDDEN, jnp.float32)}

    def top(at):
        for i in range(at, at + BLOCK, 8):
            state["top"] = jnp.maximum(state["top"], score_ref[i : i + 8, :])

    def end_top():
        state["top"] = spread(jnp.max(state["top"], axis=0, keepdims=True))
        top_out[chunk] = state["top"]
        state["total"] = jnp.zeros((8, width), jnp.float32)

    def grow(at):
        for i in range(at, at + BLOCK, 8):
            grown = jnp.exp2((score_ref[i : i + 8, :] - state["top"]) * LOG_SCALE)
            score_ref[i : i + 8, :] = grown
            state["total"] = state["total"] + grown

    def end_grow():
        total_out[chunk] = spread(jnp.sum(state["total"], axis=0, keepdims=True))

    blocks = range(0, columns, BLOCK)
    return [functools.partial(top, at) for at in blocks] + [end_top] + [functools.partial(grow, at) for at in blocks] + [end_grow]


def near_kernel(
    shifts, group, ratios, q_hbm, g_hbm, key_hbm, value_hbm, other_key, other_value, q_buf, g_buf, mask_out, grown_out,
    signal_out, top_out, total_out, own_key, own_value, key_buf, value_buf, sem,
):
    rows = q_buf.shape[0]
    heads = key_buf.shape[0]
    per_head = group // JOIN
    sub = lax.axis_index("sub")
    pairs = [(key_hbm, own_key), (value_hbm, own_value)]
    for head in range(heads):
        cols = slice(head * group * DH, (head + 1) * group * DH)
        pairs += [(q_hbm.at[:, cols], q_buf.at[:, cols]), (g_hbm.at[:, cols], g_buf.at[:, cols])]
    loads = [pltpu.make_async_copy(*pair, sem.at[i]) for i, pair in enumerate(pairs)]
    for load in loads:
        load.start()
    key_at = lax.broadcasted_iota(jnp.int32, (rows, DH), 0)
    token_at = lax.broadcasted_iota(jnp.int32, (rows, DH), 1)
    place(key_buf, value_buf, rows, other_key, other_value, mask_of(key_at < sub * rows))
    here = lax.axis_index("ctx")
    slot_at = lax.broadcasted_iota(jnp.int32, (HALF, DH), 0)
    for shift in range(shifts):
        owner = jnp.maximum(here - 1 - shift, 0)
        live = jnp.where(here > shift, SPAN // ratios[owner], 0)
        for side, first in enumerate((sub * HALF, (1 - sub) * HALF)):
            at = (2 * shift + side) * HALF
            mask_out[at : at + HALF, :] = mask_of(slot_at < live - first)
    loads[0].wait()
    loads[1].wait()
    place(key_buf, value_buf, 0, own_key, own_value, mask_of(key_at <= token_at))

    def products(chunk):
        head = chunk // per_head
        if chunk % per_head == 0:
            loads[2 + 2 * head].wait()
            loads[3 + 2 * head].wait()
        return pair_products(
            key_buf, value_buf, q_buf, g_buf, chunk, head, grown_out.at[chunk], signal_out.at[chunk]
        )

    pipeline(
        heads * per_head,
        products,
        lambda chunk: exponentials(chunk, grown_out, top_out, total_out),
        lambda chunk: [],
    )


def place_far(key_buf, value_buf, far, mask):
    wide = far[0].shape[1] // 2
    for index, source in enumerate(far):
        at = index * HALF
        place(key_buf, value_buf, at, source.at[:, :wide], source.at[:, wide:], mask[at : at + HALF, :])


def far_kernel(shifts, group, *refs):
    here = lax.axis_index("ctx")
    levels = sorted({shifts * i // 3 for i in range(4)} | set(range(min(shifts, 4))))
    for low, level in zip([-1, *levels], levels):
        pl.when((here > low) & (here <= level))(functools.partial(far_part, shifts, level, group, *refs))


def far_part(shifts, seen, group, q_buf, g_buf, far_mask, near_grown, near_signal, near_top, near_total, *refs):
    far, refs = refs[: 2 * shifts], refs[2 * shifts :]
    share_out, delta_out, slopes_out, own_outs, sent_outs = refs[0], refs[1], refs[2], refs[3 : 3 + shifts], refs[3 + shifts : 3 + 2 * shifts]
    refs = refs[3 + 2 * shifts :]
    (key_buf, value_buf, dk_buf, dv_buf), sets = refs[:4], (refs[4:7], refs[7:10])
    rows = q_buf.shape[0]
    heads = key_buf.shape[0]
    columns = seen * SLOTS
    wide = heads * DH
    per_head = group // JOIN
    chunks = heads * per_head
    width = JOIN * rows
    if seen:
        place_far(key_buf, value_buf, far[: 2 * seen], far_mask)
    for out in (*own_outs[seen:], *sent_outs[seen:]):
        out[...] = jnp.zeros_like(out)
    key_buf, value_buf = key_buf.at[:, :columns, :], value_buf.at[:, :columns, :]
    sets = [[ref.at[:columns, :] for ref in refs] for refs in sets]

    def products(chunk):
        if not seen:
            return []
        score_ref, signal_ref, _ = sets[chunk % 2]
        return pair_products(key_buf, value_buf, q_buf, g_buf, chunk, chunk // per_head, score_ref, signal_ref)

    def softmax(chunk):
        score_ref, signal_ref, weight_ref = sets[chunk % 2]
        slope_ref = slopes_out.at[chunk]
        state = {"top": near_top[chunk]}

        def top(at):
            for i in range(at, at + BLOCK, 8):
                state["top"] = jnp.maximum(state["top"], score_ref[i : i + 8, :])

        def end_top():
            state["top"] = spread(jnp.max(state["top"], axis=0, keepdims=True))
            state["total"] = jnp.zeros((8, width), jnp.float32)

        def grow(at):
            for i in range(at, at + BLOCK, 8):
                grown = jnp.exp2((score_ref[i : i + 8, :] - state["top"]) * LOG_SCALE)
                score_ref[i : i + 8, :] = grown
                state["total"] = state["total"] + grown

        def end_grow():
            total = spread(jnp.sum(state["total"], axis=0, keepdims=True))
            shrink = jnp.exp2((near_top[chunk] - state["top"]) * LOG_SCALE)
            state["far"] = 1.0 / (near_total[chunk] * shrink + total)
            state["near"] = shrink * state["far"]
            share_out[chunk] = state["near"]
            state["delta"] = jnp.zeros((8, width), jnp.float32)

        def weigh(grown, signal, share, at):
            probs = [grown[i : i + 8, :] * state[share] for i in range(at, at + BLOCK, 8)]
            weights = jnp.concatenate(probs, axis=0).astype(jnp.bfloat16)
            if share == "far":
                weight_ref[at : at + BLOCK, :] = weights
            terms = weights.astype(jnp.float32) * signal[at : at + BLOCK, :]
            for i in range(0, BLOCK, 8):
                state["delta"] = state["delta"] + terms[i : i + 8]

        def end_weigh():
            state["delta"] = spread(jnp.sum(state["delta"], axis=0, keepdims=True))
            delta_out[chunk] = state["delta"]

        def slope(at):
            slopes = []
            for i in range(at, at + BLOCK, 8):
                probs = score_ref[i : i + 8, :] * state["far"]
                slopes.append(probs * (signal_ref[i : i + 8, :] - state["delta"]))
            slope_ref[at : at + BLOCK, :] = jnp.concatenate(slopes, axis=0).astype(jnp.bfloat16)

        grown, signal = near_grown.at[chunk], near_signal.at[chunk]
        blocks = range(0, columns, BLOCK)

        def clear():
            if seen < shifts:
                slope_ref[columns:, :] = jnp.zeros((SLOTS * (shifts - seen), width), jnp.bfloat16)

        steps = [clear] + [functools.partial(top, at) for at in blocks] + [end_top]
        steps += [functools.partial(grow, at) for at in blocks] + [end_grow]
        steps += [functools.partial(weigh, score_ref, signal_ref, "far", at) for at in blocks]
        steps += [functools.partial(weigh, grown, signal, "near", at) for at in range(0, 2 * rows, BLOCK)] + [end_weigh]
        return steps + [functools.partial(slope, at) for at in blocks]

    def gradients(chunk):
        if not seen:
            return []
        weight_ref = sets[chunk % 2][2]
        head = chunk // per_head
        last = chunk % per_head == per_head - 1

        def collect(total_ref, buf, left, side, factor):
            total = None
            for start in range(0, JOIN, 2):
                cols = slice(start * rows, (start + 2) * rows)
                part = jnp.dot(left(cols), joined(buf, chunk, start, 2), preferred_element_type=jnp.float32)
                total = part if total is None else total + part
            if chunk % per_head:
                total = total + total_ref[:columns, :]
            if not last:
                total_ref[:columns, :] = total
                return
            cols = slice(side * wide + head * DH, side * wide + (head + 1) * DH)
            for shift in range(seen):
                at = shift * SLOTS
                own_outs[shift][:, cols] = total[at : at + HALF] * factor
                sent_outs[shift][:, cols] = (total[at + HALF : at + SLOTS] * factor).astype(jnp.bfloat16)

        return [
            functools.partial(collect, dk_buf, q_buf, lambda cols: slopes_out[chunk, :columns, cols], 0, SCALE),
            functools.partial(collect, dv_buf, g_buf, lambda cols: weight_ref[:, cols], 1, 1.0),
        ]

    pipeline(chunks, products, softmax, gradients)


def near_gradients_kernel(group, q_buf, g_buf, grown, signal, share, delta, slopes_out, *refs):
    own_outs, sent_outs, sets = refs[:2], refs[2:4], refs[4:]
    rows = q_buf.shape[0]
    wide = own_outs[0].shape[1]
    per_head = group // JOIN
    chunks = wide // DH * per_head
    near = 2 * rows
    totals = {}

    def softmax(chunk):
        weight_ref = sets[chunk % 2]

        def work(at):
            weights, slopes = [], []
            for i in range(at, at + BLOCK, 8):
                probs = grown[chunk, i : i + 8, :] * share[chunk]
                weights.append(probs)
                slopes.append(probs * (signal[chunk, i : i + 8, :] - delta[chunk]))
            weight_ref[at : at + BLOCK, :] = jnp.concatenate(weights, axis=0).astype(jnp.bfloat16)
            slopes_out[chunk, at : at + BLOCK, :] = jnp.concatenate(slopes, axis=0).astype(jnp.bfloat16)

        return [functools.partial(work, at) for at in range(0, near, BLOCK)]

    def gradients(chunk):
        weight_ref = sets[chunk % 2]
        head = chunk // per_head

        def collect(left, buf, side, factor):
            total = totals.pop(side, None)
            for start in range(0, JOIN, 2):
                cols = slice(start * rows, (start + 2) * rows)
                part = jnp.dot(left(cols), joined(buf, chunk, start, 2), preferred_element_type=jnp.float32)
                total = part if total is None else total + part
            if chunk % per_head < per_head - 1:
                totals[side] = total
                return
            own_outs[side][:, head_cols(head)] = total[:rows] * factor
            sent_outs[side][:, head_cols(head)] = (total[rows:] * factor).astype(jnp.bfloat16)

        return [
            functools.partial(collect, lambda cols: slopes_out[chunk, :, cols], q_buf, 0, SCALE),
            functools.partial(collect, lambda cols: weight_ref[:, cols], g_buf, 1, 1.0),
        ]

    pipeline(chunks, lambda chunk: [], softmax, gradients)


def query_gradients_kernel(group, near_slopes, far_slopes, key_hbm, other_key, *refs):
    far, (dq_hbm, own_key, key_buf, turned_buf, dq_buf, in_sem, out_sem) = refs[:-7], refs[-7:]
    rows = dq_buf.shape[0]
    heads = key_buf.shape[0]
    near = 2 * rows
    per_head = group // JOIN
    load = pltpu.make_async_copy(key_hbm, own_key, in_sem)
    load.start()
    at = rows
    for piece in (other_key, *far):
        size = piece.shape[0]
        for head in range(heads):
            key_buf[head, at : at + size, :] = piece[:, head_cols(head)]
        at += size
    load.wait()
    stores = []
    for head in range(heads):
        key_buf[head, :rows, :] = own_key[:, head_cols(head)]
        turned_buf[head] = key_buf[head].T
        for chunk in range(head * per_head, (head + 1) * per_head):
            for start in range(0, JOIN, 2):
                cols = slice(start * rows, (start + 2) * rows)
                turned = jnp.dot(
                    turned_buf[head, :, :near], near_slopes[chunk, :, cols], preferred_element_type=jnp.float32
                ) + jnp.dot(turned_buf[head, :, near:], far_slopes[chunk, :, cols], preferred_element_type=jnp.float32)
                for i in range(2):
                    dq = turned[:, i * rows : (i + 1) * rows].T * SCALE
                    dq_buf[:, head_cols(chunk * JOIN + start + i)] = dq.astype(jnp.bfloat16)
        cols = slice(head * group * DH, (head + 1) * group * DH)
        stores.append(pltpu.make_async_copy(dq_buf.at[:, cols], dq_hbm.at[:, cols], out_sem.at[head]))
        stores[-1].start()
    for store in stores:
        store.wait()


def total_kernel(own_key, own_value, got_key, got_value, *refs):
    terms, (outs, bufs, sem) = refs[:-9], (refs[-9:-5], refs[-5:-1], refs[-1])
    wide = bufs[0].shape[1]
    near = [own[...] + got[...].astype(jnp.float32) for own, got in ((own_key, got_key), (own_value, got_value))]
    beacon = functools.reduce(jnp.add, [x[...].astype(jnp.float32) for x in terms])
    stores = []
    for at, total in enumerate((*near, beacon[:, :wide], beacon[:, wide:])):
        bufs[at][...] = total.astype(jnp.bfloat16)
        stores.append(pltpu.make_async_copy(bufs[at], outs[at], sem.at[at]))
        stores[-1].start()
    for store in stores:
        store.wait()


def in_hbm(x):
    return pltpu.with_memory_space_constraint(x, pltpu.HBM)


def call(kernel, operands, spaces, outs, out_spaces, scratch, limit, products):
    return list(pl.pallas_call(
        kernel,
        out_shape=[jax.ShapeDtypeStruct(*x) for x in outs],
        in_specs=[pl.BlockSpec(memory_space=x) for x in spaces],
        out_specs=[pl.BlockSpec(memory_space=x) for x in out_spaces],
        scratch_shapes=scratch,
        compiler_params=pltpu.CompilerParams(vmem_limit_bytes=limit * 1024 * 1024),
        cost_estimate=pl.CostEstimate(flops=products, bytes_accessed=products // 256, transcendentals=products // 512),
    )(*operands))


def local(queries, keys, values, beacon_keys, beacon_values, grad_out, ratios):
    bf16, f32 = jnp.bfloat16, jnp.float32
    hbm, vmem = pltpu.HBM, pltpu.VMEM
    spans = ratios.shape[0]
    rows, wide = keys.shape
    heads = wide // DH
    group = queries.shape[1] // wide
    chunks = heads * group // JOIN
    width = JOIN * rows
    last = spans - 1
    near, columns = 2 * rows, SLOTS * last
    swap = [(0, 1), (1, 0)]
    shifts = range(1, spans)
    order = sorted(shifts, key=lambda k: abs(2 * k - spans))

    def up(k):
        return [(i, (i + k) % spans) for i in range(spans)]

    left = lax.broadcasted_iota(jnp.int32, (beacon_keys.shape[0], 2 * wide), 1) < wide
    beacons = jnp.where(left, jnp.pad(beacon_keys, ((0, 0), (0, wide))), jnp.pad(beacon_values, ((0, 0), (wide, 0))))
    near_keys, near_values, beacons = lax.optimization_barrier((keys, values, beacons))
    own = {k: lax.ppermute(beacons, "ctx", up(k)) for k in reversed(order)}
    other_key, other_value = (lax.ppermute(x, "sub", swap) for x in (near_keys, near_values))

    product = queries.shape[1] * rows * 2

    def stats_of(size):
        return [((chunks, size, width), f32)] * 2 + [((chunks, 8, width), f32)] * 2

    q_in, g_in, far_mask, *near_stats = call(
        functools.partial(near_kernel, last, group),
        [ratios, in_hbm(queries), in_hbm(grad_out), in_hbm(keys), in_hbm(values), other_key, other_value],
        [pltpu.SMEM] + [hbm] * 4 + [vmem] * 2,
        [(queries.shape, bf16)] * 2 + [((columns, DH), bf16)] + stats_of(near),
        [vmem] * 7,
        [vmem(keys.shape, bf16)] * 2
        + [vmem((heads, near, 2 * DH), bf16), vmem((heads, near, DH), bf16)]
        + [pltpu.SemaphoreType.DMA((2 + 2 * heads,))],
        8,
        2 * product * near,
    )
    first = order[0]
    own[first], near_stats[2] = lax.optimization_barrier((own[first], near_stats[2]))
    other = {first: lax.ppermute(own[first], "sub", swap)}
    own, other = lax.optimization_barrier((own, other))
    for k in order[1:]:
        other[k] = lax.ppermute(own[k], "sub", swap)
    far = [x[k] for k in shifts for x in (own, other)]
    sets = [vmem((columns, width), f32)] * 2 + [vmem((columns, width), bf16)]
    share, delta, far_slopes, *grads = call(
        functools.partial(far_kernel, last, group),
        [q_in, g_in, far_mask, *near_stats, *far],
        [vmem] * (7 + len(far)),
        [((chunks, 8, width), f32)] * 2
        + [((chunks, columns, width), bf16)]
        + [((HALF, 2 * wide), f32)] * last
        + [((HALF, 2 * wide), bf16)] * last,
        [vmem] * (3 + 2 * last),
        [vmem((heads, columns, 2 * DH), bf16), vmem((heads, columns, DH), bf16)]
        + [vmem((columns, DH), f32)] * 2
        + sets * 2,
        12 + 30 * columns * width // 2**20,
        4 * product * columns,
    )
    sent = dict(zip(shifts, grads[last:]))

    def pair(k):
        return (grads[k - 1] + lax.ppermute(sent[k], "sub", swap).astype(f32)).astype(bf16)

    pairs = {k: pair(k) for k in order}
    pairs, delta = lax.optimization_barrier((pairs, delta))
    sums = [lax.ppermute(pairs[k], "ctx", up(-k)) for k in order]
    near_slopes, *near_grads = call(
        functools.partial(near_gradients_kernel, group),
        [q_in, g_in, near_stats[0], near_stats[1], share, delta],
        [vmem] * 6,
        [((chunks, near, width), bf16)] + [(keys.shape, f32)] * 2 + [(keys.shape, bf16)] * 2,
        [vmem] * 5,
        [vmem((near, width), bf16)] * 2,
        8,
        product,
    )
    (grad_queries,) = call(
        functools.partial(query_gradients_kernel, group),
        [near_slopes, far_slopes, in_hbm(keys), other_key, *far],
        [vmem] * 2 + [hbm] + [vmem] * (1 + 2 * last),
        [(queries.shape, bf16)],
        [hbm],
        [
            vmem(keys.shape, bf16),
            vmem((heads, near + columns, DH), bf16),
            vmem((heads, DH, near + columns), bf16),
            vmem(queries.shape, bf16),
            pltpu.SemaphoreType.DMA,
            pltpu.SemaphoreType.DMA((heads,)),
        ],
        12,
        product,
    )
    near_got = [lax.ppermute(x, "sub", swap) for x in near_grads[2:]]
    sums, grad_queries = lax.optimization_barrier((sums, grad_queries))
    out_shapes = [(x.shape, bf16) for x in (keys, values, beacon_keys, beacon_values)]
    outs = call(
        total_kernel,
        [*near_grads[:2], *near_got, *sums],
        [vmem] * (4 + len(sums)),
        out_shapes,
        [hbm] * 4,
        [vmem(*x) for x in out_shapes] + [pltpu.SemaphoreType.DMA((4,))],
        4,
        product,
    )
    return (grad_queries, *outs)


def solution(mesh):
    rows = P(("grp", "ctx", "sub"), "tp")
    return jax.shard_map(
        local,
        mesh=mesh,
        in_specs=(rows,) * 6 + (P("grp"),),
        out_specs=(rows,) * 5,
        check_vma=False,
    )
```

```python
import functools
import math

import jax
import jax.numpy as jnp
from jax import lax
from jax.experimental import pallas as pl
from jax.experimental.pallas import tpu as pltpu
from jax.sharding import PartitionSpec as P

DH = 128
SPAN = 256
SLOTS = SPAN // 2
HALF = SLOTS // 2
NT = (((1,), (1,)), ((), ()))
HIDDEN = -3e38
JOIN = 4
BLOCK = 16
SCALE = DH ** (-0.5)
LOG_SCALE = SCALE * math.log2(math.e)


def interleave(first, second):
    few, many = sorted((first, second), key=len)
    done = 0
    for index, step in enumerate(few):
        step()
        upto = len(many) * (index + 1) // len(few)
        for other in many[done:upto]:
            other()
        done = upto
    for other in many[done:]:
        other()


def pipeline(chunks, products, softmax, gradients):
    for step in products(0):
        step()
    for chunk in range(chunks):
        matrix = gradients(chunk - 1) if chunk > 0 else []
        matrix = matrix + (products(chunk + 1) if chunk + 1 < chunks else [])
        interleave(matrix, softmax(chunk))
    for step in gradients(chunks - 1):
        step()


def head_cols(head):
    return slice(head * DH, (head + 1) * DH)


def joined(buf, chunk, start, count):
    first = chunk * JOIN + start
    return jnp.concatenate([buf[:, head_cols(first + i)] for i in range(count)], axis=0)


def pair_products(key_buf, value_buf, q_buf, g_buf, chunk, head, score_ref, signal_ref):
    rows = q_buf.shape[0]
    at = [lax.broadcasted_iota(jnp.int32, (rows, DH), axis) for axis in range(2)]
    one_hot = jnp.where(at[0] == at[1], 1.0, 0.0).astype(jnp.bfloat16)
    one_hot = jnp.concatenate([one_hot] * 2, axis=0)

    def score(start):
        queries = jnp.concatenate([joined(q_buf, chunk, start, 2), one_hot], axis=1)
        cols = slice(start * rows, (start + 2) * rows)
        score_ref[:, cols] = lax.dot_general(key_buf[head], queries, NT, preferred_element_type=jnp.float32)

    def signal(start):
        cols = slice(start * rows, (start + 2) * rows)
        signal_ref[:, cols] = lax.dot_general(
            value_buf[head], joined(g_buf, chunk, start, 2), NT, preferred_element_type=jnp.float32
        )

    return [functools.partial(f, start) for f in (score, signal) for start in range(0, JOIN, 2)]


def mask_of(seen):
    return jnp.where(seen, 0.0, HIDDEN).astype(jnp.bfloat16)


def place(key_buf, value_buf, at, keys, values, mask):
    size = mask.shape[0]
    for head in range(key_buf.shape[0]):
        key_buf[head, at : at + size, :DH] = keys[:, head_cols(head)]
        key_buf[head, at : at + size, DH:] = mask
        value_buf[head, at : at + size, :] = values[:, head_cols(head)]


def spread(x):
    return jnp.broadcast_to(x, (8, x.shape[1]))


def exponentials(chunk, grown_out, top_out, total_out):
    score_ref = grown_out.at[chunk]
    columns, width = score_ref.shape
    state = {"top": jnp.full((8, width), HIDDEN, jnp.float32)}

    def top(at):
        for i in range(at, at + BLOCK, 8):
            state["top"] = jnp.maximum(state["top"], score_ref[i : i + 8, :])

    def end_top():
        state["top"] = spread(jnp.max(state["top"], axis=0, keepdims=True))
        top_out[chunk] = state["top"]
        state["total"] = jnp.zeros((8, width), jnp.float32)

    def grow(at):
        for i in range(at, at + BLOCK, 8):
            grown = jnp.exp2((score_ref[i : i + 8, :] - state["top"]) * LOG_SCALE)
            score_ref[i : i + 8, :] = grown
            state["total"] = state["total"] + grown

    def end_grow():
        total_out[chunk] = spread(jnp.sum(state["total"], axis=0, keepdims=True))

    blocks = range(0, columns, BLOCK)
    return [functools.partial(top, at) for at in blocks] + [end_top] + [functools.partial(grow, at) for at in blocks] + [end_grow]


def near_kernel(
    shifts, group, ratios, q_hbm, g_hbm, key_hbm, value_hbm, other_key, other_value, q_buf, g_buf, mask_out, grown_out,
    signal_out, top_out, total_out, own_key, own_value, key_buf, value_buf, sem,
):
    rows = q_buf.shape[0]
    heads = key_buf.shape[0]
    per_head = group // JOIN
    sub = lax.axis_index("sub")
    pairs = [(key_hbm, own_key), (value_hbm, own_value)]
    for head in range(heads):
        cols = slice(head * group * DH, (head + 1) * group * DH)
        pairs += [(q_hbm.at[:, cols], q_buf.at[:, cols]), (g_hbm.at[:, cols], g_buf.at[:, cols])]
    loads = [pltpu.make_async_copy(*pair, sem.at[i]) for i, pair in enumerate(pairs)]
    for load in loads:
        load.start()
    key_at = lax.broadcasted_iota(jnp.int32, (rows, DH), 0)
    token_at = lax.broadcasted_iota(jnp.int32, (rows, DH), 1)
    place(key_buf, value_buf, rows, other_key, other_value, mask_of(key_at < sub * rows))
    here = lax.axis_index("ctx")
    slot_at = lax.broadcasted_iota(jnp.int32, (HALF, DH), 0)
    for shift in range(shifts):
        owner = jnp.maximum(here - 1 - shift, 0)
        live = jnp.where(here > shift, SPAN // ratios[owner], 0)
        for side, first in enumerate((sub * HALF, (1 - sub) * HALF)):
            at = (2 * shift + side) * HALF
            mask_out[at : at + HALF, :] = mask_of(slot_at < live - first)
    loads[0].wait()
    loads[1].wait()
    place(key_buf, value_buf, 0, own_key, own_value, mask_of(key_at <= token_at))

    def products(chunk):
        head = chunk // per_head
        if chunk % per_head == 0:
            loads[2 + 2 * head].wait()
            loads[3 + 2 * head].wait()
        return pair_products(
            key_buf, value_buf, q_buf, g_buf, chunk, head, grown_out.at[chunk], signal_out.at[chunk]
        )

    pipeline(
        heads * per_head,
        products,
        lambda chunk: exponentials(chunk, grown_out, top_out, total_out),
        lambda chunk: [],
    )


def place_far(key_buf, value_buf, far, mask):
    wide = far[0].shape[1] // 2
    for index, source in enumerate(far):
        at = index * HALF
        place(key_buf, value_buf, at, source.at[:, :wide], source.at[:, wide:], mask[at : at + HALF, :])


def far_kernel(shifts, group, *refs):
    here = lax.axis_index("ctx")
    levels = sorted({shifts * i // 3 for i in range(4)} | set(range(min(shifts, 4))))
    for low, level in zip([-1, *levels], levels):
        pl.when((here > low) & (here <= level))(functools.partial(far_part, shifts, level, group, *refs))


def far_part(shifts, seen, group, q_buf, g_buf, far_mask, near_grown, near_signal, near_top, near_total, *refs):
    far, refs = refs[: 2 * shifts], refs[2 * shifts :]
    share_out, delta_out, slopes_out, own_outs, sent_outs = refs[0], refs[1], refs[2], refs[3 : 3 + shifts], refs[3 + shifts : 3 + 2 * shifts]
    refs = refs[3 + 2 * shifts :]
    (key_buf, value_buf, dk_buf, dv_buf), sets = refs[:4], (refs[4:7], refs[7:10])
    rows = q_buf.shape[0]
    heads = key_buf.shape[0]
    columns = seen * SLOTS
    wide = heads * DH
    per_head = group // JOIN
    chunks = heads * per_head
    width = JOIN * rows
    if seen:
        place_far(key_buf, value_buf, far[: 2 * seen], far_mask)
    for out in (*own_outs[seen:], *sent_outs[seen:]):
        out[...] = jnp.zeros_like(out)
    key_buf, value_buf = key_buf.at[:, :columns, :], value_buf.at[:, :columns, :]
    sets = [[ref.at[:columns, :] for ref in refs] for refs in sets]

    def products(chunk):
        if not seen:
            return []
        score_ref, signal_ref, _ = sets[chunk % 2]
        return pair_products(key_buf, value_buf, q_buf, g_buf, chunk, chunk // per_head, score_ref, signal_ref)

    def softmax(chunk):
        score_ref, signal_ref, weight_ref = sets[chunk % 2]
        slope_ref = slopes_out.at[chunk]
        state = {"top": near_top[chunk]}

        def top(at):
            for i in range(at, at + BLOCK, 8):
                state["top"] = jnp.maximum(state["top"], score_ref[i : i + 8, :])

        def end_top():
            state["top"] = spread(jnp.max(state["top"], axis=0, keepdims=True))
            state["total"] = jnp.zeros((8, width), jnp.float32)

        def grow(at):
            for i in range(at, at + BLOCK, 8):
                grown = jnp.exp2((score_ref[i : i + 8, :] - state["top"]) * LOG_SCALE)
                score_ref[i : i + 8, :] = grown
                state["total"] = state["total"] + grown

        def end_grow():
            total = spread(jnp.sum(state["total"], axis=0, keepdims=True))
            shrink = jnp.exp2((near_top[chunk] - state["top"]) * LOG_SCALE)
            state["far"] = 1.0 / (near_total[chunk] * shrink + total)
            state["near"] = shrink * state["far"]
            share_out[chunk] = state["near"]
            state["delta"] = jnp.zeros((8, width), jnp.float32)

        def weigh(grown, signal, share, at):
            probs = [grown[i : i + 8, :] * state[share] for i in range(at, at + BLOCK, 8)]
            weights = jnp.concatenate(probs, axis=0).astype(jnp.bfloat16)
            if share == "far":
                weight_ref[at : at + BLOCK, :] = weights
            terms = weights.astype(jnp.float32) * signal[at : at + BLOCK, :]
            for i in range(0, BLOCK, 8):
                state["delta"] = state["delta"] + terms[i : i + 8]

        def end_weigh():
            state["delta"] = spread(jnp.sum(state["delta"], axis=0, keepdims=True))
            delta_out[chunk] = state["delta"]

        def slope(at):
            slopes = []
            for i in range(at, at + BLOCK, 8):
                probs = score_ref[i : i + 8, :] * state["far"]
                slopes.append(probs * (signal_ref[i : i + 8, :] - state["delta"]))
            slope_ref[at : at + BLOCK, :] = jnp.concatenate(slopes, axis=0).astype(jnp.bfloat16)

        grown, signal = near_grown.at[chunk], near_signal.at[chunk]
        blocks = range(0, columns, BLOCK)

        def clear():
            if seen < shifts:
                slope_ref[columns:, :] = jnp.zeros((SLOTS * (shifts - seen), width), jnp.bfloat16)

        steps = [clear] + [functools.partial(top, at) for at in blocks] + [end_top]
        steps += [functools.partial(grow, at) for at in blocks] + [end_grow]
        steps += [functools.partial(weigh, score_ref, signal_ref, "far", at) for at in blocks]
        steps += [functools.partial(weigh, grown, signal, "near", at) for at in range(0, 2 * rows, BLOCK)] + [end_weigh]
        return steps + [functools.partial(slope, at) for at in blocks]

    def gradients(chunk):
        if not seen:
            return []
        weight_ref = sets[chunk % 2][2]
        head = chunk // per_head
        last = chunk % per_head == per_head - 1

        def collect(total_ref, buf, left, side, factor):
            total = None
            for start in range(0, JOIN, 2):
                cols = slice(start * rows, (start + 2) * rows)
                part = jnp.dot(left(cols), joined(buf, chunk, start, 2), preferred_element_type=jnp.float32)
                total = part if total is None else total + part
            if chunk % per_head:
                total = total + total_ref[:columns, :]
            if not last:
                total_ref[:columns, :] = total
                return
            cols = slice(side * wide + head * DH, side * wide + (head + 1) * DH)
            for shift in range(seen):
                at = shift * SLOTS
                own_outs[shift][:, cols] = total[at : at + HALF] * factor
                sent_outs[shift][:, cols] = (total[at + HALF : at + SLOTS] * factor).astype(jnp.bfloat16)

        return [
            functools.partial(collect, dk_buf, q_buf, lambda cols: slopes_out[chunk, :columns, cols], 0, SCALE),
            functools.partial(collect, dv_buf, g_buf, lambda cols: weight_ref[:, cols], 1, 1.0),
        ]

    pipeline(chunks, products, softmax, gradients)


def near_gradients_kernel(group, q_buf, g_buf, grown, signal, share, delta, slopes_out, *refs):
    own_outs, sent_outs, sets = refs[:2], refs[2:4], refs[4:]
    rows = q_buf.shape[0]
    wide = own_outs[0].shape[1]
    per_head = group // JOIN
    chunks = wide // DH * per_head
    near = 2 * rows
    totals = {}

    def softmax(chunk):
        weight_ref = sets[chunk % 2]

        def work(at):
            weights, slopes = [], []
            for i in range(at, at + BLOCK, 8):
                probs = grown[chunk, i : i + 8, :] * share[chunk]
                weights.append(probs)
                slopes.append(probs * (signal[chunk, i : i + 8, :] - delta[chunk]))
            weight_ref[at : at + BLOCK, :] = jnp.concatenate(weights, axis=0).astype(jnp.bfloat16)
            slopes_out[chunk, at : at + BLOCK, :] = jnp.concatenate(slopes, axis=0).astype(jnp.bfloat16)

        return [functools.partial(work, at) for at in range(0, near, BLOCK)]

    def gradients(chunk):
        weight_ref = sets[chunk % 2]
        head = chunk // per_head

        def collect(left, buf, side, factor):
            total = totals.pop(side, None)
            for start in range(0, JOIN, 2):
                cols = slice(start * rows, (start + 2) * rows)
                part = jnp.dot(left(cols), joined(buf, chunk, start, 2), preferred_element_type=jnp.float32)
                total = part if total is None else total + part
            if chunk % per_head < per_head - 1:
                totals[side] = total
                return
            own_outs[side][:, head_cols(head)] = total[:rows] * factor
            sent_outs[side][:, head_cols(head)] = (total[rows:] * factor).astype(jnp.bfloat16)

        return [
            functools.partial(collect, lambda cols: slopes_out[chunk, :, cols], q_buf, 0, SCALE),
            functools.partial(collect, lambda cols: weight_ref[:, cols], g_buf, 1, 1.0),
        ]

    pipeline(chunks, lambda chunk: [], softmax, gradients)


def query_gradients_kernel(group, near_slopes, far_slopes, key_hbm, other_key, *refs):
    far, (dq_hbm, own_key, key_buf, turned_buf, dq_buf, in_sem, out_sem) = refs[:-7], refs[-7:]
    rows = dq_buf.shape[0]
    heads = key_buf.shape[0]
    near = 2 * rows
    per_head = group // JOIN
    load = pltpu.make_async_copy(key_hbm, own_key, in_sem)
    load.start()
    at = rows
    for piece in (other_key, *far):
        size = piece.shape[0]
        for head in range(heads):
            key_buf[head, at : at + size, :] = piece[:, head_cols(head)]
        at += size
    load.wait()
    stores = []
    for head in range(heads):
        key_buf[head, :rows, :] = own_key[:, head_cols(head)]
        turned_buf[head] = key_buf[head].T
        for chunk in range(head * per_head, (head + 1) * per_head):
            for start in range(0, JOIN, 2):
                cols = slice(start * rows, (start + 2) * rows)
                turned = jnp.dot(
                    turned_buf[head, :, :near], near_slopes[chunk, :, cols], preferred_element_type=jnp.float32
                ) + jnp.dot(turned_buf[head, :, near:], far_slopes[chunk, :, cols], preferred_element_type=jnp.float32)
                for i in range(2):
                    dq = turned[:, i * rows : (i + 1) * rows].T * SCALE
                    dq_buf[:, head_cols(chunk * JOIN + start + i)] = dq.astype(jnp.bfloat16)
        cols = slice(head * group * DH, (head + 1) * group * DH)
        stores.append(pltpu.make_async_copy(dq_buf.at[:, cols], dq_hbm.at[:, cols], out_sem.at[head]))
        stores[-1].start()
    for store in stores:
        store.wait()


def total_kernel(own_key, own_value, got_key, got_value, *refs):
    terms, (outs, bufs, sem) = refs[:-9], (refs[-9:-5], refs[-5:-1], refs[-1])
    wide = bufs[0].shape[1]
    near = [own[...] + got[...].astype(jnp.float32) for own, got in ((own_key, got_key), (own_value, got_value))]
    beacon = functools.reduce(jnp.add, [x[...].astype(jnp.float32) for x in terms])
    stores = []
    for at, total in enumerate((*near, beacon[:, :wide], beacon[:, wide:])):
        bufs[at][...] = total.astype(jnp.bfloat16)
        stores.append(pltpu.make_async_copy(bufs[at], outs[at], sem.at[at]))
        stores[-1].start()
    for store in stores:
        store.wait()


def in_hbm(x):
    return pltpu.with_memory_space_constraint(x, pltpu.HBM)


def call(kernel, operands, spaces, outs, out_spaces, scratch, limit, products):
    return list(pl.pallas_call(
        kernel,
        out_shape=[jax.ShapeDtypeStruct(*x) for x in outs],
        in_specs=[pl.BlockSpec(memory_space=x) for x in spaces],
        out_specs=[pl.BlockSpec(memory_space=x) for x in out_spaces],
        scratch_shapes=scratch,
        compiler_params=pltpu.CompilerParams(vmem_limit_bytes=limit * 1024 * 1024),
        cost_estimate=pl.CostEstimate(flops=products, bytes_accessed=products // 256, transcendentals=products // 512),
    )(*operands))


def local(queries, keys, values, beacon_keys, beacon_values, grad_out, ratios):
    bf16, f32 = jnp.bfloat16, jnp.float32
    hbm, vmem = pltpu.HBM, pltpu.VMEM
    spans = ratios.shape[0]
    rows, wide = keys.shape
    heads = wide // DH
    group = queries.shape[1] // wide
    chunks = heads * group // JOIN
    width = JOIN * rows
    last = spans - 1
    near, columns = 2 * rows, SLOTS * last
    swap = [(0, 1), (1, 0)]
    shifts = range(1, spans)
    order = sorted(shifts, key=lambda k: abs(2 * k - spans))

    def up(k):
        return [(i, (i + k) % spans) for i in range(spans)]

    left = lax.broadcasted_iota(jnp.int32, (beacon_keys.shape[0], 2 * wide), 1) < wide
    beacons = jnp.where(left, jnp.pad(beacon_keys, ((0, 0), (0, wide))), jnp.pad(beacon_values, ((0, 0), (wide, 0))))
    near_keys, near_values, beacons = lax.optimization_barrier((keys, values, beacons))
    own = {k: lax.ppermute(beacons, "ctx", up(k)) for k in reversed(order)}
    other_key, other_value = (lax.ppermute(x, "sub", swap) for x in (near_keys, near_values))

    product = queries.shape[1] * rows * 2

    def stats_of(size):
        return [((chunks, size, width), f32)] * 2 + [((chunks, 8, width), f32)] * 2

    q_in, g_in, far_mask, *near_stats = call(
        functools.partial(near_kernel, last, group),
        [ratios, in_hbm(queries), in_hbm(grad_out), in_hbm(keys), in_hbm(values), other_key, other_value],
        [pltpu.SMEM] + [hbm] * 4 + [vmem] * 2,
        [(queries.shape, bf16)] * 2 + [((columns, DH), bf16)] + stats_of(near),
        [vmem] * 7,
        [vmem(keys.shape, bf16)] * 2
        + [vmem((heads, near, 2 * DH), bf16), vmem((heads, near, DH), bf16)]
        + [pltpu.SemaphoreType.DMA((2 + 2 * heads,))],
        8,
        2 * product * near,
    )
    first = order[0]
    own[first], near_stats[2] = lax.optimization_barrier((own[first], near_stats[2]))
    other = {k: lax.ppermute(own[k], "sub", swap) for k in order}
    far = [x[k] for k in shifts for x in (own, other)]
    sets = [vmem((columns, width), f32)] * 2 + [vmem((columns, width), bf16)]
    share, delta, far_slopes, *grads = call(
        functools.partial(far_kernel, last, group),
        [q_in, g_in, far_mask, *near_stats, *far],
        [vmem] * (7 + len(far)),
        [((chunks, 8, width), f32)] * 2
        + [((chunks, columns, width), bf16)]
        + [((HALF, 2 * wide), f32)] * last
        + [((HALF, 2 * wide), bf16)] * last,
        [vmem] * (3 + 2 * last),
        [vmem((heads, columns, 2 * DH), bf16), vmem((heads, columns, DH), bf16)]
        + [vmem((columns, DH), f32)] * 2
        + sets * 2,
        12 + 30 * columns * width // 2**20,
        4 * product * columns,
    )
    sent = dict(zip(shifts, grads[last:]))

    def pair(k):
        return (grads[k - 1] + lax.ppermute(sent[k], "sub", swap).astype(f32)).astype(bf16)

    pairs = {k: pair(k) for k in order}
    pairs[order[-1]], delta = lax.optimization_barrier((pairs[order[-1]], delta))
    sums = [lax.ppermute(pairs[k], "ctx", up(-k)) for k in order]
    near_slopes, *near_grads = call(
        functools.partial(near_gradients_kernel, group),
        [q_in, g_in, near_stats[0], near_stats[1], share, delta],
        [vmem] * 6,
        [((chunks, near, width), bf16)] + [(keys.shape, f32)] * 2 + [(keys.shape, bf16)] * 2,
        [vmem] * 5,
        [vmem((near, width), bf16)] * 2,
        8,
        product,
    )
    (grad_queries,) = call(
        functools.partial(query_gradients_kernel, group),
        [near_slopes, far_slopes, in_hbm(keys), other_key, *far],
        [vmem] * 2 + [hbm] + [vmem] * (1 + 2 * last),
        [(queries.shape, bf16)],
        [hbm],
        [
            vmem(keys.shape, bf16),
            vmem((heads, near + columns, DH), bf16),
            vmem((heads, DH, near + columns), bf16),
            vmem(queries.shape, bf16),
            pltpu.SemaphoreType.DMA,
            pltpu.SemaphoreType.DMA((heads,)),
        ],
        12,
        product,
    )
    near_got = [lax.ppermute(x, "sub", swap) for x in near_grads[2:]]
    sums, grad_queries = lax.optimization_barrier((sums, grad_queries))
    out_shapes = [(x.shape, bf16) for x in (keys, values, beacon_keys, beacon_values)]
    outs = call(
        total_kernel,
        [*near_grads[:2], *near_got, *sums],
        [vmem] * (4 + len(sums)),
        out_shapes,
        [hbm] * 4,
        [vmem(*x) for x in out_shapes] + [pltpu.SemaphoreType.DMA((4,))],
        4,
        product,
    )
    return (grad_queries, *outs)


def solution(mesh):
    rows = P(("grp", "ctx", "sub"), "tp")
    return jax.shard_map(
        local,
        mesh=mesh,
        in_specs=(rows,) * 6 + (P("grp"),),
        out_specs=(rows,) * 5,
        check_vma=False,
    )
```

```python
import functools
import math

import jax
import jax.numpy as jnp
from jax import lax
from jax.experimental import pallas as pl
from jax.experimental.pallas import tpu as pltpu
from jax.sharding import PartitionSpec as P

DH = 128
SPAN = 256
SLOTS = SPAN // 2
HALF = SLOTS // 2
NT = (((1,), (1,)), ((), ()))
HIDDEN = -3e38
JOIN = 4
BLOCK = 16
SCALE = DH ** (-0.5)
LOG_SCALE = SCALE * math.log2(math.e)


def interleave(first, second):
    few, many = sorted((first, second), key=len)
    done = 0
    for index, step in enumerate(few):
        step()
        upto = len(many) * (index + 1) // len(few)
        for other in many[done:upto]:
            other()
        done = upto
    for other in many[done:]:
        other()


def pipeline(chunks, products, softmax, gradients):
    for step in products(0):
        step()
    for chunk in range(chunks):
        matrix = gradients(chunk - 1) if chunk > 0 else []
        matrix = matrix + (products(chunk + 1) if chunk + 1 < chunks else [])
        interleave(matrix, softmax(chunk))
    for step in gradients(chunks - 1):
        step()


def head_cols(head):
    return slice(head * DH, (head + 1) * DH)


def joined(buf, chunk, start, count):
    first = chunk * JOIN + start
    return jnp.concatenate([buf[:, head_cols(first + i)] for i in range(count)], axis=0)


def pair_products(key_buf, value_buf, q_buf, g_buf, chunk, head, score_ref, signal_ref):
    rows = q_buf.shape[0]
    at = [lax.broadcasted_iota(jnp.int32, (rows, DH), axis) for axis in range(2)]
    one_hot = jnp.where(at[0] == at[1], 1.0, 0.0).astype(jnp.bfloat16)
    one_hot = jnp.concatenate([one_hot] * 2, axis=0)

    def score(start):
        queries = jnp.concatenate([joined(q_buf, chunk, start, 2), one_hot], axis=1)
        cols = slice(start * rows, (start + 2) * rows)
        score_ref[:, cols] = lax.dot_general(key_buf[head], queries, NT, preferred_element_type=jnp.float32)

    def signal(start):
        cols = slice(start * rows, (start + 2) * rows)
        signal_ref[:, cols] = lax.dot_general(
            value_buf[head], joined(g_buf, chunk, start, 2), NT, preferred_element_type=jnp.float32
        )

    return [functools.partial(f, start) for f in (score, signal) for start in range(0, JOIN, 2)]


def mask_of(seen):
    return jnp.where(seen, 0.0, HIDDEN).astype(jnp.bfloat16)


def place(key_buf, value_buf, at, keys, values, mask):
    size = mask.shape[0]
    for head in range(key_buf.shape[0]):
        key_buf[head, at : at + size, :DH] = keys[:, head_cols(head)]
        key_buf[head, at : at + size, DH:] = mask
        value_buf[head, at : at + size, :] = values[:, head_cols(head)]


def spread(x):
    return jnp.broadcast_to(x, (8, x.shape[1]))


def exponentials(chunk, grown_out, top_out, total_out):
    score_ref = grown_out.at[chunk]
    columns, width = score_ref.shape
    state = {"top": jnp.full((8, width), HIDDEN, jnp.float32)}

    def top(at):
        for i in range(at, at + BLOCK, 8):
            state["top"] = jnp.maximum(state["top"], score_ref[i : i + 8, :])

    def end_top():
        state["top"] = spread(jnp.max(state["top"], axis=0, keepdims=True))
        top_out[chunk] = state["top"]
        state["total"] = jnp.zeros((8, width), jnp.float32)

    def grow(at):
        for i in range(at, at + BLOCK, 8):
            grown = jnp.exp2((score_ref[i : i + 8, :] - state["top"]) * LOG_SCALE)
            score_ref[i : i + 8, :] = grown
            state["total"] = state["total"] + grown

    def end_grow():
        total_out[chunk] = spread(jnp.sum(state["total"], axis=0, keepdims=True))

    blocks = range(0, columns, BLOCK)
    return [functools.partial(top, at) for at in blocks] + [end_top] + [functools.partial(grow, at) for at in blocks] + [end_grow]


def near_kernel(
    shifts, group, ratios, q_hbm, g_hbm, key_hbm, value_hbm, other_key, other_value, q_buf, g_buf, mask_out, grown_out,
    signal_out, top_out, total_out, own_key, own_value, key_buf, value_buf, sem,
):
    rows = q_buf.shape[0]
    heads = key_buf.shape[0]
    per_head = group // JOIN
    sub = lax.axis_index("sub")
    pairs = [(key_hbm, own_key), (value_hbm, own_value)]
    for head in range(heads):
        cols = slice(head * group * DH, (head + 1) * group * DH)
        pairs += [(q_hbm.at[:, cols], q_buf.at[:, cols]), (g_hbm.at[:, cols], g_buf.at[:, cols])]
    loads = [pltpu.make_async_copy(*pair, sem.at[i]) for i, pair in enumerate(pairs)]
    for load in loads:
        load.start()
    key_at = lax.broadcasted_iota(jnp.int32, (rows, DH), 0)
    token_at = lax.broadcasted_iota(jnp.int32, (rows, DH), 1)
    place(key_buf, value_buf, rows, other_key, other_value, mask_of(key_at < sub * rows))
    here = lax.axis_index("ctx")
    slot_at = lax.broadcasted_iota(jnp.int32, (HALF, DH), 0)
    for shift in range(shifts):
        owner = jnp.maximum(here - 1 - shift, 0)
        live = jnp.where(here > shift, SPAN // ratios[owner], 0)
        for side, first in enumerate((sub * HALF, (1 - sub) * HALF)):
            at = (2 * shift + side) * HALF
            mask_out[at : at + HALF, :] = mask_of(slot_at < live - first)
    loads[0].wait()
    loads[1].wait()
    place(key_buf, value_buf, 0, own_key, own_value, mask_of(key_at <= token_at))

    def products(chunk):
        head = chunk // per_head
        if chunk % per_head == 0:
            loads[2 + 2 * head].wait()
            loads[3 + 2 * head].wait()
        return pair_products(
            key_buf, value_buf, q_buf, g_buf, chunk, head, grown_out.at[chunk], signal_out.at[chunk]
        )

    pipeline(
        heads * per_head,
        products,
        lambda chunk: exponentials(chunk, grown_out, top_out, total_out),
        lambda chunk: [],
    )


def place_far(key_buf, value_buf, far, mask):
    wide = far[0].shape[1] // 2
    for index, source in enumerate(far):
        at = index * HALF
        place(key_buf, value_buf, at, source.at[:, :wide], source.at[:, wide:], mask[at : at + HALF, :])


def far_kernel(shifts, group, *refs):
    here = lax.axis_index("ctx")
    levels = sorted({shifts * i // 3 for i in range(4)} | set(range(min(shifts, 4))))
    for low, level in zip([-1, *levels], levels):
        pl.when((here > low) & (here <= level))(functools.partial(far_part, shifts, level, group, *refs))


def far_part(shifts, seen, group, q_buf, g_buf, far_mask, near_grown, near_signal, near_top, near_total, *refs):
    far, refs = refs[: 2 * shifts], refs[2 * shifts :]
    share_out, delta_out, slopes_out, own_outs, sent_outs = refs[0], refs[1], refs[2], refs[3 : 3 + shifts], refs[3 + shifts : 3 + 2 * shifts]
    refs = refs[3 + 2 * shifts :]
    (key_buf, value_buf, dk_buf, dv_buf), sets = refs[:4], (refs[4:7], refs[7:10])
    rows = q_buf.shape[0]
    heads = key_buf.shape[0]
    columns = seen * SLOTS
    wide = heads * DH
    per_head = group // JOIN
    chunks = heads * per_head
    width = JOIN * rows
    if seen:
        place_far(key_buf, value_buf, far[: 2 * seen], far_mask)
    for out in (*own_outs[seen:], *sent_outs[seen:]):
        out[...] = jnp.zeros_like(out)
    key_buf, value_buf = key_buf.at[:, :columns, :], value_buf.at[:, :columns, :]
    sets = [[ref.at[:columns, :] for ref in refs] for refs in sets]

    def products(chunk):
        if not seen:
            return []
        score_ref, signal_ref, _ = sets[chunk % 2]
        return pair_products(key_buf, value_buf, q_buf, g_buf, chunk, chunk // per_head, score_ref, signal_ref)

    def softmax(chunk):
        score_ref, signal_ref, weight_ref = sets[chunk % 2]
        slope_ref = slopes_out.at[chunk]
        state = {"top": near_top[chunk]}

        def top(at):
            for i in range(at, at + BLOCK, 8):
                state["top"] = jnp.maximum(state["top"], score_ref[i : i + 8, :])

        def end_top():
            state["top"] = spread(jnp.max(state["top"], axis=0, keepdims=True))
            state["total"] = jnp.zeros((8, width), jnp.float32)

        def grow(at):
            for i in range(at, at + BLOCK, 8):
                grown = jnp.exp2((score_ref[i : i + 8, :] - state["top"]) * LOG_SCALE)
                score_ref[i : i + 8, :] = grown
                state["total"] = state["total"] + grown

        def end_grow():
            total = spread(jnp.sum(state["total"], axis=0, keepdims=True))
            shrink = jnp.exp2((near_top[chunk] - state["top"]) * LOG_SCALE)
            state["far"] = 1.0 / (near_total[chunk] * shrink + total)
            state["near"] = shrink * state["far"]
            share_out[chunk] = state["near"]
            state["delta"] = jnp.zeros((8, width), jnp.float32)

        def weigh(grown, signal, share, at):
            probs = [grown[i : i + 8, :] * state[share] for i in range(at, at + BLOCK, 8)]
            weights = jnp.concatenate(probs, axis=0).astype(jnp.bfloat16)
            if share == "far":
                weight_ref[at : at + BLOCK, :] = weights
            terms = weights.astype(jnp.float32) * signal[at : at + BLOCK, :]
            for i in range(0, BLOCK, 8):
                state["delta"] = state["delta"] + terms[i : i + 8]

        def end_weigh():
            state["delta"] = spread(jnp.sum(state["delta"], axis=0, keepdims=True))
            delta_out[chunk] = state["delta"]

        def slope(at):
            slopes = []
            for i in range(at, at + BLOCK, 8):
                probs = score_ref[i : i + 8, :] * state["far"]
                slopes.append(probs * (signal_ref[i : i + 8, :] - state["delta"]))
            slope_ref[at : at + BLOCK, :] = jnp.concatenate(slopes, axis=0).astype(jnp.bfloat16)

        grown, signal = near_grown.at[chunk], near_signal.at[chunk]
        blocks = range(0, columns, BLOCK)

        def clear():
            if seen < shifts:
                slope_ref[columns:, :] = jnp.zeros((SLOTS * (shifts - seen), width), jnp.bfloat16)

        steps = [clear] + [functools.partial(top, at) for at in blocks] + [end_top]
        steps += [functools.partial(grow, at) for at in blocks] + [end_grow]
        steps += [functools.partial(weigh, score_ref, signal_ref, "far", at) for at in blocks]
        steps += [functools.partial(weigh, grown, signal, "near", at) for at in range(0, 2 * rows, BLOCK)] + [end_weigh]
        return steps + [functools.partial(slope, at) for at in blocks]

    def gradients(chunk):
        if not seen:
            return []
        weight_ref = sets[chunk % 2][2]
        head = chunk // per_head
        last = chunk % per_head == per_head - 1

        def collect(total_ref, buf, left, side, factor):
            total = None
            for start in range(0, JOIN, 2):
                cols = slice(start * rows, (start + 2) * rows)
                part = jnp.dot(left(cols), joined(buf, chunk, start, 2), preferred_element_type=jnp.float32)
                total = part if total is None else total + part
            if chunk % per_head:
                total = total + total_ref[:columns, :]
            if not last:
                total_ref[:columns, :] = total
                return
            cols = slice(side * wide + head * DH, side * wide + (head + 1) * DH)
            for shift in range(seen):
                at = shift * SLOTS
                own_outs[shift][:, cols] = total[at : at + HALF] * factor
                sent_outs[shift][:, cols] = (total[at + HALF : at + SLOTS] * factor).astype(jnp.bfloat16)

        return [
            functools.partial(collect, dk_buf, q_buf, lambda cols: slopes_out[chunk, :columns, cols], 0, SCALE),
            functools.partial(collect, dv_buf, g_buf, lambda cols: weight_ref[:, cols], 1, 1.0),
        ]

    pipeline(chunks, products, softmax, gradients)


def near_gradients_kernel(group, q_buf, g_buf, grown, signal, share, delta, slopes_out, *refs):
    own_outs, sent_outs, sets = refs[:2], refs[2:4], refs[4:]
    rows = q_buf.shape[0]
    wide = own_outs[0].shape[1]
    per_head = group // JOIN
    chunks = wide // DH * per_head
    near = 2 * rows
    totals = {}

    def softmax(chunk):
        weight_ref = sets[chunk % 2]

        def work(at):
            weights, slopes = [], []
            for i in range(at, at + BLOCK, 8):
                probs = grown[chunk, i : i + 8, :] * share[chunk]
                weights.append(probs)
                slopes.append(probs * (signal[chunk, i : i + 8, :] - delta[chunk]))
            weight_ref[at : at + BLOCK, :] = jnp.concatenate(weights, axis=0).astype(jnp.bfloat16)
            slopes_out[chunk, at : at + BLOCK, :] = jnp.concatenate(slopes, axis=0).astype(jnp.bfloat16)

        return [functools.partial(work, at) for at in range(0, near, BLOCK)]

    def gradients(chunk):
        weight_ref = sets[chunk % 2]
        head = chunk // per_head

        def collect(left, buf, side, factor):
            total = totals.pop(side, None)
            for start in range(0, JOIN, 2):
                cols = slice(start * rows, (start + 2) * rows)
                part = jnp.dot(left(cols), joined(buf, chunk, start, 2), preferred_element_type=jnp.float32)
                total = part if total is None else total + part
            if chunk % per_head < per_head - 1:
                totals[side] = total
                return
            own_outs[side][:, head_cols(head)] = total[:rows] * factor
            sent_outs[side][:, head_cols(head)] = (total[rows:] * factor).astype(jnp.bfloat16)

        return [
            functools.partial(collect, lambda cols: slopes_out[chunk, :, cols], q_buf, 0, SCALE),
            functools.partial(collect, lambda cols: weight_ref[:, cols], g_buf, 1, 1.0),
        ]

    pipeline(chunks, lambda chunk: [], softmax, gradients)


def query_gradients_kernel(group, near_slopes, far_slopes, key_hbm, other_key, *refs):
    far, (dq_hbm, own_key, key_buf, turned_buf, dq_buf, in_sem, out_sem) = refs[:-7], refs[-7:]
    rows = dq_buf.shape[0]
    heads = key_buf.shape[0]
    near = 2 * rows
    per_head = group // JOIN
    load = pltpu.make_async_copy(key_hbm, own_key, in_sem)
    load.start()
    at = rows
    for piece in (other_key, *far):
        size = piece.shape[0]
        for head in range(heads):
            key_buf[head, at : at + size, :] = piece[:, head_cols(head)]
        at += size
    load.wait()
    stores = []
    for head in range(heads):
        key_buf[head, :rows, :] = own_key[:, head_cols(head)]
        turned_buf[head] = key_buf[head].T
        for chunk in range(head * per_head, (head + 1) * per_head):
            for start in range(0, JOIN, 2):
                cols = slice(start * rows, (start + 2) * rows)
                turned = jnp.dot(
                    turned_buf[head, :, :near], near_slopes[chunk, :, cols], preferred_element_type=jnp.float32
                ) + jnp.dot(turned_buf[head, :, near:], far_slopes[chunk, :, cols], preferred_element_type=jnp.float32)
                for i in range(2):
                    dq = turned[:, i * rows : (i + 1) * rows].T * SCALE
                    dq_buf[:, head_cols(chunk * JOIN + start + i)] = dq.astype(jnp.bfloat16)
        cols = slice(head * group * DH, (head + 1) * group * DH)
        stores.append(pltpu.make_async_copy(dq_buf.at[:, cols], dq_hbm.at[:, cols], out_sem.at[head]))
        stores[-1].start()
    for store in stores:
        store.wait()


def total_kernel(own_key, own_value, got_key, got_value, *refs):
    terms, (outs, bufs, sem) = refs[:-9], (refs[-9:-5], refs[-5:-1], refs[-1])
    wide = bufs[0].shape[1]
    near = [own[...] + got[...].astype(jnp.float32) for own, got in ((own_key, got_key), (own_value, got_value))]
    beacon = functools.reduce(jnp.add, [x[...].astype(jnp.float32) for x in terms])
    stores = []
    for at, total in enumerate((*near, beacon[:, :wide], beacon[:, wide:])):
        bufs[at][...] = total.astype(jnp.bfloat16)
        stores.append(pltpu.make_async_copy(bufs[at], outs[at], sem.at[at]))
        stores[-1].start()
    for store in stores:
        store.wait()


def in_hbm(x):
    return pltpu.with_memory_space_constraint(x, pltpu.HBM)


def call(kernel, operands, spaces, outs, out_spaces, scratch, limit, products):
    return list(pl.pallas_call(
        kernel,
        out_shape=[jax.ShapeDtypeStruct(*x) for x in outs],
        in_specs=[pl.BlockSpec(memory_space=x) for x in spaces],
        out_specs=[pl.BlockSpec(memory_space=x) for x in out_spaces],
        scratch_shapes=scratch,
        compiler_params=pltpu.CompilerParams(vmem_limit_bytes=limit * 1024 * 1024),
        cost_estimate=pl.CostEstimate(flops=products, bytes_accessed=products // 256, transcendentals=products // 512),
    )(*operands))


def local(queries, keys, values, beacon_keys, beacon_values, grad_out, ratios):
    bf16, f32 = jnp.bfloat16, jnp.float32
    hbm, vmem = pltpu.HBM, pltpu.VMEM
    spans = ratios.shape[0]
    rows, wide = keys.shape
    heads = wide // DH
    group = queries.shape[1] // wide
    chunks = heads * group // JOIN
    width = JOIN * rows
    last = spans - 1
    near, columns = 2 * rows, SLOTS * last
    swap = [(0, 1), (1, 0)]
    shifts = range(1, spans)
    order = sorted(shifts, key=lambda k: abs(2 * k - spans))

    def up(k):
        return [(i, (i + k) % spans) for i in range(spans)]

    left = lax.broadcasted_iota(jnp.int32, (beacon_keys.shape[0], 2 * wide), 1) < wide
    beacons = jnp.where(left, jnp.pad(beacon_keys, ((0, 0), (0, wide))), jnp.pad(beacon_values, ((0, 0), (wide, 0))))
    near_keys, near_values, beacons = lax.optimization_barrier((keys, values, beacons))
    own = {k: lax.ppermute(beacons, "ctx", up(k)) for k in reversed(order)}
    other_key, other_value = (lax.ppermute(x, "sub", swap) for x in (near_keys, near_values))

    product = queries.shape[1] * rows * 2

    def stats_of(size):
        return [((chunks, size, width), f32)] * 2 + [((chunks, 8, width), f32)] * 2

    q_in, g_in, far_mask, *near_stats = call(
        functools.partial(near_kernel, last, group),
        [ratios, in_hbm(queries), in_hbm(grad_out), in_hbm(keys), in_hbm(values), other_key, other_value],
        [pltpu.SMEM] + [hbm] * 4 + [vmem] * 2,
        [(queries.shape, bf16)] * 2 + [((columns, DH), bf16)] + stats_of(near),
        [vmem] * 7,
        [vmem(keys.shape, bf16)] * 2
        + [vmem((heads, near, 2 * DH), bf16), vmem((heads, near, DH), bf16)]
        + [pltpu.SemaphoreType.DMA((2 + 2 * heads,))],
        8,
        2 * product * near,
    )
    first = order[0]
    own[first], near_stats[2] = lax.optimization_barrier((own[first], near_stats[2]))
    other = {k: lax.ppermute(own[k], "sub", swap) for k in order}
    far = [x[k] for k in shifts for x in (own, other)]
    sets = [vmem((columns, width), f32)] * 2 + [vmem((columns, width), bf16)]
    share, delta, far_slopes, *grads = call(
        functools.partial(far_kernel, last, group),
        [q_in, g_in, far_mask, *near_stats, *far],
        [vmem] * (7 + len(far)),
        [((chunks, 8, width), f32)] * 2
        + [((chunks, columns, width), bf16)]
        + [((HALF, 2 * wide), f32)] * last
        + [((HALF, 2 * wide), bf16)] * last,
        [vmem] * (3 + 2 * last),
        [vmem((heads, columns, 2 * DH), bf16), vmem((heads, columns, DH), bf16)]
        + [vmem((columns, DH), f32)] * 2
        + sets * 2,
        12 + 30 * columns * width // 2**20,
        4 * product * columns,
    )
    sent = dict(zip(shifts, grads[last:]))

    def pair(k):
        return (grads[k - 1] + lax.ppermute(sent[k], "sub", swap).astype(f32)).astype(bf16)

    pairs = {k: pair(k) for k in order}
    pairs[order[-1]], delta = lax.optimization_barrier((pairs[order[-1]], delta))
    down = {k: up(-k) for k in order} | {last: [(last, 0)]}
    sums = [lax.ppermute(pairs[k], "ctx", down[k]) for k in order]
    near_slopes, *near_grads = call(
        functools.partial(near_gradients_kernel, group),
        [q_in, g_in, near_stats[0], near_stats[1], share, delta],
        [vmem] * 6,
        [((chunks, near, width), bf16)] + [(keys.shape, f32)] * 2 + [(keys.shape, bf16)] * 2,
        [vmem] * 5,
        [vmem((near, width), bf16)] * 2,
        8,
        product,
    )
    (grad_queries,) = call(
        functools.partial(query_gradients_kernel, group),
        [near_slopes, far_slopes, in_hbm(keys), other_key, *far],
        [vmem] * 2 + [hbm] + [vmem] * (1 + 2 * last),
        [(queries.shape, bf16)],
        [hbm],
        [
            vmem(keys.shape, bf16),
            vmem((heads, near + columns, DH), bf16),
            vmem((heads, DH, near + columns), bf16),
            vmem(queries.shape, bf16),
            pltpu.SemaphoreType.DMA,
            pltpu.SemaphoreType.DMA((heads,)),
        ],
        12,
        product,
    )
    near_got = [lax.ppermute(x, "sub", swap) for x in near_grads[2:]]
    sums, grad_queries = lax.optimization_barrier((sums, grad_queries))
    out_shapes = [(x.shape, bf16) for x in (keys, values, beacon_keys, beacon_values)]
    outs = call(
        total_kernel,
        [*near_grads[:2], *near_got, *sums],
        [vmem] * (4 + len(sums)),
        out_shapes,
        [hbm] * 4,
        [vmem(*x) for x in out_shapes] + [pltpu.SemaphoreType.DMA((4,))],
        4,
        product,
    )
    return (grad_queries, *outs)


def solution(mesh):
    rows = P(("grp", "ctx", "sub"), "tp")
    return jax.shard_map(
        local,
        mesh=mesh,
        in_specs=(rows,) * 6 + (P("grp"),),
        out_specs=(rows,) * 5,
        check_vma=False,
    )
```

```python
import functools
import math

import jax
import jax.numpy as jnp
from jax import lax
from jax.experimental import pallas as pl
from jax.experimental.pallas import tpu as pltpu
from jax.sharding import PartitionSpec as P

DH = 128
SPAN = 256
SLOTS = SPAN // 2
HALF = SLOTS // 2
NT = (((1,), (1,)), ((), ()))
HIDDEN = -3e38
JOIN = 4
BLOCK = 16
SCALE = DH ** (-0.5)
LOG_SCALE = SCALE * math.log2(math.e)


def interleave(first, second):
    few, many = sorted((first, second), key=len)
    done = 0
    for index, step in enumerate(few):
        step()
        upto = len(many) * (index + 1) // len(few)
        for other in many[done:upto]:
            other()
        done = upto
    for other in many[done:]:
        other()


def pipeline(chunks, products, softmax, gradients):
    for step in products(0):
        step()
    for chunk in range(chunks):
        matrix = gradients(chunk - 1) if chunk > 0 else []
        matrix = matrix + (products(chunk + 1) if chunk + 1 < chunks else [])
        interleave(matrix, softmax(chunk))
    for step in gradients(chunks - 1):
        step()


def head_cols(head):
    return slice(head * DH, (head + 1) * DH)


def joined(buf, chunk, start, count):
    first = chunk * JOIN + start
    return jnp.concatenate([buf[:, head_cols(first + i)] for i in range(count)], axis=0)


def pair_products(key_buf, value_buf, q_buf, g_buf, chunk, head, score_ref, signal_ref):
    rows = q_buf.shape[0]
    at = [lax.broadcasted_iota(jnp.int32, (rows, DH), axis) for axis in range(2)]
    one_hot = jnp.where(at[0] == at[1], 1.0, 0.0).astype(jnp.bfloat16)
    one_hot = jnp.concatenate([one_hot] * 2, axis=0)

    def score(start):
        queries = jnp.concatenate([joined(q_buf, chunk, start, 2), one_hot], axis=1)
        cols = slice(start * rows, (start + 2) * rows)
        score_ref[:, cols] = lax.dot_general(key_buf[head], queries, NT, preferred_element_type=jnp.float32)

    def signal(start):
        cols = slice(start * rows, (start + 2) * rows)
        signal_ref[:, cols] = lax.dot_general(
            value_buf[head], joined(g_buf, chunk, start, 2), NT, preferred_element_type=jnp.float32
        )

    return [functools.partial(f, start) for f in (score, signal) for start in range(0, JOIN, 2)]


def mask_of(seen):
    return jnp.where(seen, 0.0, HIDDEN).astype(jnp.bfloat16)


def place(key_buf, value_buf, at, keys, values, mask):
    size = mask.shape[0]
    for head in range(key_buf.shape[0]):
        key_buf[head, at : at + size, :DH] = keys[:, head_cols(head)]
        key_buf[head, at : at + size, DH:] = mask
        value_buf[head, at : at + size, :] = values[:, head_cols(head)]


def spread(x):
    return jnp.broadcast_to(x, (8, x.shape[1]))


def exponentials(chunk, grown_out, top_out, total_out):
    score_ref = grown_out.at[chunk]
    columns, width = score_ref.shape
    state = {"top": jnp.full((8, width), HIDDEN, jnp.float32)}

    def top(at):
        for i in range(at, at + BLOCK, 8):
            state["top"] = jnp.maximum(state["top"], score_ref[i : i + 8, :])

    def end_top():
        state["top"] = spread(jnp.max(state["top"], axis=0, keepdims=True))
        top_out[chunk] = state["top"]
        state["total"] = jnp.zeros((8, width), jnp.float32)

    def grow(at):
        for i in range(at, at + BLOCK, 8):
            grown = jnp.exp2((score_ref[i : i + 8, :] - state["top"]) * LOG_SCALE)
            score_ref[i : i + 8, :] = grown
            state["total"] = state["total"] + grown

    def end_grow():
        total_out[chunk] = spread(jnp.sum(state["total"], axis=0, keepdims=True))

    blocks = range(0, columns, BLOCK)
    return [functools.partial(top, at) for at in blocks] + [end_top] + [functools.partial(grow, at) for at in blocks] + [end_grow]


def near_kernel(
    shifts, group, ratios, q_hbm, g_hbm, key_hbm, value_hbm, other_key, other_value, q_buf, g_buf, mask_out, grown_out,
    signal_out, top_out, total_out, own_key, own_value, key_buf, value_buf, sem,
):
    rows = q_buf.shape[0]
    heads = key_buf.shape[0]
    per_head = group // JOIN
    sub = lax.axis_index("sub")
    pairs = [(key_hbm, own_key), (value_hbm, own_value)]
    for head in range(heads):
        cols = slice(head * group * DH, (head + 1) * group * DH)
        pairs += [(q_hbm.at[:, cols], q_buf.at[:, cols]), (g_hbm.at[:, cols], g_buf.at[:, cols])]
    loads = [pltpu.make_async_copy(*pair, sem.at[i]) for i, pair in enumerate(pairs)]
    for load in loads:
        load.start()
    key_at = lax.broadcasted_iota(jnp.int32, (rows, DH), 0)
    token_at = lax.broadcasted_iota(jnp.int32, (rows, DH), 1)
    place(key_buf, value_buf, rows, other_key, other_value, mask_of(key_at < sub * rows))
    here = lax.axis_index("ctx")
    slot_at = lax.broadcasted_iota(jnp.int32, (HALF, DH), 0)
    for shift in range(shifts):
        owner = jnp.maximum(here - 1 - shift, 0)
        live = jnp.where(here > shift, SPAN // ratios[owner], 0)
        for side, first in enumerate((sub * HALF, (1 - sub) * HALF)):
            at = (2 * shift + side) * HALF
            mask_out[at : at + HALF, :] = mask_of(slot_at < live - first)
    loads[0].wait()
    loads[1].wait()
    place(key_buf, value_buf, 0, own_key, own_value, mask_of(key_at <= token_at))

    def products(chunk):
        head = chunk // per_head
        if chunk % per_head == 0:
            loads[2 + 2 * head].wait()
            loads[3 + 2 * head].wait()
        return pair_products(
            key_buf, value_buf, q_buf, g_buf, chunk, head, grown_out.at[chunk], signal_out.at[chunk]
        )

    pipeline(
        heads * per_head,
        products,
        lambda chunk: exponentials(chunk, grown_out, top_out, total_out),
        lambda chunk: [],
    )


def place_far(key_buf, value_buf, far, mask):
    wide = far[0].shape[1] // 2
    for index, source in enumerate(far):
        at = index * HALF
        place(key_buf, value_buf, at, source.at[:, :wide], source.at[:, wide:], mask[at : at + HALF, :])


def far_kernel(shifts, group, *refs):
    here = lax.axis_index("ctx")
    levels = sorted({shifts * i // 3 for i in range(4)} | set(range(min(shifts, 4))))
    for low, level in zip([-1, *levels], levels):
        pl.when((here > low) & (here <= level))(functools.partial(far_part, shifts, level, group, *refs))


def far_part(shifts, seen, group, q_buf, g_buf, far_mask, near_grown, near_signal, near_top, near_total, *refs):
    far, refs = refs[: 2 * shifts], refs[2 * shifts :]
    share_out, delta_out, slopes_out, own_outs, sent_outs = refs[0], refs[1], refs[2], refs[3 : 3 + shifts], refs[3 + shifts : 3 + 2 * shifts]
    refs = refs[3 + 2 * shifts :]
    (key_buf, value_buf, dk_buf, dv_buf), sets = refs[:4], (refs[4:7], refs[7:10])
    rows = q_buf.shape[0]
    heads = key_buf.shape[0]
    columns = seen * SLOTS
    wide = heads * DH
    per_head = group // JOIN
    chunks = heads * per_head
    width = JOIN * rows
    if seen:
        place_far(key_buf, value_buf, far[: 2 * seen], far_mask)
    for out in (*own_outs[seen:], *sent_outs[seen:]):
        out[...] = jnp.zeros_like(out)
    key_buf, value_buf = key_buf.at[:, :columns, :], value_buf.at[:, :columns, :]
    sets = [[ref.at[:columns, :] for ref in refs] for refs in sets]

    def products(chunk):
        if not seen:
            return []
        score_ref, signal_ref, _ = sets[chunk % 2]
        return pair_products(key_buf, value_buf, q_buf, g_buf, chunk, chunk // per_head, score_ref, signal_ref)

    def softmax(chunk):
        score_ref, signal_ref, weight_ref = sets[chunk % 2]
        slope_ref = slopes_out.at[chunk]
        state = {"top": near_top[chunk]}

        def top(at):
            for i in range(at, at + BLOCK, 8):
                state["top"] = jnp.maximum(state["top"], score_ref[i : i + 8, :])

        def end_top():
            state["top"] = spread(jnp.max(state["top"], axis=0, keepdims=True))
            state["total"] = jnp.zeros((8, width), jnp.float32)

        def grow(at):
            for i in range(at, at + BLOCK, 8):
                grown = jnp.exp2((score_ref[i : i + 8, :] - state["top"]) * LOG_SCALE)
                score_ref[i : i + 8, :] = grown
                state["total"] = state["total"] + grown

        def end_grow():
            total = spread(jnp.sum(state["total"], axis=0, keepdims=True))
            shrink = jnp.exp2((near_top[chunk] - state["top"]) * LOG_SCALE)
            state["far"] = 1.0 / (near_total[chunk] * shrink + total)
            state["near"] = shrink * state["far"]
            share_out[chunk] = state["near"]
            state["delta"] = jnp.zeros((8, width), jnp.float32)

        def weigh(grown, signal, share, at):
            probs = [grown[i : i + 8, :] * state[share] for i in range(at, at + BLOCK, 8)]
            weights = jnp.concatenate(probs, axis=0).astype(jnp.bfloat16)
            if share == "far":
                weight_ref[at : at + BLOCK, :] = weights
            terms = weights.astype(jnp.float32) * signal[at : at + BLOCK, :]
            for i in range(0, BLOCK, 8):
                state["delta"] = state["delta"] + terms[i : i + 8]

        def end_weigh():
            state["delta"] = spread(jnp.sum(state["delta"], axis=0, keepdims=True))
            delta_out[chunk] = state["delta"]

        def slope(at):
            slopes = []
            for i in range(at, at + BLOCK, 8):
                probs = score_ref[i : i + 8, :] * state["far"]
                slopes.append(probs * (signal_ref[i : i + 8, :] - state["delta"]))
            slope_ref[at : at + BLOCK, :] = jnp.concatenate(slopes, axis=0).astype(jnp.bfloat16)

        grown, signal = near_grown.at[chunk], near_signal.at[chunk]
        blocks = range(0, columns, BLOCK)

        def clear():
            if seen < shifts:
                slope_ref[columns:, :] = jnp.zeros((SLOTS * (shifts - seen), width), jnp.bfloat16)

        steps = [clear] + [functools.partial(top, at) for at in blocks] + [end_top]
        steps += [functools.partial(grow, at) for at in blocks] + [end_grow]
        steps += [functools.partial(weigh, score_ref, signal_ref, "far", at) for at in blocks]
        steps += [functools.partial(weigh, grown, signal, "near", at) for at in range(0, 2 * rows, BLOCK)] + [end_weigh]
        return steps + [functools.partial(slope, at) for at in blocks]

    def gradients(chunk):
        if not seen:
            return []
        weight_ref = sets[chunk % 2][2]
        head = chunk // per_head
        last = chunk % per_head == per_head - 1

        def collect(total_ref, buf, left, side, factor):
            total = None
            for start in range(0, JOIN, 2):
                cols = slice(start * rows, (start + 2) * rows)
                part = jnp.dot(left(cols), joined(buf, chunk, start, 2), preferred_element_type=jnp.float32)
                total = part if total is None else total + part
            if chunk % per_head:
                total = total + total_ref[:columns, :]
            if not last:
                total_ref[:columns, :] = total
                return
            cols = slice(side * wide + head * DH, side * wide + (head + 1) * DH)
            for shift in range(seen):
                at = shift * SLOTS
                own_outs[shift][:, cols] = total[at : at + HALF] * factor
                sent_outs[shift][:, cols] = (total[at + HALF : at + SLOTS] * factor).astype(jnp.bfloat16)

        return [
            functools.partial(collect, dk_buf, q_buf, lambda cols: slopes_out[chunk, :columns, cols], 0, SCALE),
            functools.partial(collect, dv_buf, g_buf, lambda cols: weight_ref[:, cols], 1, 1.0),
        ]

    pipeline(chunks, products, softmax, gradients)


def near_gradients_kernel(group, q_buf, g_buf, grown, signal, share, delta, slopes_out, *refs):
    own_outs, sent_outs, sets = refs[:2], refs[2:4], refs[4:]
    rows = q_buf.shape[0]
    wide = own_outs[0].shape[1]
    per_head = group // JOIN
    chunks = wide // DH * per_head
    near = 2 * rows
    totals = {}

    def softmax(chunk):
        weight_ref = sets[chunk % 2]

        def work(at):
            weights, slopes = [], []
            for i in range(at, at + BLOCK, 8):
                probs = grown[chunk, i : i + 8, :] * share[chunk]
                weights.append(probs)
                slopes.append(probs * (signal[chunk, i : i + 8, :] - delta[chunk]))
            weight_ref[at : at + BLOCK, :] = jnp.concatenate(weights, axis=0).astype(jnp.bfloat16)
            slopes_out[chunk, at : at + BLOCK, :] = jnp.concatenate(slopes, axis=0).astype(jnp.bfloat16)

        return [functools.partial(work, at) for at in range(0, near, BLOCK)]

    def gradients(chunk):
        weight_ref = sets[chunk % 2]
        head = chunk // per_head

        def collect(left, buf, side, factor):
            total = totals.pop(side, None)
            for start in range(0, JOIN, 2):
                cols = slice(start * rows, (start + 2) * rows)
                part = jnp.dot(left(cols), joined(buf, chunk, start, 2), preferred_element_type=jnp.float32)
                total = part if total is None else total + part
            if chunk % per_head < per_head - 1:
                totals[side] = total
                return
            own_outs[side][:, head_cols(head)] = total[:rows] * factor
            sent_outs[side][:, head_cols(head)] = (total[rows:] * factor).astype(jnp.bfloat16)

        return [
            functools.partial(collect, lambda cols: slopes_out[chunk, :, cols], q_buf, 0, SCALE),
            functools.partial(collect, lambda cols: weight_ref[:, cols], g_buf, 1, 1.0),
        ]

    pipeline(chunks, lambda chunk: [], softmax, gradients)


def query_gradients_kernel(group, near_slopes, far_slopes, key_hbm, other_key, *refs):
    far, (dq_hbm, own_key, key_buf, turned_buf, dq_buf, in_sem, out_sem) = refs[:-7], refs[-7:]
    rows = dq_buf.shape[0]
    heads = key_buf.shape[0]
    near = 2 * rows
    per_head = group // JOIN
    load = pltpu.make_async_copy(key_hbm, own_key, in_sem)
    load.start()
    at = rows
    for piece in (other_key, *far):
        size = piece.shape[0]
        for head in range(heads):
            key_buf[head, at : at + size, :] = piece[:, head_cols(head)]
        at += size
    load.wait()
    stores = []
    for head in range(heads):
        key_buf[head, :rows, :] = own_key[:, head_cols(head)]
        turned_buf[head] = key_buf[head].T
        for chunk in range(head * per_head, (head + 1) * per_head):
            for start in range(0, JOIN, 2):
                cols = slice(start * rows, (start + 2) * rows)
                turned = jnp.dot(
                    turned_buf[head, :, :near], near_slopes[chunk, :, cols], preferred_element_type=jnp.float32
                ) + jnp.dot(turned_buf[head, :, near:], far_slopes[chunk, :, cols], preferred_element_type=jnp.float32)
                for i in range(2):
                    dq = turned[:, i * rows : (i + 1) * rows].T * SCALE
                    dq_buf[:, head_cols(chunk * JOIN + start + i)] = dq.astype(jnp.bfloat16)
        cols = slice(head * group * DH, (head + 1) * group * DH)
        stores.append(pltpu.make_async_copy(dq_buf.at[:, cols], dq_hbm.at[:, cols], out_sem.at[head]))
        stores[-1].start()
    for store in stores:
        store.wait()


def total_kernel(own_key, own_value, got_key, got_value, *refs):
    terms, (outs, bufs, sem) = refs[:-9], (refs[-9:-5], refs[-5:-1], refs[-1])
    wide = bufs[0].shape[1]
    near = [own[...] + got[...].astype(jnp.float32) for own, got in ((own_key, got_key), (own_value, got_value))]
    beacon = functools.reduce(jnp.add, [x[...].astype(jnp.float32) for x in terms])
    stores = []
    for at, total in enumerate((*near, beacon[:, :wide], beacon[:, wide:])):
        bufs[at][...] = total.astype(jnp.bfloat16)
        stores.append(pltpu.make_async_copy(bufs[at], outs[at], sem.at[at]))
        stores[-1].start()
    for store in stores:
        store.wait()


def in_hbm(x):
    return pltpu.with_memory_space_constraint(x, pltpu.HBM)


def call(kernel, operands, spaces, outs, out_spaces, scratch, limit, products):
    return list(pl.pallas_call(
        kernel,
        out_shape=[jax.ShapeDtypeStruct(*x) for x in outs],
        in_specs=[pl.BlockSpec(memory_space=x) for x in spaces],
        out_specs=[pl.BlockSpec(memory_space=x) for x in out_spaces],
        scratch_shapes=scratch,
        compiler_params=pltpu.CompilerParams(vmem_limit_bytes=limit * 1024 * 1024),
        cost_estimate=pl.CostEstimate(flops=products, bytes_accessed=products // 256, transcendentals=products // 512),
    )(*operands))


def local(queries, keys, values, beacon_keys, beacon_values, grad_out, ratios):
    bf16, f32 = jnp.bfloat16, jnp.float32
    hbm, vmem = pltpu.HBM, pltpu.VMEM
    spans = ratios.shape[0]
    rows, wide = keys.shape
    heads = wide // DH
    group = queries.shape[1] // wide
    chunks = heads * group // JOIN
    width = JOIN * rows
    last = spans - 1
    near, columns = 2 * rows, SLOTS * last
    swap = [(0, 1), (1, 0)]
    shifts = range(1, spans)
    order = sorted(shifts, key=lambda k: abs(2 * k - spans))

    def up(k):
        return [(i, (i + k) % spans) for i in range(spans)]

    left = lax.broadcasted_iota(jnp.int32, (beacon_keys.shape[0], 2 * wide), 1) < wide
    beacons = jnp.where(left, jnp.pad(beacon_keys, ((0, 0), (0, wide))), jnp.pad(beacon_values, ((0, 0), (wide, 0))))
    near_keys, near_values, beacons = lax.optimization_barrier((keys, values, beacons))
    own = {k: lax.ppermute(beacons, "ctx", up(k)) for k in reversed(order)}
    other_key, other_value = (lax.ppermute(x, "sub", swap) for x in (near_keys, near_values))

    product = queries.shape[1] * rows * 2

    def stats_of(size):
        return [((chunks, size, width), f32)] * 2 + [((chunks, 8, width), f32)] * 2

    q_in, g_in, far_mask, *near_stats = call(
        functools.partial(near_kernel, last, group),
        [ratios, in_hbm(queries), in_hbm(grad_out), in_hbm(keys), in_hbm(values), other_key, other_value],
        [pltpu.SMEM] + [hbm] * 4 + [vmem] * 2,
        [(queries.shape, bf16)] * 2 + [((columns, DH), bf16)] + stats_of(near),
        [vmem] * 7,
        [vmem(keys.shape, bf16)] * 2
        + [vmem((heads, near, 2 * DH), bf16), vmem((heads, near, DH), bf16)]
        + [pltpu.SemaphoreType.DMA((2 + 2 * heads,))],
        8,
        2 * product * near,
    )
    first = order[0]
    own[first], near_stats[2] = lax.optimization_barrier((own[first], near_stats[2]))
    other = {k: lax.ppermute(own[k], "sub", swap) for k in {first, last}}
    middle = [k for k in order if k not in other]
    kept, other[first] = lax.optimization_barrier(([own[k] for k in middle], other[first]))
    own |= dict(zip(middle, kept))
    other |= {k: lax.ppermute(own[k], "sub", swap) for k in middle}
    far = [x[k] for k in shifts for x in (own, other)]
    sets = [vmem((columns, width), f32)] * 2 + [vmem((columns, width), bf16)]
    share, delta, far_slopes, *grads = call(
        functools.partial(far_kernel, last, group),
        [q_in, g_in, far_mask, *near_stats, *far],
        [vmem] * (7 + len(far)),
        [((chunks, 8, width), f32)] * 2
        + [((chunks, columns, width), bf16)]
        + [((HALF, 2 * wide), f32)] * last
        + [((HALF, 2 * wide), bf16)] * last,
        [vmem] * (3 + 2 * last),
        [vmem((heads, columns, 2 * DH), bf16), vmem((heads, columns, DH), bf16)]
        + [vmem((columns, DH), f32)] * 2
        + sets * 2,
        12 + 30 * columns * width // 2**20,
        4 * product * columns,
    )
    sent = dict(zip(shifts, grads[last:]))

    def pair(k):
        return (grads[k - 1] + lax.ppermute(sent[k], "sub", swap).astype(f32)).astype(bf16)

    pairs = {k: pair(k) for k in order}
    pairs[order[-1]], delta = lax.optimization_barrier((pairs[order[-1]], delta))
    down = {k: up(-k) for k in order} | {last: [(last, 0)]}
    sums = [lax.ppermute(pairs[k], "ctx", down[k]) for k in order]
    near_slopes, *near_grads = call(
        functools.partial(near_gradients_kernel, group),
        [q_in, g_in, near_stats[0], near_stats[1], share, delta],
        [vmem] * 6,
        [((chunks, near, width), bf16)] + [(keys.shape, f32)] * 2 + [(keys.shape, bf16)] * 2,
        [vmem] * 5,
        [vmem((near, width), bf16)] * 2,
        8,
        product,
    )
    (grad_queries,) = call(
        functools.partial(query_gradients_kernel, group),
        [near_slopes, far_slopes, in_hbm(keys), other_key, *far],
        [vmem] * 2 + [hbm] + [vmem] * (1 + 2 * last),
        [(queries.shape, bf16)],
        [hbm],
        [
            vmem(keys.shape, bf16),
            vmem((heads, near + columns, DH), bf16),
            vmem((heads, DH, near + columns), bf16),
            vmem(queries.shape, bf16),
            pltpu.SemaphoreType.DMA,
            pltpu.SemaphoreType.DMA((heads,)),
        ],
        12,
        product,
    )
    near_got = [lax.ppermute(x, "sub", swap) for x in near_grads[2:]]
    sums, grad_queries = lax.optimization_barrier((sums, grad_queries))
    out_shapes = [(x.shape, bf16) for x in (keys, values, beacon_keys, beacon_values)]
    outs = call(
        total_kernel,
        [*near_grads[:2], *near_got, *sums],
        [vmem] * (4 + len(sums)),
        out_shapes,
        [hbm] * 4,
        [vmem(*x) for x in out_shapes] + [pltpu.SemaphoreType.DMA((4,))],
        4,
        product,
    )
    return (grad_queries, *outs)


def solution(mesh):
    rows = P(("grp", "ctx", "sub"), "tp")
    return jax.shard_map(
        local,
        mesh=mesh,
        in_specs=(rows,) * 6 + (P("grp"),),
        out_specs=(rows,) * 5,
        check_vma=False,
    )
```

```python
import functools
import math

import jax
import jax.numpy as jnp
from jax import lax
from jax.experimental import pallas as pl
from jax.experimental.pallas import tpu as pltpu
from jax.sharding import PartitionSpec as P

DH = 128
SPAN = 256
SLOTS = SPAN // 2
HALF = SLOTS // 2
NT = (((1,), (1,)), ((), ()))
HIDDEN = -3e38
JOIN = 4
BLOCK = 32
SCALE = DH ** (-0.5)
LOG_SCALE = SCALE * math.log2(math.e)


def interleave(first, second):
    few, many = sorted((first, second), key=len)
    done = 0
    for index, step in enumerate(few):
        step()
        upto = len(many) * (index + 1) // len(few)
        for other in many[done:upto]:
            other()
        done = upto
    for other in many[done:]:
        other()


def pipeline(chunks, products, softmax, gradients):
    for step in products(0):
        step()
    for chunk in range(chunks):
        matrix = gradients(chunk - 1) if chunk > 0 else []
        matrix = matrix + (products(chunk + 1) if chunk + 1 < chunks else [])
        interleave(matrix, softmax(chunk))
    for step in gradients(chunks - 1):
        step()


def head_cols(head):
    return slice(head * DH, (head + 1) * DH)


def joined(buf, chunk, start, count):
    first = chunk * JOIN + start
    return jnp.concatenate([buf[:, head_cols(first + i)] for i in range(count)], axis=0)


def pair_products(key_buf, value_buf, q_buf, g_buf, chunk, head, score_ref, signal_ref):
    rows = q_buf.shape[0]
    at = [lax.broadcasted_iota(jnp.int32, (rows, DH), axis) for axis in range(2)]
    one_hot = jnp.where(at[0] == at[1], 1.0, 0.0).astype(jnp.bfloat16)
    one_hot = jnp.concatenate([one_hot] * 2, axis=0)

    def score(start):
        queries = jnp.concatenate([joined(q_buf, chunk, start, 2), one_hot], axis=1)
        cols = slice(start * rows, (start + 2) * rows)
        score_ref[:, cols] = lax.dot_general(key_buf[head], queries, NT, preferred_element_type=jnp.float32)

    def signal(start):
        cols = slice(start * rows, (start + 2) * rows)
        signal_ref[:, cols] = lax.dot_general(
            value_buf[head], joined(g_buf, chunk, start, 2), NT, preferred_element_type=jnp.float32
        )

    return [functools.partial(f, start) for f in (score, signal) for start in range(0, JOIN, 2)]


def mask_of(seen):
    return jnp.where(seen, 0.0, HIDDEN).astype(jnp.bfloat16)


def place(key_buf, value_buf, at, keys, values, mask):
    size = mask.shape[0]
    for head in range(key_buf.shape[0]):
        key_buf[head, at : at + size, :DH] = keys[:, head_cols(head)]
        key_buf[head, at : at + size, DH:] = mask
        value_buf[head, at : at + size, :] = values[:, head_cols(head)]


def spread(x):
    return jnp.broadcast_to(x, (8, x.shape[1]))


def exponentials(chunk, grown_out, top_out, total_out):
    score_ref = grown_out.at[chunk]
    columns, width = score_ref.shape
    state = {"top": jnp.full((8, width), HIDDEN, jnp.float32)}

    def top(at):
        for i in range(at, at + BLOCK, 8):
            state["top"] = jnp.maximum(state["top"], score_ref[i : i + 8, :])

    def end_top():
        state["top"] = spread(jnp.max(state["top"], axis=0, keepdims=True))
        top_out[chunk] = state["top"]
        state["total"] = jnp.zeros((8, width), jnp.float32)

    def grow(at):
        for i in range(at, at + BLOCK, 8):
            grown = jnp.exp2((score_ref[i : i + 8, :] - state["top"]) * LOG_SCALE)
            score_ref[i : i + 8, :] = grown
            state["total"] = state["total"] + grown

    def end_grow():
        total_out[chunk] = spread(jnp.sum(state["total"], axis=0, keepdims=True))

    blocks = range(0, columns, BLOCK)
    return [functools.partial(top, at) for at in blocks] + [end_top] + [functools.partial(grow, at) for at in blocks] + [end_grow]


def near_kernel(
    shifts, group, ratios, q_hbm, g_hbm, key_hbm, value_hbm, other_key, other_value, q_buf, g_buf, mask_out, grown_out,
    signal_out, top_out, total_out, own_key, own_value, key_buf, value_buf, sem,
):
    rows = q_buf.shape[0]
    heads = key_buf.shape[0]
    per_head = group // JOIN
    sub = lax.axis_index("sub")
    pairs = [(key_hbm, own_key), (value_hbm, own_value)]
    for head in range(heads):
        cols = slice(head * group * DH, (head + 1) * group * DH)
        pairs += [(q_hbm.at[:, cols], q_buf.at[:, cols]), (g_hbm.at[:, cols], g_buf.at[:, cols])]
    loads = [pltpu.make_async_copy(*pair, sem.at[i]) for i, pair in enumerate(pairs)]
    for load in loads:
        load.start()
    key_at = lax.broadcasted_iota(jnp.int32, (rows, DH), 0)
    token_at = lax.broadcasted_iota(jnp.int32, (rows, DH), 1)
    place(key_buf, value_buf, rows, other_key, other_value, mask_of(key_at < sub * rows))
    here = lax.axis_index("ctx")
    slot_at = lax.broadcasted_iota(jnp.int32, (HALF, DH), 0)
    for shift in range(shifts):
        owner = jnp.maximum(here - 1 - shift, 0)
        live = jnp.where(here > shift, SPAN // ratios[owner], 0)
        for side, first in enumerate((sub * HALF, (1 - sub) * HALF)):
            at = (2 * shift + side) * HALF
            mask_out[at : at + HALF, :] = mask_of(slot_at < live - first)
    loads[0].wait()
    loads[1].wait()
    place(key_buf, value_buf, 0, own_key, own_value, mask_of(key_at <= token_at))

    def products(chunk):
        head = chunk // per_head
        if chunk % per_head == 0:
            loads[2 + 2 * head].wait()
            loads[3 + 2 * head].wait()
        return pair_products(
            key_buf, value_buf, q_buf, g_buf, chunk, head, grown_out.at[chunk], signal_out.at[chunk]
        )

    pipeline(
        heads * per_head,
        products,
        lambda chunk: exponentials(chunk, grown_out, top_out, total_out),
        lambda chunk: [],
    )


def place_far(key_buf, value_buf, far, mask):
    wide = far[0].shape[1] // 2
    for index, source in enumerate(far):
        at = index * HALF
        place(key_buf, value_buf, at, source.at[:, :wide], source.at[:, wide:], mask[at : at + HALF, :])


def far_kernel(shifts, group, *refs):
    here = lax.axis_index("ctx")
    levels = sorted({shifts * i // 3 for i in range(4)} | set(range(min(shifts, 4))))
    for low, level in zip([-1, *levels], levels):
        pl.when((here > low) & (here <= level))(functools.partial(far_part, shifts, level, group, *refs))


def far_part(shifts, seen, group, q_buf, g_buf, far_mask, near_grown, near_signal, near_top, near_total, *refs):
    far, refs = refs[: 2 * shifts], refs[2 * shifts :]
    share_out, delta_out, slopes_out, own_outs, sent_outs = refs[0], refs[1], refs[2], refs[3 : 3 + shifts], refs[3 + shifts : 3 + 2 * shifts]
    refs = refs[3 + 2 * shifts :]
    (key_buf, value_buf, dk_buf, dv_buf), sets = refs[:4], (refs[4:7], refs[7:10])
    rows = q_buf.shape[0]
    heads = key_buf.shape[0]
    columns = seen * SLOTS
    wide = heads * DH
    per_head = group // JOIN
    chunks = heads * per_head
    width = JOIN * rows
    if seen:
        place_far(key_buf, value_buf, far[: 2 * seen], far_mask)
    for out in (*own_outs[seen:], *sent_outs[seen:]):
        out[...] = jnp.zeros_like(out)
    key_buf, value_buf = key_buf.at[:, :columns, :], value_buf.at[:, :columns, :]
    sets = [[ref.at[:columns, :] for ref in refs] for refs in sets]

    def products(chunk):
        if not seen:
            return []
        score_ref, signal_ref, _ = sets[chunk % 2]
        return pair_products(key_buf, value_buf, q_buf, g_buf, chunk, chunk // per_head, score_ref, signal_ref)

    def softmax(chunk):
        score_ref, signal_ref, weight_ref = sets[chunk % 2]
        slope_ref = slopes_out.at[chunk]
        state = {"top": near_top[chunk]}

        def top(at):
            for i in range(at, at + BLOCK, 8):
                state["top"] = jnp.maximum(state["top"], score_ref[i : i + 8, :])

        def end_top():
            state["top"] = spread(jnp.max(state["top"], axis=0, keepdims=True))
            state["total"] = jnp.zeros((8, width), jnp.float32)

        def grow(at):
            for i in range(at, at + BLOCK, 8):
                grown = jnp.exp2((score_ref[i : i + 8, :] - state["top"]) * LOG_SCALE)
                score_ref[i : i + 8, :] = grown
                state["total"] = state["total"] + grown

        def end_grow():
            total = spread(jnp.sum(state["total"], axis=0, keepdims=True))
            shrink = jnp.exp2((near_top[chunk] - state["top"]) * LOG_SCALE)
            state["far"] = 1.0 / (near_total[chunk] * shrink + total)
            state["near"] = shrink * state["far"]
            share_out[chunk] = state["near"]
            state["delta"] = jnp.zeros((8, width), jnp.float32)

        def weigh(grown, signal, share, at):
            probs = [grown[i : i + 8, :] * state[share] for i in range(at, at + BLOCK, 8)]
            weights = jnp.concatenate(probs, axis=0).astype(jnp.bfloat16)
            if share == "far":
                weight_ref[at : at + BLOCK, :] = weights
            terms = weights.astype(jnp.float32) * signal[at : at + BLOCK, :]
            for i in range(0, BLOCK, 8):
                state["delta"] = state["delta"] + terms[i : i + 8]

        def end_weigh():
            state["delta"] = spread(jnp.sum(state["delta"], axis=0, keepdims=True))
            delta_out[chunk] = state["delta"]

        def slope(at):
            slopes = []
            for i in range(at, at + BLOCK, 8):
                probs = score_ref[i : i + 8, :] * state["far"]
                slopes.append(probs * (signal_ref[i : i + 8, :] - state["delta"]))
            slope_ref[at : at + BLOCK, :] = jnp.concatenate(slopes, axis=0).astype(jnp.bfloat16)

        grown, signal = near_grown.at[chunk], near_signal.at[chunk]
        blocks = range(0, columns, BLOCK)

        def clear():
            if seen < shifts:
                slope_ref[columns:, :] = jnp.zeros((SLOTS * (shifts - seen), width), jnp.bfloat16)

        steps = [clear] + [functools.partial(top, at) for at in blocks] + [end_top]
        steps += [functools.partial(grow, at) for at in blocks] + [end_grow]
        steps += [functools.partial(weigh, score_ref, signal_ref, "far", at) for at in blocks]
        steps += [functools.partial(weigh, grown, signal, "near", at) for at in range(0, 2 * rows, BLOCK)] + [end_weigh]
        return steps + [functools.partial(slope, at) for at in blocks]

    def gradients(chunk):
        if not seen:
            return []
        weight_ref = sets[chunk % 2][2]
        head = chunk // per_head
        last = chunk % per_head == per_head - 1

        def collect(total_ref, buf, left, side, factor):
            total = None
            for start in range(0, JOIN, 2):
                cols = slice(start * rows, (start + 2) * rows)
                part = jnp.dot(left(cols), joined(buf, chunk, start, 2), preferred_element_type=jnp.float32)
                total = part if total is None else total + part
            if chunk % per_head:
                total = total + total_ref[:columns, :]
            if not last:
                total_ref[:columns, :] = total
                return
            cols = slice(side * wide + head * DH, side * wide + (head + 1) * DH)
            for shift in range(seen):
                at = shift * SLOTS
                own_outs[shift][:, cols] = total[at : at + HALF] * factor
                sent_outs[shift][:, cols] = (total[at + HALF : at + SLOTS] * factor).astype(jnp.bfloat16)

        return [
            functools.partial(collect, dk_buf, q_buf, lambda cols: slopes_out[chunk, :columns, cols], 0, SCALE),
            functools.partial(collect, dv_buf, g_buf, lambda cols: weight_ref[:, cols], 1, 1.0),
        ]

    pipeline(chunks, products, softmax, gradients)


def near_gradients_kernel(group, q_buf, g_buf, grown, signal, share, delta, slopes_out, *refs):
    own_outs, sent_outs, sets = refs[:2], refs[2:4], refs[4:]
    rows = q_buf.shape[0]
    wide = own_outs[0].shape[1]
    per_head = group // JOIN
    chunks = wide // DH * per_head
    near = 2 * rows
    totals = {}

    def softmax(chunk):
        weight_ref = sets[chunk % 2]

        def work(at):
            weights, slopes = [], []
            for i in range(at, at + BLOCK, 8):
                probs = grown[chunk, i : i + 8, :] * share[chunk]
                weights.append(probs)
                slopes.append(probs * (signal[chunk, i : i + 8, :] - delta[chunk]))
            weight_ref[at : at + BLOCK, :] = jnp.concatenate(weights, axis=0).astype(jnp.bfloat16)
            slopes_out[chunk, at : at + BLOCK, :] = jnp.concatenate(slopes, axis=0).astype(jnp.bfloat16)

        return [functools.partial(work, at) for at in range(0, near, BLOCK)]

    def gradients(chunk):
        weight_ref = sets[chunk % 2]
        head = chunk // per_head

        def collect(left, buf, side, factor):
            total = totals.pop(side, None)
            for start in range(0, JOIN, 2):
                cols = slice(start * rows, (start + 2) * rows)
                part = jnp.dot(left(cols), joined(buf, chunk, start, 2), preferred_element_type=jnp.float32)
                total = part if total is None else total + part
            if chunk % per_head < per_head - 1:
                totals[side] = total
                return
            own_outs[side][:, head_cols(head)] = total[:rows] * factor
            sent_outs[side][:, head_cols(head)] = (total[rows:] * factor).astype(jnp.bfloat16)

        return [
            functools.partial(collect, lambda cols: slopes_out[chunk, :, cols], q_buf, 0, SCALE),
            functools.partial(collect, lambda cols: weight_ref[:, cols], g_buf, 1, 1.0),
        ]

    pipeline(chunks, lambda chunk: [], softmax, gradients)


def query_gradients_kernel(group, near_slopes, far_slopes, key_hbm, other_key, *refs):
    far, (dq_hbm, own_key, key_buf, turned_buf, dq_buf, in_sem, out_sem) = refs[:-7], refs[-7:]
    rows = dq_buf.shape[0]
    heads = key_buf.shape[0]
    near = 2 * rows
    per_head = group // JOIN
    load = pltpu.make_async_copy(key_hbm, own_key, in_sem)
    load.start()
    at = rows
    for piece in (other_key, *far):
        size = piece.shape[0]
        for head in range(heads):
            key_buf[head, at : at + size, :] = piece[:, head_cols(head)]
        at += size
    load.wait()
    stores = []
    for head in range(heads):
        key_buf[head, :rows, :] = own_key[:, head_cols(head)]
        turned_buf[head] = key_buf[head].T
        for chunk in range(head * per_head, (head + 1) * per_head):
            for start in range(0, JOIN, 2):
                cols = slice(start * rows, (start + 2) * rows)
                turned = jnp.dot(
                    turned_buf[head, :, :near], near_slopes[chunk, :, cols], preferred_element_type=jnp.float32
                ) + jnp.dot(turned_buf[head, :, near:], far_slopes[chunk, :, cols], preferred_element_type=jnp.float32)
                for i in range(2):
                    dq = turned[:, i * rows : (i + 1) * rows].T * SCALE
                    dq_buf[:, head_cols(chunk * JOIN + start + i)] = dq.astype(jnp.bfloat16)
        cols = slice(head * group * DH, (head + 1) * group * DH)
        stores.append(pltpu.make_async_copy(dq_buf.at[:, cols], dq_hbm.at[:, cols], out_sem.at[head]))
        stores[-1].start()
    for store in stores:
        store.wait()


def total_kernel(own_key, own_value, got_key, got_value, *refs):
    terms, (outs, bufs, sem) = refs[:-9], (refs[-9:-5], refs[-5:-1], refs[-1])
    wide = bufs[0].shape[1]
    near = [own[...] + got[...].astype(jnp.float32) for own, got in ((own_key, got_key), (own_value, got_value))]
    beacon = functools.reduce(jnp.add, [x[...].astype(jnp.float32) for x in terms])
    stores = []
    for at, total in enumerate((*near, beacon[:, :wide], beacon[:, wide:])):
        bufs[at][...] = total.astype(jnp.bfloat16)
        stores.append(pltpu.make_async_copy(bufs[at], outs[at], sem.at[at]))
        stores[-1].start()
    for store in stores:
        store.wait()


def in_hbm(x):
    return pltpu.with_memory_space_constraint(x, pltpu.HBM)


def call(kernel, operands, spaces, outs, out_spaces, scratch, limit, products):
    return list(pl.pallas_call(
        kernel,
        out_shape=[jax.ShapeDtypeStruct(*x) for x in outs],
        in_specs=[pl.BlockSpec(memory_space=x) for x in spaces],
        out_specs=[pl.BlockSpec(memory_space=x) for x in out_spaces],
        scratch_shapes=scratch,
        compiler_params=pltpu.CompilerParams(vmem_limit_bytes=limit * 1024 * 1024),
        cost_estimate=pl.CostEstimate(flops=products, bytes_accessed=products // 256, transcendentals=products // 512),
    )(*operands))


def local(queries, keys, values, beacon_keys, beacon_values, grad_out, ratios):
    bf16, f32 = jnp.bfloat16, jnp.float32
    hbm, vmem = pltpu.HBM, pltpu.VMEM
    spans = ratios.shape[0]
    rows, wide = keys.shape
    heads = wide // DH
    group = queries.shape[1] // wide
    chunks = heads * group // JOIN
    width = JOIN * rows
    last = spans - 1
    near, columns = 2 * rows, SLOTS * last
    swap = [(0, 1), (1, 0)]
    shifts = range(1, spans)
    order = sorted(shifts, key=lambda k: abs(2 * k - spans))

    def up(k):
        return [(i, (i + k) % spans) for i in range(spans)]

    left = lax.broadcasted_iota(jnp.int32, (beacon_keys.shape[0], 2 * wide), 1) < wide
    beacons = jnp.where(left, jnp.pad(beacon_keys, ((0, 0), (0, wide))), jnp.pad(beacon_values, ((0, 0), (wide, 0))))
    near_keys, near_values, beacons = lax.optimization_barrier((keys, values, beacons))
    own = {k: lax.ppermute(beacons, "ctx", up(k)) for k in reversed(order)}
    other_key, other_value = (lax.ppermute(x, "sub", swap) for x in (near_keys, near_values))

    product = queries.shape[1] * rows * 2

    def stats_of(size):
        return [((chunks, size, width), f32)] * 2 + [((chunks, 8, width), f32)] * 2

    q_in, g_in, far_mask, *near_stats = call(
        functools.partial(near_kernel, last, group),
        [ratios, in_hbm(queries), in_hbm(grad_out), in_hbm(keys), in_hbm(values), other_key, other_value],
        [pltpu.SMEM] + [hbm] * 4 + [vmem] * 2,
        [(queries.shape, bf16)] * 2 + [((columns, DH), bf16)] + stats_of(near),
        [vmem] * 7,
        [vmem(keys.shape, bf16)] * 2
        + [vmem((heads, near, 2 * DH), bf16), vmem((heads, near, DH), bf16)]
        + [pltpu.SemaphoreType.DMA((2 + 2 * heads,))],
        8,
        2 * product * near,
    )
    first = order[0]
    own[first], near_stats[2] = lax.optimization_barrier((own[first], near_stats[2]))
    other = {k: lax.ppermute(own[k], "sub", swap) for k in {first, last}}
    middle = [k for k in order if k not in other]
    kept, other[first] = lax.optimization_barrier(([own[k] for k in middle], other[first]))
    own |= dict(zip(middle, kept))
    other |= {k: lax.ppermute(own[k], "sub", swap) for k in middle}
    far = [x[k] for k in shifts for x in (own, other)]
    sets = [vmem((columns, width), f32)] * 2 + [vmem((columns, width), bf16)]
    share, delta, far_slopes, *grads = call(
        functools.partial(far_kernel, last, group),
        [q_in, g_in, far_mask, *near_stats, *far],
        [vmem] * (7 + len(far)),
        [((chunks, 8, width), f32)] * 2
        + [((chunks, columns, width), bf16)]
        + [((HALF, 2 * wide), f32)] * last
        + [((HALF, 2 * wide), bf16)] * last,
        [vmem] * (3 + 2 * last),
        [vmem((heads, columns, 2 * DH), bf16), vmem((heads, columns, DH), bf16)]
        + [vmem((columns, DH), f32)] * 2
        + sets * 2,
        12 + 30 * columns * width // 2**20,
        4 * product * columns,
    )
    sent = dict(zip(shifts, grads[last:]))

    def pair(k):
        return (grads[k - 1] + lax.ppermute(sent[k], "sub", swap).astype(f32)).astype(bf16)

    pairs = {k: pair(k) for k in order}
    pairs[order[-1]], delta = lax.optimization_barrier((pairs[order[-1]], delta))
    down = {k: up(-k) for k in order} | {last: [(last, 0)]}
    sums = [lax.ppermute(pairs[k], "ctx", down[k]) for k in order]
    near_slopes, *near_grads = call(
        functools.partial(near_gradients_kernel, group),
        [q_in, g_in, near_stats[0], near_stats[1], share, delta],
        [vmem] * 6,
        [((chunks, near, width), bf16)] + [(keys.shape, f32)] * 2 + [(keys.shape, bf16)] * 2,
        [vmem] * 5,
        [vmem((near, width), bf16)] * 2,
        8,
        product,
    )
    (grad_queries,) = call(
        functools.partial(query_gradients_kernel, group),
        [near_slopes, far_slopes, in_hbm(keys), other_key, *far],
        [vmem] * 2 + [hbm] + [vmem] * (1 + 2 * last),
        [(queries.shape, bf16)],
        [hbm],
        [
            vmem(keys.shape, bf16),
            vmem((heads, near + columns, DH), bf16),
            vmem((heads, DH, near + columns), bf16),
            vmem(queries.shape, bf16),
            pltpu.SemaphoreType.DMA,
            pltpu.SemaphoreType.DMA((heads,)),
        ],
        12,
        product,
    )
    near_got = [lax.ppermute(x, "sub", swap) for x in near_grads[2:]]
    sums, grad_queries = lax.optimization_barrier((sums, grad_queries))
    out_shapes = [(x.shape, bf16) for x in (keys, values, beacon_keys, beacon_values)]
    outs = call(
        total_kernel,
        [*near_grads[:2], *near_got, *sums],
        [vmem] * (4 + len(sums)),
        out_shapes,
        [hbm] * 4,
        [vmem(*x) for x in out_shapes] + [pltpu.SemaphoreType.DMA((4,))],
        4,
        product,
    )
    return (grad_queries, *outs)


def solution(mesh):
    rows = P(("grp", "ctx", "sub"), "tp")
    return jax.shard_map(
        local,
        mesh=mesh,
        in_specs=(rows,) * 6 + (P("grp"),),
        out_specs=(rows,) * 5,
        check_vma=False,
    )
```
